32 devices in a mesh: gx: 8 (over z, core), gy: 4 (over y, x).
Axes of the slice: x: 2, y: 2, z: 4, core: 2. Of those that a mesh axis runs over, the one named last changes fastest.
Arguments:
- prev_wave: float32 [32, 256, 2048], P(None, 'gy', 'gx'), may hold values from -6 to 6
- source: float32 [32, 256, 2048], P(None, 'gy', 'gx'), may hold values from -6 to 6
- start_state: float32 [256, 2048], P('gy', 'gx'), may hold values from -6 to 6
- storage: float32 [256, 2048], P('gy', 'gx'), may hold values from 0.5 to 4
- leakage: float32 [256, 2048], P('gy', 'gx'), may hold values from 0.1 to 1
- cond_east: float32 [256, 2048], P('gy', 'gx'), may hold values from 0.5 to 2
- cond_south: float32 [256, 2048], P('gy', 'gx'), may hold values from 0.5 to 2
- owner_weight: int32 [256, 2048], P('gy', 'gx'), may hold values from 1 to 3
- aggregate: int32 [256, 2048], P('gy', 'gx'), may hold values from 0 to 2047, as said below
- coarse_inverse: float32 [2048, 2048], P(('gx', 'gy')), as said below
Outputs:
- relaxed: float32 [32, 256, 2048], P(None, 'gy', 'gx')
The draws below stay inside these ranges and needn't reach their ends.
Inputs may be any that keep to these rules, and one draw needn't show every extreme that they name: coarse_inverse is exactly symmetric, with diagonal entries from 1 / 256 to 4 / 256. `aggregate`: the nodes of tile (a, b) carry exactly the aggregates (b * 4 + a) * 64 to (b * 4 + a + 1) * 64 - 1, each of them inside that tile.
All inputs are finite; a program needn't handle non-finite values.
Results may differ from the reference program's by a relative error of at most 0.0003.
Values sent between devices are 32-bit elements; how exact they have to be, the bound alone decides.
A program may use at most 128 MiB of HBM per device.

```python
import math
import jax
import jax.numpy as jnp
from jax import lax

RD = 64
CD = 256
NT = 32
DEG = 8
OV = 2
AGG_ROWS = 8
AGG_COLS = 8
AGG_DEV = 64
NR = 256
NC = 2048
GROUP_COUNT = 2048
NODES_PER_GROUP = 256
N_GX = 8
N_GY = 4


def draw_coarse_inverse(key, part):
    first_key = jax.random.fold_in(key, 11)
    second_key = jax.random.fold_in(key, 12)
    unscaled_values = jax.random.normal(first_key, (GROUP_COUNT, GROUP_COUNT), jnp.float32)
    diagonal_entries = jnp.exp(jax.random.uniform(second_key, (GROUP_COUNT,), jnp.float32, 0.0, 1.3862943))
    offdiagonal_entries = (unscaled_values + unscaled_values.T) * (0.7 / (NODES_PER_GROUP * jnp.sqrt(jnp.float32(GROUP_COUNT))))
    identity_pattern_mask = jnp.eye(GROUP_COUNT, dtype=jnp.float32)
    return offdiagonal_entries * (1.0 - identity_pattern_mask) + identity_pattern_mask * (diagonal_entries / NODES_PER_GROUP)[:, None]


def draw_aggregate(key, part):
    row_key = jax.random.fold_in(key, 21)
    col_key = jax.random.fold_in(key, 22)
    rows = lax.broadcasted_iota(jnp.int32, (NR, NC), 0)
    cols = lax.broadcasted_iota(jnp.int32, (NR, NC), 1)
    tile_row = rows // RD
    tile_col = cols // CD
    inner_row = rows % RD
    inner_col = cols % CD
    jitter_row = jax.random.randint(row_key, (NR, NC), -1, 2, dtype=jnp.int32)
    jitter_col = jax.random.randint(col_key, (NR, NC), -2, 3, dtype=jnp.int32)
    moved_row = jnp.clip(inner_row + jitter_row, 0, RD - 1)
    moved_col = jnp.clip(inner_col + jitter_col, 0, CD - 1)
    patch = moved_row * AGG_ROWS // RD * AGG_COLS + moved_col * AGG_COLS // CD
    owner = tile_col * (NR // RD) + tile_row
    return (owner * AGG_DEV + patch).astype(jnp.int32)


def touch_ends(drawn, rng, low, largest):
    longest = drawn.shape.index(max(drawn.shape))
    spots = []
    for shift in (0, 1):
        where = [jax.random.randint(jax.random.fold_in(rng, axis), (), 0, length) for axis, length in enumerate(drawn.shape)]
        where[longest] = (where[longest] + shift) % drawn.shape[longest]
        spots.append(tuple(where))
    return drawn.at[spots[0]].set(low).at[spots[1]].set(largest)


def steps_of(key, extent, pieces, smallest, top_value):
    loudness = 1.0
    for dim, parts in pieces:
        heights = jax.random.uniform(jax.random.fold_in(jax.random.fold_in(key, 6), dim), (parts,), jnp.float32, smallest / len(pieces), top_value / len(pieces))
        loudness = loudness * jnp.repeat(jnp.exp(heights), extent[dim] // parts).reshape((-1,) + (1,) * (len(extent) - 1 - dim))
    return loudness


def scatter_about(own_key, shape, deviation, bound, pieces=(), held_as=jnp.bfloat16):
    drawn = deviation * jax.random.normal(own_key, shape, jnp.float32)
    if pieces:
        drawn = drawn * steps_of(own_key, shape, pieces, -0.22, 0.18)
    return jnp.clip(drawn, -bound, bound).astype(held_as)


def setup_inputs(seed: int = 0) -> dict:
    key_of = jax.random.split(jax.random.key(seed), 11)
    prev_wave = scatter_about(key_of[0], (NT, NR, NC), 1.0, 6.0, ((1, 4), (2, 8)), jnp.float32)
    source = scatter_about(key_of[1], (NT, NR, NC), 1.0, 6.0, ((1, 4), (2, 8)), jnp.float32)
    start_state = scatter_about(key_of[2], (NR, NC), 1.0, 6.0, ((0, 4), (1, 8)), jnp.float32)
    storage = jnp.clip(jnp.exp(math.log(4.0) - 2.0794415 * jax.random.uniform(key_of[3], (NR, NC), jnp.float32) ** steps_of(key_of[3], (NR, NC), ((0, 4), (1, 8)), -0.2, 0.2)), 0.5, 4.0)
    leakage = jnp.clip(jnp.exp(math.log(1.0) - 2.3025851 * jax.random.uniform(key_of[4], (NR, NC), jnp.float32) ** steps_of(key_of[4], (NR, NC), ((0, 4), (1, 8)), -0.2, 0.2)), 0.1, 1.0)
    cond_east = jnp.clip(jnp.exp(math.log(2.0) - 1.3862944 * jax.random.uniform(key_of[5], (NR, NC), jnp.float32) ** steps_of(key_of[5], (NR, NC), ((0, 4), (1, 8)), -0.2, 0.2)), 0.5, 2.0)
    cond_south = jnp.clip(jnp.exp(math.log(2.0) - 1.3862944 * jax.random.uniform(key_of[6], (NR, NC), jnp.float32) ** steps_of(key_of[6], (NR, NC), ((0, 4), (1, 8)), -0.2, 0.2)), 0.5, 2.0)
    owner_weight = touch_ends(jax.random.randint(key_of[7], (NR, NC), 1, 4), jax.random.fold_in(key_of[7], 1), 1, 3).astype(jnp.int32)
    aggregate = draw_aggregate(jax.random.fold_in(key_of[10], 71), 0)
    coarse_inverse = draw_coarse_inverse(jax.random.fold_in(key_of[10], 71), 0)
    return dict(prev_wave=prev_wave, source=source, start_state=start_state, storage=storage, leakage=leakage, cond_east=cond_east, cond_south=cond_south, owner_weight=owner_weight, aggregate=aggregate, coarse_inverse=coarse_inverse)


cheb_theta = 1.0
cheb_delta = 0.95


def apply_operator(full, diagonal_mid, east_mid, east_west, south_mid, south_north):
    centre = full[1:-1, 1:-1]
    return (diagonal_mid * centre - east_mid * full[1:-1, 2:] - east_west * full[1:-1, :-2]
            - south_mid * full[2:, 1:-1] - south_north * full[:-2, 1:-1])


def local_sweep(stack, steps_count):
    prev_full = stack[:steps_count]
    source_mid = stack[steps_count:2 * steps_count, 1:-1, 1:-1]
    start_mid = stack[2 * steps_count, 1:-1, 1:-1]
    storage_full = stack[2 * steps_count + 1]
    leakage_full = stack[2 * steps_count + 2]
    east_full = stack[2 * steps_count + 3]
    south_full = stack[2 * steps_count + 4]
    present_full = stack[2 * steps_count + 5]
    east_mid = east_full[1:-1, 1:-1]
    east_west = east_full[1:-1, :-2]
    south_mid = south_full[1:-1, 1:-1]
    south_north = south_full[:-2, 1:-1]
    storage_mid = storage_full[1:-1, 1:-1]
    diagonal_mid = (storage_mid + leakage_full[1:-1, 1:-1] + east_mid + east_west + south_mid
                    + south_north + (1.0 - present_full[1:-1, 1:-1]))
    inner_mask = jnp.pad(jnp.ones_like(storage_mid), 1) > 0.5
    sigma = cheb_theta / cheb_delta

    def advance(carried, inputs):
        cycle_full, source_now = inputs
        rhs = source_now + storage_mid * carried

        def residual_of(interior):
            full = jnp.where(inner_mask, jnp.pad(interior, 1), cycle_full)
            return rhs - apply_operator(full, diagonal_mid, east_mid, east_west, south_mid, south_north)

        iterate = cycle_full[1:-1, 1:-1]
        update = residual_of(iterate) / diagonal_mid / cheb_theta
        iterate = iterate + update
        rho_prev = 1.0 / sigma
        for degree in range(1, DEG):
            rho_now = 1.0 / (2.0 * sigma - rho_prev)
            update = rho_now * rho_prev * update + (2.0 * rho_now / cheb_delta) * (residual_of(iterate) / diagonal_mid)
            iterate = iterate + update
            rho_prev = rho_now
        return iterate, iterate

    final_state, waves = lax.scan(advance, start_mid, (prev_full, source_mid), unroll=8)
    return waves


def tile_shift(values, down, right):
    padded = jnp.pad(values, ((1, 1), (1, 1)) + ((0, 0),) * (values.ndim - 2))
    return padded[1 - down:1 - down + values.shape[0], 1 - right:1 - right + values.shape[1]]


def gather_rims(folded):
    extended_rows = RD + 2 * OV
    ext_cols = CD + 2 * OV
    incoming = jnp.zeros(folded.shape[:3] + (RD, CD), folded.dtype)
    incoming = incoming.at[..., :OV, :].add(tile_shift(folded[..., extended_rows - OV:, OV:OV + CD], 1, 0))
    incoming = incoming.at[..., RD - OV:, :].add(tile_shift(folded[..., :OV, OV:OV + CD], -1, 0))
    incoming = incoming.at[..., :, :OV].add(tile_shift(folded[..., OV:OV + RD, ext_cols - OV:], 0, 1))
    incoming = incoming.at[..., :, CD - OV:].add(tile_shift(folded[..., OV:OV + RD, :OV], 0, -1))
    incoming = incoming.at[..., :OV, :OV].add(tile_shift(folded[..., extended_rows - OV:, ext_cols - OV:], 1, 1))
    incoming = incoming.at[..., :OV, CD - OV:].add(tile_shift(folded[..., extended_rows - OV:, :OV], 1, -1))
    incoming = incoming.at[..., RD - OV:, :OV].add(tile_shift(folded[..., :OV, ext_cols - OV:], -1, 1))
    incoming = incoming.at[..., RD - OV:, CD - OV:].add(tile_shift(folded[..., :OV, :OV], -1, -1))
    return incoming


def globalize(tiles_array):
    planes = tiles_array.shape[2]
    return jnp.transpose(tiles_array, (2, 0, 3, 1, 4)).reshape(planes, N_GY * RD, N_GX * CD)


def reference(prev_wave, source, start_state, storage, leakage, cond_east, cond_south, owner_weight, aggregate, coarse_inverse):
    steps_count, rows_all, cols_all = prev_wave.shape
    col_ids = lax.broadcasted_iota(jnp.int32, (rows_all, cols_all), 1)
    row_ids = lax.broadcasted_iota(jnp.int32, (rows_all, cols_all), 0)
    east = jnp.where(col_ids < cols_all - 1, cond_east, jnp.zeros_like(cond_east))
    south = jnp.where(row_ids < rows_all - 1, cond_south, jnp.zeros_like(cond_south))
    stack = jnp.concatenate([prev_wave, source, start_state[None], storage[None], leakage[None],
                             east[None], south[None], jnp.ones_like(storage)[None]], 0)
    cycle = OV + 1
    padded = jnp.pad(stack, ((0, 0), (cycle, cycle), (cycle, cycle)))

    def one_tile(tile):
        tile_row = (tile // N_GX).astype(jnp.int32)
        tile_col = (tile % N_GX).astype(jnp.int32)
        window = lax.dynamic_slice(padded, (jnp.int32(0), tile_row * RD, tile_col * CD),
                                   (2 * steps_count + 6, RD + 2 * cycle, CD + 2 * cycle))
        return local_sweep(window, steps_count)

    waves = lax.map(one_tile, jnp.arange(N_GY * N_GX, dtype=jnp.int32))
    waves = waves.reshape((N_GY, N_GX) + waves.shape[1:])
    counts_src = jnp.ones((N_GY, N_GX, 1, RD + 2 * OV, CD + 2 * OV), jnp.float32)
    incoming = globalize(gather_rims(waves))
    copies = globalize(gather_rims(counts_src))[0]
    own = globalize(waves[..., OV:OV + RD, OV:OV + CD])
    weight = owner_weight.astype(jnp.float32)
    settled = (weight * own + incoming) / (weight + copies)
    upad = jnp.pad(settled, ((0, 0), (1, 1), (1, 1)))
    east_west = jnp.pad(east, ((0, 0), (1, 0)))[:, :-1]
    south_north = jnp.pad(south, ((1, 0), (0, 0)))[:-1]
    diagonal_entries = storage + leakage + east + east_west + south + south_north
    image = (diagonal_entries * settled - east * upad[:, 1:-1, 2:] - east_west * upad[:, 1:-1, :-2]
             - south * upad[:, 2:, 1:-1] - south_north * upad[:, :-2, 1:-1])
    before = jnp.concatenate([start_state[None], settled[:-1]], 0)
    resid = source + storage * before - image
    coarse = jax.ops.segment_sum(resid.reshape(steps_count, -1).T, aggregate.reshape(-1), num_segments=GROUP_COUNT)
    correction = jnp.dot(coarse_inverse, coarse, precision=lax.Precision.HIGHEST, preferred_element_type=jnp.float32)
    prolonged = jnp.take(correction.T, aggregate, axis=1)
    return settled + prolonged
```

```python
import functools

import jax
import jax.numpy as jnp
from jax import lax
from jax.experimental import pallas as pl
from jax.experimental.pallas import tpu as pltpu
from jax.sharding import PartitionSpec as P

DEG = 8
OV = 2
HALO = OV + 1
LANES = 128
VR = 9
ROWS_L = 8 * VR
COEFS = 6
DELTA = 0.95
SIGMA = 1.0 / DELTA
OFFSETS = (0, 67, 134)
SPLIT_AB, SPLIT_BC = 98, 164
F32 = jnp.float32
BF16 = jnp.bfloat16
MESH = pl.DeviceIdType.MESH
VMEM_LIMIT = 56 * 1024 * 1024


def lane_id():
    return lax.broadcasted_iota(jnp.int32, (8, LANES), 1)


def sub_id():
    return lax.broadcasted_iota(jnp.int32, (8, LANES), 0)


def turn(x, by):
    by = by % LANES
    return pltpu.roll(x, by, 1) if not (isinstance(by, int) and by == 0) else x


def position(axes):
    gx, gy = lax.axis_index("gx"), lax.axis_index("gy")
    return gx > 0, gx < axes[0] - 1, gy > 0, gy < axes[1] - 1


def masked_coefs(refs, rows, half, axes, first_row):
    _, has_e, _, has_s = position(axes)
    start, sto, leak, east, south, owner = [ref[rows, :] for ref in refs]
    if half == 1:
        cut = jnp.logical_and(lane_id() == LANES - 1, jnp.logical_not(has_e))
        east = jnp.where(cut, 0.0, east)
    cut = jnp.logical_and(sub_id() + first_row == 63, jnp.logical_not(has_s))
    south = jnp.where(cut, 0.0, south)
    return start, sto, leak, east, south, owner.astype(F32)


def pack_kernel(axes, steps, rows, *refs):
    prev, src = refs[0:2], refs[2:4]
    coef = [refs[4 + 2 * p : 6 + 2 * p] for p in range(COEFS)]
    xw, xe, yn, ys = refs[4 + 2 * COEFS :]
    group = lane_id() // 4

    @pl.loop(0, rows // 8)
    def _(t):
        first = pl.multiple_of(t * 8, 8)
        for k, arr in enumerate((prev, src)):
            low = jnp.zeros((8, LANES), F32)
            high = jnp.zeros((8, LANES), F32)
            for n in range(steps):
                at = pl.ds(pl.multiple_of(n * rows + first, 8), 8)
                low = jnp.where(group == n, turn(arr[0][at, :], 4 * n), low)
                high = jnp.where(group == n, turn(arr[1][at, :], 4 * n - 125), high)
            xw[k, pl.ds(first, 8), :] = low
            xe[k, pl.ds(first, 8), :] = high
        at = pl.ds(first, 8)
        low = jnp.zeros((8, LANES), F32)
        high = jnp.zeros((8, LANES), F32)
        planes0 = masked_coefs([c[0] for c in coef], at, 0, axes, first)
        planes1 = masked_coefs([c[1] for c in coef], at, 1, axes, first)
        for p in range(COEFS):
            low = jnp.where(group == p, turn(planes0[p], 4 * p), low)
            high = jnp.where(group == p, turn(planes1[p], 4 * p - 125), high)
        xw[2, at, :] = low
        xe[2, at, :] = high

    for out, first, base in ((yn, 0, 0), (ys, rows - HALO, rows - 8)):
        for h in range(2):
            for j in range(HALO):
                for k, arr in enumerate((prev, src)):
                    for q in range(steps // 8):
                        start = 8 * q * rows + first + j
                        out[h, j, k * steps + 8 * q : k * steps + 8 * q + 8, :] = arr[h][
                            pl.ds(start, 8, stride=rows), :
                        ]
            planes = masked_coefs([c[h] for c in coef], pl.ds(base, 8), h, axes, base)
            for j in range(HALO):
                at = first + j - base
                pieces = [p[at : at + 1] for p in planes]
                pieces += [jnp.zeros((8 - COEFS, LANES), F32)]
                out[h, j, 2 * steps : 2 * steps + 8, :] = jnp.concatenate(pieces, 0)


def exchange_kernel(axes, xw, xe, yn, ys, *refs):
    outs = refs[:8]
    send, recv = refs[8:]
    n_x, n_y = axes
    gx, gy = lax.axis_index("gx"), lax.axis_index("gy")
    west, east = lax.rem(gx + n_x - 1, n_x), lax.rem(gx + 1, n_x)
    north, south = lax.rem(gy + n_y - 1, n_y), lax.rem(gy + 1, n_y)
    from_w, from_e, from_n, from_s, from_nw, from_ne, from_sw, from_se = outs
    last = yn.shape[0] - 1
    plan = (
        (yn, from_s, (gx, north)),
        (ys, from_n, (gx, south)),
        (xw, from_e, (west, gy)),
        (xe, from_w, (east, gy)),
        (yn.at[0], from_se, (west, north)),
        (yn.at[last], from_sw, (east, north)),
        (ys.at[0], from_ne, (west, south)),
        (ys.at[last], from_nw, (east, south)),
    )
    barrier = pltpu.get_barrier_semaphore()
    for _, _, to in plan:
        pl.semaphore_signal(barrier, inc=1, device_id=to, device_id_type=MESH)
    pl.semaphore_wait(barrier, len(plan))
    copies = []
    for i, (src, dst, to) in enumerate(plan):
        copy = pltpu.make_async_remote_copy(
            src_ref=src, dst_ref=dst, send_sem=send.at[i], recv_sem=recv.at[i],
            device_id=to, device_id_type=MESH,
        )
        copy.start()
        copies.append(copy)
    for copy in copies:
        copy.wait()


def exchange(axes, ident, xw, xe, yn, ys):
    corner = jax.ShapeDtypeStruct(yn.shape[1:], F32)
    shape = lambda a: jax.ShapeDtypeStruct(a.shape, F32)
    return pl.pallas_call(
        functools.partial(exchange_kernel, axes),
        out_shape=[shape(xw), shape(xw), shape(yn), shape(yn)] + [corner] * 4,
        in_specs=[pl.BlockSpec(memory_space=pl.ANY)] * 4,
        out_specs=[pl.BlockSpec(memory_space=pl.ANY)] * 8,
        scratch_shapes=[pltpu.SemaphoreType.DMA((8,)), pltpu.SemaphoreType.DMA((8,))],
        compiler_params=pltpu.CompilerParams(collective_id=ident, has_side_effects=True),
        name="neighbour_exchange",
    )(xw, xe, yn, ys)


def lay(a, b, west, east):
    lane = lane_id()
    first = jnp.where(lane < HALO, west, turn(a, HALO))
    mid = jnp.where(lane < 64, turn(a, 64), turn(b, 64))
    last = jnp.where(lane >= LANES - HALO, turn(east, LANES - HALO), turn(b, LANES - HALO))
    return first, mid, last


def sweep_kernel(axes, steps, rows, *refs):
    prev, src = refs[0:2], refs[2:4]
    coef = [refs[4 + 2 * p : 6 + 2 * p] for p in range(COEFS)]
    base = 4 + 2 * COEFS
    from_w, from_e, from_n, from_s, from_nw, from_ne, from_sw, from_se = refs[base : base + 8]
    waves, co, xw, xe, yn, ys = refs[base + 8 : base + 14]
    ext, cc, gbuf, carry = refs[base + 14 :]
    has_w, has_e, has_n, has_s = position(axes)
    lane, sub = lane_id(), sub_id()
    zero = jnp.zeros((8, LANES), F32)

    def keep(flag, value):
        return jnp.where(flag, value, 0.0)

    def put_own(plane, t, a, b, k, slot):
        at = pl.ds(t * 8, 8)
        west = keep(has_w, turn(from_w[k, at, :], -4 * slot + LANES * 4))
        east = keep(has_e, turn(from_e[k, at, :], -4 * slot + LANES * 4))
        for g, value in enumerate(lay(a, b, west, east)):
            ext[g, pl.ds(plane * ROWS_L + HALO + 8 * t, 8), :] = value

    @pl.loop(0, steps)
    def _(n):
        for k, arr in enumerate((prev, src)):
            for t in range(rows // 8):
                at = pl.ds(pl.multiple_of(n * rows + 8 * t, 8), 8)
                put_own(k * steps + n, t, arr[0][at, :], arr[1][at, :], k, n)

    for t in range(rows // 8):
        at = pl.ds(8 * t, 8)
        planes0 = masked_coefs([c[0] for c in coef], at, 0, axes, 8 * t)
        planes1 = masked_coefs([c[1] for c in coef], at, 1, axes, 8 * t)
        for p in range(COEFS):
            put_own(2 * steps + p, t, planes0[p], planes1[p], 2, p)
    for j in range(HALO):
        for strip, cw, ce, flag, row in (
            (from_n, from_nw, from_ne, has_n, j),
            (from_s, from_sw, from_se, has_s, rows + HALO + j),
        ):
            for q in range(2 * steps // 8 + 1):
                at = pl.ds(8 * q, 8)
                a = keep(flag, strip[0, j, at, :])
                b = keep(flag, strip[1, j, at, :])
                west = keep(jnp.logical_and(flag, has_w), turn(cw[j, at, :], -125))
                east = keep(jnp.logical_and(flag, has_e), ce[j, at, :])
                for g, value in enumerate(lay(a, b, west, east)):
                    ext[g, pl.ds(8 * q * ROWS_L + row, 8, stride=ROWS_L), :] = value
    for row in range(rows + 2 * HALO, ROWS_L):
        for q in range(2 * steps // 8 + 1):
            for g in range(3):
                ext[g, pl.ds(8 * q * ROWS_L + row, 8, stride=ROWS_L), :] = zero

    def plane(index, v, g):
        return ext[g, pl.ds(index * ROWS_L + v, 8, stride=VR), :]

    first_coef = 2 * steps
    for g in range(3):
        col = lane + OFFSETS[g]
        col_in = jnp.logical_and(col >= 1, col <= 260)
        col_own = jnp.logical_and(col >= HALO, col <= 258)
        col_there = jnp.logical_and(
            jnp.logical_or(col >= HALO, has_w), jnp.logical_or(col <= 258, has_e)
        )
        n_cols = (
            1.0
            + jnp.where(jnp.logical_and(col <= 4, has_w), 1.0, 0.0)
            + jnp.where(jnp.logical_and(col >= 257, has_e), 1.0, 0.0)
        )
        souths = [plane(first_coef + 4, v, g) for v in range(VR)]
        for v in range(VR):
            row = sub * VR + v
            row_in = jnp.logical_and(row >= 1, row <= 68)
            row_own = jnp.logical_and(row >= HALO, row <= 66)
            row_there = jnp.logical_and(
                jnp.logical_or(row >= HALO, has_n), jnp.logical_or(row <= 66, has_s)
            )
            inner = jnp.logical_and(row_in, col_in)
            own = jnp.logical_and(row_own, col_own)
            there = jnp.logical_and(jnp.logical_and(row_there, col_there), inner)
            n_rows = (
                1.0
                + jnp.where(jnp.logical_and(row <= 4, has_n), 1.0, 0.0)
                + jnp.where(jnp.logical_and(row >= 65, has_s), 1.0, 0.0)
            )
            start, sto, leak, east, south, owner = [
                plane(first_coef + p, v, g) for p in range(COEFS)
            ]
            ea_w = turn(east, 1)
            so_n = souths[v - 1] if v else pltpu.roll(souths[VR - 1], 1, 0)
            diag = sto + leak + east + ea_w + south + so_n
            safe = jnp.where(there, diag, 1.0)
            scale = jnp.where(there, 2.0 * SIGMA / safe, 0.0)
            cc[0, g, v] = jnp.where(lane == LANES - 1, 0.0, scale * east)
            cc[1, g, v] = jnp.where(lane == 0, 0.0, scale * ea_w)
            cc[2, g, v] = scale * south
            cc[3, g, v] = scale * so_n
            cc[4, g, v] = scale
            cc[5, g, v] = scale * sto
            cc[6, g, v] = jnp.where(inner, 0.0, 2.0 * SIGMA)
            weight = jnp.where(own, owner, jnp.where(there, 1.0, 0.0))
            cc[7, g, v] = weight * (1.0 / TAU[DEG])
            den = jnp.where(there, owner + n_rows * n_cols - 1.0, 1.0)
            at = slice(8 * v, 8 * v + 8)
            co[0, g, at, :] = weight
            co[1, g, at, :] = jnp.where(there, 1.0 / den, 0.0)
            co[2, g, at, :] = diag
            co[3, g, at, :] = east
            co[4, g, at, :] = ea_w
            co[5, g, at, :] = south
            co[6, g, at, :] = so_n
            co[7, g, at, :] = sto
            co[8, g, at, :] = start
            carry[g, v] = start

    xw[...] = jnp.zeros_like(xw)
    xe[...] = jnp.zeros_like(xe)
    group = lane // 4

    def stencil(y, g, v):
        cur = y[g][v]
        down = y[g][v + 1] if v < VR - 1 else pltpu.roll(y[g][0], 7, 0)
        up = y[g][v - 1] if v else pltpu.roll(y[g][VR - 1], 1, 0)
        return (
            cc[0, g, v] * turn(cur, LANES - 1)
            + cc[1, g, v] * turn(cur, 1)
            + (cc[2, g, v] * down + cc[3, g, v] * up)
        )

    def advance(n, held):
        old = [[None] * VR for _ in range(3)]
        for g in range(3):
            for v in range(VR):
                old[g][v] = plane(n, v, g)
                gbuf[g, v] = (
                    cc[4, g, v] * plane(steps + n, v, g)
                    + cc[5, g, v] * held[g][v]
                    + cc[6, g, v] * old[g][v]
                )
        now = [
            [0.5 * (stencil(old, g, v) + gbuf[g, v]) for v in range(VR)] for g in range(3)
        ]
        for k in range(1, DEG):
            new = [
                [stencil(now, g, v) + (TAU[k] * gbuf[g, v] - old[g][v]) for v in range(VR)]
                for g in range(3)
            ]
            old, now = now, new
        return now

    def finish(n, now):
        for g in range(3):
            for v in range(VR):
                at = pl.ds(pl.multiple_of(n * ROWS_L + 8 * v, 8), 8)
                waves[g, at, :] = now[g][v] * (1.0 / TAU[DEG])
        weighted = [[cc[7, g, v] * now[g][v] for v in range(VR)] for g in range(3)]
        for v in range(VR):
            at = slice(8 * v, 8 * v + 8)
            xw[at, :] = jnp.where(group == n, turn(weighted[0][v], 4 * n + LANES - 1), xw[at, :])
            xe[at, :] = jnp.where(group == n, turn(weighted[2][v], 4 * n + 4), xe[at, :])
        for j in range(HALO):
            for g in range(3):
                yn[g, j, pl.ds(n, 1), :] = weighted[g][1 + j][0:1]
                ys[g, j, pl.ds(n, 1), :] = weighted[g][3 + j][7:8]
        return [[now[g][v] * (1.0 / TAU[DEG]) for v in range(VR)] for g in range(3)]

    @pl.loop(0, steps)
    def _(n):
        held = [[carry[g, v] for v in range(VR)] for g in range(3)]
        held = finish(n, advance(n, held))
        for v in range(VR):
            a, b, c = held[0][v], held[1][v], held[2][v]
            carry[0, v] = jnp.where(lane < SPLIT_AB, a, turn(b, 67))
            left = jnp.where(lane < SPLIT_AB - 67, turn(a, 61), b)
            carry[1, v] = jnp.where(lane < SPLIT_BC - 67, left, turn(c, 67))
            carry[2, v] = jnp.where(lane < SPLIT_BC - 134, turn(b, 61), c)


def chebyshev_scales():
    tau = [1.0, SIGMA]
    for _ in range(DEG):
        tau.append(2.0 * SIGMA * tau[-1] - tau[-2])
    return tau


TAU = chebyshev_scales()


def one_hot_of(row, count, first):
    ids = jnp.broadcast_to(row - first, (count, row.shape[1]))
    return jnp.where(
        ids == lax.broadcasted_iota(jnp.int32, ids.shape, 0), 1.0, 0.0
    ).astype(BF16)


def settle_kernel(axes, steps, rows, aggs, *refs):
    waves, co, from_w, from_e, from_n, from_s, from_nw, from_ne, from_sw, from_se = refs[:10]
    src = refs[10:12]
    agg = refs[12]
    settled, coarse = refs[13:15]
    before, rest = refs[15:]
    has_w, has_e, has_n, has_s = position(axes)
    lane, sub = lane_id(), sub_id()
    tile = lax.axis_index("gx") * axes[1] + lax.axis_index("gy")

    for g in range(3):
        for v in range(VR):
            before[g, v] = co[8, g, 8 * v : 8 * v + 8, :]

    west_lanes = jnp.logical_and(jnp.logical_and(lane >= 2, lane <= 4), has_w)
    east_lanes = jnp.logical_and(jnp.logical_and(lane >= 123, lane <= 125), has_e)
    top, bottom = jnp.logical_and(sub == 0, has_n), jnp.logical_and(sub == 7, has_s)

    def spread(row):
        return jnp.broadcast_to(row, (8, LANES))

    @pl.loop(0, steps)
    def _(n):
        now = [[None] * VR for _ in range(3)]
        for v in range(VR):
            at = slice(8 * v, 8 * v + 8)
            for g in range(3):
                here = pl.ds(pl.multiple_of(n * ROWS_L + 8 * v, 8), 8)
                total = co[0, g, at, :] * waves[g, here, :]
                if g == 0:
                    total += jnp.where(west_lanes, turn(from_w[at, :], 2 - 4 * n + 4 * LANES), 0.0)
                if g == 2:
                    total += jnp.where(east_lanes, turn(from_e[at, :], 123 - 4 * n + 4 * LANES), 0.0)
                if 2 <= v <= 4:
                    one = pl.ds(n, 1)
                    total += jnp.where(top, spread(from_n[g, v - 2, one, :]), 0.0)
                    total += jnp.where(bottom, spread(from_s[g, v - 2, one, :]), 0.0)
                    if g == 0:
                        for flag, ref in ((top, from_nw), (bottom, from_sw)):
                            piece = turn(spread(ref[v - 2, one, :]), 2 - 124)
                            total += jnp.where(jnp.logical_and(flag, west_lanes), piece, 0.0)
                    if g == 2:
                        for flag, ref in ((top, from_ne), (bottom, from_se)):
                            piece = turn(spread(ref[v - 2, one, :]), 123 - 1)
                            total += jnp.where(jnp.logical_and(flag, east_lanes), piece, 0.0)
                now[g][v] = total * co[1, g, at, :]
        out = [[None] * VR for _ in range(3)]
        for g in range(3):
            for v in range(VR):
                at = slice(8 * v, 8 * v + 8)
                cur = now[g][v]
                down = now[g][v + 1] if v < VR - 1 else pltpu.roll(now[g][0], 7, 0)
                up = now[g][v - 1] if v else pltpu.roll(now[g][VR - 1], 1, 0)
                image = (
                    co[2, g, at, :] * cur
                    - co[3, g, at, :] * turn(cur, LANES - 1)
                    - co[4, g, at, :] * turn(cur, 1)
                    - co[5, g, at, :] * down
                    - co[6, g, at, :] * up
                )
                out[g][v] = co[7, g, at, :] * before[g, v] - image
                before[g, v] = cur
        for v in range(VR):
            at = pl.ds(n * ROWS_L + v, 8, stride=VR)
            for ref, values in ((settled, now), (rest, out)):
                a, b, c = values[0][v], values[1][v], values[2][v]
                mid = turn(b, 64)
                ref[0, at, :] = jnp.where(lane < SPLIT_AB - HALO, turn(a, -HALO), mid)
                ref[1, at, :] = jnp.where(lane < SPLIT_BC - 131, mid, turn(c, HALO))

    def add_row(row, total):
        rest_at = pl.ds(row + HALO, steps, stride=ROWS_L)
        src_at = pl.ds(row, steps, stride=rows)
        values = jnp.concatenate([rest[h, rest_at, :] + src[h][src_at, :] for h in range(2)], 1)
        high = values.astype(BF16)
        low = (values - high.astype(F32)).astype(BF16)
        hot = one_hot_of(agg[pl.ds(row, 1), :], aggs, tile * aggs)
        return total + lax.dot_general(
            jnp.concatenate([high, low], 0), hot, (((1,), (1,)), ((), ())),
            preferred_element_type=F32,
        )

    def add_rows(i, total):
        for k in range(4):
            total = add_row(4 * i + k, total)
        return total

    total = lax.fori_loop(0, rows // 4, add_rows, jnp.zeros((2 * steps, aggs), F32))
    total = total[:steps] + total[steps:]
    coarse[...] = jnp.concatenate([total[: steps // 2], total[steps // 2 :]], 1)


def gather_kernel(axes, own, everyone, send, recv, local):
    n_x, n_y = axes
    count = n_x * n_y
    me = lax.axis_index("gx") * n_y + lax.axis_index("gy")

    def other(i):
        which = lax.rem(me + i, count)
        return which // n_y, lax.rem(which, n_y)

    barrier = pltpu.get_barrier_semaphore()

    @pl.loop(1, count)
    def _(i):
        pl.semaphore_signal(barrier, inc=1, device_id=other(i), device_id_type=MESH)

    pl.semaphore_wait(barrier, count - 1)
    mine = pltpu.make_async_copy(own, everyone.at[me], local)
    mine.start()

    def copy(i):
        return pltpu.make_async_remote_copy(
            src_ref=own, dst_ref=everyone.at[me], send_sem=send.at[i], recv_sem=recv.at[i],
            device_id=other(i), device_id_type=MESH,
        )

    @pl.loop(1, count)
    def _(i):
        copy(i).start()

    @pl.loop(1, count)
    def _(i):
        source = lax.rem(me + count - i, count)
        pltpu.make_async_remote_copy(
            src_ref=own, dst_ref=everyone.at[source], send_sem=send.at[i], recv_sem=recv.at[i],
            device_id=other(i), device_id_type=MESH,
        ).wait()

    mine.wait()


def gather(axes, ident, own):
    count = axes[0] * axes[1]
    return pl.pallas_call(
        functools.partial(gather_kernel, axes),
        out_shape=jax.ShapeDtypeStruct((count,) + own.shape, F32),
        in_specs=[pl.BlockSpec(memory_space=pl.ANY)],
        out_specs=pl.BlockSpec(memory_space=pl.ANY),
        scratch_shapes=[
            pltpu.SemaphoreType.DMA((count,)),
            pltpu.SemaphoreType.DMA((count,)),
            pltpu.SemaphoreType.DMA,
        ],
        compiler_params=pltpu.CompilerParams(collective_id=ident, has_side_effects=True),
        name="coarse_gather",
    )(own)


def correct_kernel(axes, steps, rows, aggs, everyone, inverse, agg, settled, out, fixed):
    tile = lax.axis_index("gx") * axes[1] + lax.axis_index("gy")
    count = axes[0] * axes[1]

    @pl.when(pl.program_id(0) == 0)
    def _():
        low_lanes = lax.broadcasted_iota(jnp.int32, (steps // 2, LANES), 1) < aggs
        total = jnp.zeros((steps, aggs), F32)
        for d in range(0, count, 2):
            a, b = everyone[d], everyone[d + 1]
            upper = jnp.where(low_lanes, a, pltpu.roll(b, aggs, 1))
            lower = jnp.where(low_lanes, pltpu.roll(a, aggs, 1), b)
            total += lax.dot_general(
                jnp.concatenate([upper, lower], 0),
                inverse[:, d * aggs : (d + 2) * aggs],
                (((1,), (1,)), ((), ())),
                precision=lax.Precision.HIGHEST,
                preferred_element_type=F32,
            )
        high = total.astype(BF16)
        low = (total - high.astype(F32)).astype(BF16)
        fixed[...] = jnp.concatenate([high, low], 1)

    factor = fixed[...]

    @pl.loop(0, rows // 4)
    def _(i):
        for k in range(4):
            row = 4 * i + k
            hot = one_hot_of(agg[pl.ds(row, 1), :], aggs, tile * aggs)
            grown = jnp.dot(
                factor, jnp.concatenate([hot, hot], 0), preferred_element_type=F32
            )
            out[pl.ds(row, steps, stride=rows), :] = (
                settled[0, pl.ds(row + HALO, steps, stride=ROWS_L), :] + grown
            )


def halves(shape):
    block = (shape[0], LANES)
    return [pl.BlockSpec(block, lambda i: (0, 0)), pl.BlockSpec(block, lambda i: (0, 1))]


def whole(shape):
    return pl.BlockSpec(shape, lambda i: (0,) * len(shape))


def shards(axes, prev_wave, source, start_state, storage, leakage, cond_east, cond_south,
           owner_weight, aggregate, coarse_inverse):
    steps, rows, cols = prev_wave.shape
    aggs = coarse_inverse.shape[0]
    planes = 2 * steps + 8
    flat = (steps * rows, cols)
    prev, src = prev_wave.reshape(flat), source.reshape(flat)
    coef = (start_state, storage, leakage, cond_east, cond_south, owner_weight)
    params = pltpu.CompilerParams(vmem_limit_bytes=VMEM_LIMIT)
    fields, field_specs = [], []
    for arr in (prev, src) + coef:
        fields += [arr, arr]
        field_specs += halves(arr.shape)

    def local(kernel, name, args, in_specs, outs, scratch):
        return pl.pallas_call(
            kernel,
            grid=(1,),
            out_shape=[jax.ShapeDtypeStruct(s, F32) for s in outs],
            in_specs=in_specs,
            out_specs=[whole(s) for s in outs],
            scratch_shapes=scratch,
            compiler_params=params,
            name=name,
        )(*args)

    strips = local(
        functools.partial(pack_kernel, axes, steps, rows), "halo_pack", fields, field_specs,
        [(3, rows, LANES)] * 2 + [(cols // LANES, HALO, planes, LANES)] * 2, [],
    )
    halo = exchange(axes, 0, *strips)
    waves, co, *rims = local(
        functools.partial(sweep_kernel, axes, steps, rows), "local_sweep",
        fields + list(halo), field_specs + [whole(h.shape) for h in halo],
        [(3, steps * ROWS_L, LANES), (9, 3, ROWS_L, LANES)]
        + [(ROWS_L, LANES)] * 2 + [(3, HALO, steps, LANES)] * 2,
        [
            pltpu.VMEM((3, planes * ROWS_L, LANES), F32),
            pltpu.VMEM((8, 3, VR, 8, LANES), F32),
            pltpu.VMEM((3, VR, 8, LANES), F32),
            pltpu.VMEM((3, VR, 8, LANES), F32),
        ],
    )
    rim = exchange(axes, 1, *rims)
    args = [waves, co, *rim]
    settled, coarse = local(
        functools.partial(settle_kernel, axes, steps, rows, aggs), "settle_and_restrict",
        args + [src, src, aggregate],
        [whole(a.shape) for a in args] + halves(flat) + [whole(aggregate.shape)],
        [(2, steps * ROWS_L, LANES), (steps // 2, 2 * aggs)],
        [pltpu.VMEM((3, VR, 8, LANES), F32), pltpu.VMEM((2, steps * ROWS_L, LANES), F32)],
    )
    everyone = gather(axes, 2, coarse)
    out = pl.pallas_call(
        functools.partial(correct_kernel, axes, steps, rows, aggs),
        grid=(2,),
        out_shape=jax.ShapeDtypeStruct(flat, F32),
        in_specs=[
            whole(everyone.shape),
            whole(coarse_inverse.shape),
            pl.BlockSpec((rows, LANES), lambda i: (0, i)),
            pl.BlockSpec((1, steps * ROWS_L, LANES), lambda i: (i, 0, 0)),
        ],
        out_specs=pl.BlockSpec((steps * rows, LANES), lambda i: (0, i)),
        scratch_shapes=[pltpu.VMEM((steps, 2 * aggs), BF16)],
        compiler_params=params,
        name="correct",
    )(everyone, coarse_inverse, aggregate, settled)
    return out.reshape(prev_wave.shape)


def solution(mesh):
    axes = (mesh.shape["gx"], mesh.shape["gy"])
    plane = P("gy", "gx")
    wave = P(None, "gy", "gx")
    return jax.shard_map(
        functools.partial(shards, axes),
        mesh=mesh,
        in_specs=(wave, wave) + (plane,) * 7 + (P(("gx", "gy"), None),),
        out_specs=wave,
        check_vma=False,
    )
```

```python
import functools

import jax
import jax.numpy as jnp
from jax import lax
from jax.experimental import pallas as pl
from jax.experimental.pallas import tpu as pltpu
from jax.sharding import PartitionSpec as P

DEG = 8
OV = 2
HALO = OV + 1
LANES = 128
VR = 9
ROWS_L = 8 * VR
COEFS = 6
DELTA = 0.95
SIGMA = 1.0 / DELTA
OFFSETS = (0, 67, 134)
SPLIT_AB, SPLIT_BC = 98, 164
F32 = jnp.float32
BF16 = jnp.bfloat16
MESH = pl.DeviceIdType.MESH
VMEM_LIMIT = 56 * 1024 * 1024


def lane_id():
    return lax.broadcasted_iota(jnp.int32, (8, LANES), 1)


def sub_id():
    return lax.broadcasted_iota(jnp.int32, (8, LANES), 0)


def turn(x, by):
    by = by % LANES
    return pltpu.roll(x, by, 1) if not (isinstance(by, int) and by == 0) else x


def position(axes):
    gx, gy = lax.axis_index("gx"), lax.axis_index("gy")
    return gx > 0, gx < axes[0] - 1, gy > 0, gy < axes[1] - 1


def masked_coefs(refs, rows, half, axes, first_row):
    _, has_e, _, has_s = position(axes)
    start, sto, leak, east, south, owner = [ref[rows, :] for ref in refs]
    if half == 1:
        cut = jnp.logical_and(lane_id() == LANES - 1, jnp.logical_not(has_e))
        east = jnp.where(cut, 0.0, east)
    cut = jnp.logical_and(sub_id() + first_row == 63, jnp.logical_not(has_s))
    south = jnp.where(cut, 0.0, south)
    return start, sto, leak, east, south, owner.astype(F32)


def pack_kernel(axes, steps, rows, *refs):
    prev, src = refs[0:2], refs[2:4]
    coef = [refs[4 + 2 * p : 6 + 2 * p] for p in range(COEFS)]
    xw, xe, yn, ys, *corners = refs[4 + 2 * COEFS :]
    group = lane_id() // 4

    @pl.loop(0, rows // 8)
    def _(t):
        first = pl.multiple_of(t * 8, 8)
        for k, arr in enumerate((prev, src)):
            low = jnp.zeros((8, LANES), F32)
            high = jnp.zeros((8, LANES), F32)
            for n in range(steps):
                at = pl.ds(pl.multiple_of(n * rows + first, 8), 8)
                low = jnp.where(group == n, turn(arr[0][at, :], 4 * n), low)
                high = jnp.where(group == n, turn(arr[1][at, :], 4 * n - 125), high)
            xw[k, pl.ds(first, 8), :] = low
            xe[k, pl.ds(first, 8), :] = high
        at = pl.ds(first, 8)
        low = jnp.zeros((8, LANES), F32)
        high = jnp.zeros((8, LANES), F32)
        planes0 = masked_coefs([c[0] for c in coef], at, 0, axes, first)
        planes1 = masked_coefs([c[1] for c in coef], at, 1, axes, first)
        for p in range(COEFS):
            low = jnp.where(group == p, turn(planes0[p], 4 * p), low)
            high = jnp.where(group == p, turn(planes1[p], 4 * p - 125), high)
        xw[2, at, :] = low
        xe[2, at, :] = high

    for side, (out, first, base) in enumerate(((yn, 0, 0), (ys, rows - HALO, rows - 8))):
        for h in range(2):
            planes = masked_coefs([c[h] for c in coef], pl.ds(base, 8), h, axes, base)
            corner = jnp.zeros((8, LANES), F32)
            for q, j, at in strip_blocks(steps, side):
                if q < 2 * steps // 8:
                    arr, part = (prev, q) if q < steps // 8 else (src, q - steps // 8)
                    value = arr[h][pl.ds(8 * part * rows + first + j, 8, stride=rows), :]
                else:
                    row = first + j - base
                    pieces = [p[row : row + 1] for p in planes]
                    value = jnp.concatenate(pieces + [jnp.zeros((8 - COEFS, LANES), F32)], 0)
                out[h, at : at + 8, :] = value
                slot = 4 * (HALO * q + j)
                corner = jnp.where(group == slot // 4, turn(value, slot - (0, 125)[h]), corner)
            corners[2 * side + h][...] = corner


def strip_blocks(steps, side):
    at, blocks = 0, []
    for q in range(2 * steps // 8 + 1):
        for j in range(HALO):
            if steps // 8 <= q < 2 * steps // 8 and j == (HALO - 1, 0)[side]:
                continue
            blocks.append((q, j, at))
            at += 8
    return blocks


def exchange_kernel(axes, xw, xe, yn, ys, c_nw, c_ne, c_sw, c_se, *refs):
    outs = refs[:8]
    send, recv = refs[8:]
    gx, gy = lax.axis_index("gx"), lax.axis_index("gy")
    has_w, has_e, has_n, has_s = position(axes)
    west, east, north, south = gx - 1, gx + 1, gy - 1, gy + 1
    both = jnp.logical_and
    has_nw, has_ne = both(has_n, has_w), both(has_n, has_e)
    has_sw, has_se = both(has_s, has_w), both(has_s, has_e)
    from_w, from_e, from_n, from_s, from_nw, from_ne, from_sw, from_se = outs
    plan = (
        (yn, from_s, (gx, north), has_n, has_s),
        (ys, from_n, (gx, south), has_s, has_n),
        (xw, from_e, (west, gy), has_w, has_e),
        (xe, from_w, (east, gy), has_e, has_w),
        (c_nw, from_se, (west, north), has_nw, has_se),
        (c_ne, from_sw, (east, north), has_ne, has_sw),
        (c_sw, from_ne, (west, south), has_sw, has_ne),
        (c_se, from_nw, (east, south), has_se, has_nw),
    )
    barrier = pltpu.get_barrier_semaphore()
    copies = []
    for i, (src, dst, to, goes, comes) in enumerate(plan):

        @pl.when(goes)
        def _():
            pl.semaphore_signal(barrier, inc=1, device_id=to, device_id_type=MESH)

        copy = pltpu.make_async_remote_copy(
            src_ref=src, dst_ref=dst, send_sem=send.at[i], recv_sem=recv.at[i],
            device_id=to, device_id_type=MESH,
        )
        copies.append((copy, goes, comes))
    pl.semaphore_wait(barrier, sum(jnp.where(step[3], 1, 0) for step in plan))
    for copy, goes, _ in copies:
        pl.when(goes)(copy.start)
    for copy, goes, comes in copies:
        pl.when(goes)(copy.wait_send)
        pl.when(comes)(copy.wait_recv)


def exchange(axes, ident, *strips):
    return pl.pallas_call(
        functools.partial(exchange_kernel, axes),
        out_shape=[jax.ShapeDtypeStruct(s.shape, F32) for s in strips],
        in_specs=[pl.BlockSpec(memory_space=pl.ANY)] * 8,
        out_specs=[pl.BlockSpec(memory_space=pl.ANY)] * 8,
        scratch_shapes=[pltpu.SemaphoreType.DMA((8,)), pltpu.SemaphoreType.DMA((8,))],
        compiler_params=pltpu.CompilerParams(collective_id=ident, has_side_effects=True),
        name="neighbour_exchange",
    )(*strips)


def lay(a, b, west, east):
    lane = lane_id()
    first = jnp.where(lane < HALO, west, turn(a, HALO))
    mid = jnp.where(lane < 64, turn(a, 64), turn(b, 64))
    last = jnp.where(lane >= LANES - HALO, turn(east, LANES - HALO), turn(b, LANES - HALO))
    return first, mid, last


def unlay(a, b, c):
    lane, mid = lane_id(), turn(b, 64)
    return (
        jnp.where(lane < SPLIT_AB - HALO, turn(a, -HALO), mid),
        jnp.where(lane < SPLIT_BC - 131, mid, turn(c, HALO)),
    )


def sweep_kernel(axes, steps, rows, *refs):
    prev, src = refs[0:2], refs[2:4]
    coef = [refs[4 + 2 * p : 6 + 2 * p] for p in range(COEFS)]
    base = 4 + 2 * COEFS
    from_w, from_e, from_n, from_s, from_nw, from_ne, from_sw, from_se = refs[base : base + 8]
    waves, co, xw, xe, yn, ys = refs[base + 8 : base + 14]
    corners = refs[base + 14 : base + 18]
    ext, cc, gbuf, carry, north_rows, south_rows = refs[base + 18 :]
    has_w, has_e, has_n, has_s = position(axes)
    lane, sub = lane_id(), sub_id()
    zero = jnp.zeros((8, LANES), F32)

    def keep(flag, value):
        return jnp.where(flag, value, 0.0)

    def put_own(plane, t, a, b, k, slot):
        at = pl.ds(t * 8, 8)
        west = keep(has_w, turn(from_w[k, at, :], -4 * slot + LANES * 4))
        east = keep(has_e, turn(from_e[k, at, :], -4 * slot + LANES * 4))
        for g, value in enumerate(lay(a, b, west, east)):
            ext[g, pl.ds(plane * ROWS_L + HALO + 8 * t, 8), :] = value

    @pl.loop(0, steps)
    def _(n):
        for k, arr in enumerate((prev, src)):
            for t in range(rows // 8):
                at = pl.ds(pl.multiple_of(n * rows + 8 * t, 8), 8)
                put_own(k * steps + n, t, arr[0][at, :], arr[1][at, :], k, n)

    for t in range(rows // 8):
        at = pl.ds(8 * t, 8)
        planes0 = masked_coefs([c[0] for c in coef], at, 0, axes, 8 * t)
        planes1 = masked_coefs([c[1] for c in coef], at, 1, axes, 8 * t)
        for p in range(COEFS):
            put_own(2 * steps + p, t, planes0[p], planes1[p], 2, p)
    for side, (strip, cw, ce, flag, first) in enumerate((
        (from_n, from_nw, from_ne, has_n, 0),
        (from_s, from_sw, from_se, has_s, rows + HALO),
    )):
        for q, j, at in strip_blocks(steps, 1 - side):
            a = keep(flag, strip[0, at : at + 8, :])
            b = keep(flag, strip[1, at : at + 8, :])
            slot = 4 * (HALO * q + j)
            west = keep(jnp.logical_and(flag, has_w), turn(cw[...], -slot))
            east = keep(jnp.logical_and(flag, has_e), turn(ce[...], -slot))
            for g, value in enumerate(lay(a, b, west, east)):
                ext[g, pl.ds(8 * q * ROWS_L + first + j, 8, stride=ROWS_L), :] = value
    for row in (0, rows + 2 * HALO - 1):
        for q in range(steps // 8, 2 * steps // 8):
            for g in range(3):
                ext[g, pl.ds(8 * q * ROWS_L + row, 8, stride=ROWS_L), :] = zero
    for row in range(rows + 2 * HALO, ROWS_L):
        for q in range(2 * steps // 8 + 1):
            for g in range(3):
                ext[g, pl.ds(8 * q * ROWS_L + row, 8, stride=ROWS_L), :] = zero

    def plane(index, v, g):
        return ext[g, pl.ds(index * ROWS_L + v, 8, stride=VR), :]

    first_coef = 2 * steps
    for g in range(3):
        col = lane + OFFSETS[g]
        col_in = jnp.logical_and(col >= 1, col <= 260)
        col_own = jnp.logical_and(col >= HALO, col <= 258)
        col_there = jnp.logical_and(
            jnp.logical_or(col >= HALO, has_w), jnp.logical_or(col <= 258, has_e)
        )
        n_cols = (
            1.0
            + jnp.where(jnp.logical_and(col <= 4, has_w), 1.0, 0.0)
            + jnp.where(jnp.logical_and(col >= 257, has_e), 1.0, 0.0)
        )
        souths = [plane(first_coef + 4, v, g) for v in range(VR)]
        for v in range(VR):
            row = sub * VR + v
            row_in = jnp.logical_and(row >= 1, row <= 68)
            row_own = jnp.logical_and(row >= HALO, row <= 66)
            row_there = jnp.logical_and(
                jnp.logical_or(row >= HALO, has_n), jnp.logical_or(row <= 66, has_s)
            )
            inner = jnp.logical_and(row_in, col_in)
            own = jnp.logical_and(row_own, col_own)
            there = jnp.logical_and(jnp.logical_and(row_there, col_there), inner)
            n_rows = (
                1.0
                + jnp.where(jnp.logical_and(row <= 4, has_n), 1.0, 0.0)
                + jnp.where(jnp.logical_and(row >= 65, has_s), 1.0, 0.0)
            )
            start, sto, leak, east, south, owner = [
                plane(first_coef + p, v, g) for p in range(COEFS)
            ]
            ea_w = turn(east, 1)
            so_n = souths[v - 1] if v else pltpu.roll(souths[VR - 1], 1, 0)
            diag = sto + leak + east + ea_w + south + so_n
            safe = jnp.where(there, diag, 1.0)
            scale = jnp.where(there, 2.0 * SIGMA / safe, 0.0)
            cc[0, g, v] = jnp.where(lane == LANES - 1, 0.0, scale * east)
            cc[1, g, v] = jnp.where(lane == 0, 0.0, scale * ea_w)
            cc[2, g, v] = scale * south
            cc[3, g, v] = scale * so_n
            cc[4, g, v] = scale
            cc[5, g, v] = scale * sto
            cc[6, g, v] = jnp.where(inner, 0.0, 2.0 * SIGMA)
            weight = jnp.where(own, owner, jnp.where(there, 1.0, 0.0))
            cc[7, g, v] = weight * (1.0 / TAU[DEG])
            den = jnp.where(there, owner + n_rows * n_cols - 1.0, 1.0)
            at = slice(8 * v, 8 * v + 8)
            co[0, g, at, :] = weight
            co[1, g, at, :] = jnp.where(there, 1.0 / den, 0.0)
            co[2, g, at, :] = diag
            co[3, g, at, :] = east
            co[4, g, at, :] = ea_w
            co[5, g, at, :] = south
            co[6, g, at, :] = so_n
            co[7, g, at, :] = sto
            co[8, g, at, :] = start
            carry[g, v] = start

    xw[...] = jnp.zeros_like(xw)
    xe[...] = jnp.zeros_like(xe)
    group = lane // 4

    def stencil(y, g, v):
        cur = y[g][v]
        down = y[g][v + 1] if v < VR - 1 else pltpu.roll(y[g][0], 7, 0)
        up = y[g][v - 1] if v else pltpu.roll(y[g][VR - 1], 1, 0)
        return (
            cc[0, g, v] * turn(cur, LANES - 1)
            + cc[1, g, v] * turn(cur, 1)
            + (cc[2, g, v] * down + cc[3, g, v] * up)
        )

    def advance(n, held):
        old = [[None] * VR for _ in range(3)]
        for g in range(3):
            for v in range(VR):
                old[g][v] = plane(n, v, g)
                gbuf[g, v] = (
                    cc[4, g, v] * plane(steps + n, v, g)
                    + cc[5, g, v] * held[g][v]
                    + cc[6, g, v] * old[g][v]
                )
        now = [
            [0.5 * (stencil(old, g, v) + gbuf[g, v]) for v in range(VR)] for g in range(3)
        ]
        for k in range(1, DEG):
            new = [
                [stencil(now, g, v) + (TAU[k] * gbuf[g, v] - old[g][v]) for v in range(VR)]
                for g in range(3)
            ]
            old, now = now, new
        return now

    def finish(n, now):
        for g in range(3):
            for v in range(VR):
                at = pl.ds(pl.multiple_of(n * ROWS_L + 8 * v, 8), 8)
                waves[g, at, :] = now[g][v] * (1.0 / TAU[DEG])
        weighted = [[cc[7, g, v] * now[g][v] for v in range(VR)] for g in range(3)]
        for v in range(VR):
            at = slice(8 * v, 8 * v + 8)
            xw[at, :] = jnp.where(group == n, turn(weighted[0][v], 4 * n + LANES - 1), xw[at, :])
            xe[at, :] = jnp.where(group == n, turn(weighted[2][v], 4 * n + 4), xe[at, :])
        for j in range(HALO):
            for g in range(3):
                north_rows[g, pl.ds(j * steps + n, 1), :] = weighted[g][1 + j][0:1]
                south_rows[g, pl.ds(j * steps + n, 1), :] = weighted[g][3 + j][7:8]
        return [[now[g][v] * (1.0 / TAU[DEG]) for v in range(VR)] for g in range(3)]

    @pl.loop(0, steps)
    def _(n):
        held = [[carry[g, v] for v in range(VR)] for g in range(3)]
        held = finish(n, advance(n, held))
        for v in range(VR):
            a, b, c = held[0][v], held[1][v], held[2][v]
            carry[0, v] = jnp.where(lane < SPLIT_AB, a, turn(b, 67))
            left = jnp.where(lane < SPLIT_AB - 67, turn(a, 61), b)
            carry[1, v] = jnp.where(lane < SPLIT_BC - 67, left, turn(c, 67))
            carry[2, v] = jnp.where(lane < SPLIT_BC - 134, turn(b, 61), c)

    for side, (rows_of, out) in enumerate(((north_rows, yn), (south_rows, ys))):
        packs = [zero, zero]
        for i in range(HALO * steps // 8):
            at = slice(8 * i, 8 * i + 8)
            a, b, c = [rows_of[g, at, :] for g in range(3)]
            out[0, at, :], out[1, at, :] = unlay(a, b, c)
            packs[0] = jnp.where(group == i, turn(a, 4 * i - 1), packs[0])
            packs[1] = jnp.where(group == i, turn(c, 4 * i - 124), packs[1])
        for h in range(2):
            out[h, HALO * steps : HALO * steps + 8, :] = packs[h]
            corners[2 * side + h][...] = packs[h]


def chebyshev_scales():
    tau = [1.0, SIGMA]
    for _ in range(DEG):
        tau.append(2.0 * SIGMA * tau[-1] - tau[-2])
    return tau


TAU = chebyshev_scales()


def one_hot_of(row, count, first):
    ids = jnp.broadcast_to(row - first, (count, row.shape[1]))
    return jnp.where(
        ids == lax.broadcasted_iota(jnp.int32, ids.shape, 0), 1.0, 0.0
    ).astype(BF16)


def settle_kernel(axes, steps, rows, aggs, *refs):
    waves, co, from_w, from_e, from_n, from_s, from_nw, from_ne, from_sw, from_se = refs[:10]
    src = refs[10:12]
    agg = refs[12]
    settled, coarse = refs[13:15]
    before, rest, north, south = refs[15:]
    has_w, has_e, has_n, has_s = position(axes)
    lane, sub = lane_id(), sub_id()
    tile = lax.axis_index("gx") * axes[1] + lax.axis_index("gy")

    for g in range(3):
        for v in range(VR):
            before[g, v] = co[8, g, 8 * v : 8 * v + 8, :]

    west_lanes = jnp.logical_and(jnp.logical_and(lane >= 2, lane <= 4), has_w)
    east_lanes = jnp.logical_and(jnp.logical_and(lane >= 123, lane <= 125), has_e)

    def spread(row):
        return jnp.broadcast_to(row, (8, LANES))

    for strip, cw, ce, flag, out in (
        (from_n, from_nw, from_ne, has_n, north),
        (from_s, from_sw, from_se, has_s, south),
    ):
        for i in range(HALO * steps // 8):
            at = slice(8 * i, 8 * i + 8)
            edge = slice(HALO * steps, HALO * steps + 8)
            west, east = turn(strip[0, edge, :], 1 - 4 * i), turn(strip[1, edge, :], -1 - 4 * i)
            a, b, c = lay(strip[0, at, :], strip[1, at, :], west, east)
            a += jnp.where(west_lanes, turn(cw[...], 2 - 4 * i), 0.0)
            c += jnp.where(east_lanes, turn(ce[...], 123 - 4 * i), 0.0)
            for g, value in enumerate((a, b, c)):
                out[g, at, :] = jnp.where(flag, value, 0.0)

    @pl.loop(0, steps)
    def _(n):
        now = [[None] * VR for _ in range(3)]
        for v in range(VR):
            at = slice(8 * v, 8 * v + 8)
            for g in range(3):
                here = pl.ds(pl.multiple_of(n * ROWS_L + 8 * v, 8), 8)
                total = co[0, g, at, :] * waves[g, here, :]
                if g == 0:
                    total += jnp.where(west_lanes, turn(from_w[at, :], 2 - 4 * n + 4 * LANES), 0.0)
                if g == 2:
                    total += jnp.where(east_lanes, turn(from_e[at, :], 123 - 4 * n + 4 * LANES), 0.0)
                if 2 <= v <= 4:
                    one = pl.ds((v - 2) * steps + n, 1)
                    total += jnp.where(sub == 0, spread(north[g, one, :]), 0.0)
                    total += jnp.where(sub == 7, spread(south[g, one, :]), 0.0)
                now[g][v] = total * co[1, g, at, :]
        out = [[None] * VR for _ in range(3)]
        for g in range(3):
            for v in range(VR):
                at = slice(8 * v, 8 * v + 8)
                cur = now[g][v]
                down = now[g][v + 1] if v < VR - 1 else pltpu.roll(now[g][0], 7, 0)
                up = now[g][v - 1] if v else pltpu.roll(now[g][VR - 1], 1, 0)
                image = (
                    co[2, g, at, :] * cur
                    - co[3, g, at, :] * turn(cur, LANES - 1)
                    - co[4, g, at, :] * turn(cur, 1)
                    - co[5, g, at, :] * down
                    - co[6, g, at, :] * up
                )
                out[g][v] = co[7, g, at, :] * before[g, v] - image
                before[g, v] = cur
        for v in range(VR):
            at = pl.ds(n * ROWS_L + v, 8, stride=VR)
            for ref, values in ((settled, now), (rest, out)):
                ref[0, at, :], ref[1, at, :] = unlay(*[value[v] for value in values])

    def add_row(row, total):
        rest_at = pl.ds(row + HALO, steps, stride=ROWS_L)
        src_at = pl.ds(row, steps, stride=rows)
        values = jnp.concatenate([rest[h, rest_at, :] + src[h][src_at, :] for h in range(2)], 1)
        high = values.astype(BF16)
        low = (values - high.astype(F32)).astype(BF16)
        hot = one_hot_of(agg[pl.ds(row, 1), :], aggs, tile * aggs)
        return total + lax.dot_general(
            jnp.concatenate([high, low], 0), hot, (((1,), (1,)), ((), ())),
            preferred_element_type=F32,
        )

    def add_rows(i, total):
        for k in range(4):
            total = add_row(4 * i + k, total)
        return total

    total = lax.fori_loop(0, rows // 4, add_rows, jnp.zeros((2 * steps, aggs), F32))
    total = total[:steps] + total[steps:]
    coarse[...] = jnp.concatenate([total[: steps // 2], total[steps // 2 :]], 1)


def gather_kernel(axes, own, everyone, send, recv, local):
    n_x, n_y = axes
    count = n_x * n_y
    me = lax.axis_index("gx") * n_y + lax.axis_index("gy")

    def other(i):
        which = lax.rem(me + i, count)
        return which // n_y, lax.rem(which, n_y)

    barrier = pltpu.get_barrier_semaphore()

    @pl.loop(1, count)
    def _(i):
        pl.semaphore_signal(barrier, inc=1, device_id=other(i), device_id_type=MESH)

    pl.semaphore_wait(barrier, count - 1)
    mine = pltpu.make_async_copy(own, everyone.at[me], local)
    mine.start()

    def copy(i):
        return pltpu.make_async_remote_copy(
            src_ref=own, dst_ref=everyone.at[me], send_sem=send.at[i], recv_sem=recv.at[i],
            device_id=other(i), device_id_type=MESH,
        )

    @pl.loop(1, count)
    def _(i):
        copy(i).start()

    @pl.loop(1, count)
    def _(i):
        source = lax.rem(me + count - i, count)
        pltpu.make_async_remote_copy(
            src_ref=own, dst_ref=everyone.at[source], send_sem=send.at[i], recv_sem=recv.at[i],
            device_id=other(i), device_id_type=MESH,
        ).wait()

    mine.wait()


def gather(axes, ident, own):
    count = axes[0] * axes[1]
    return pl.pallas_call(
        functools.partial(gather_kernel, axes),
        out_shape=jax.ShapeDtypeStruct((count,) + own.shape, F32),
        in_specs=[pl.BlockSpec(memory_space=pl.ANY)],
        out_specs=pl.BlockSpec(memory_space=pl.ANY),
        scratch_shapes=[
            pltpu.SemaphoreType.DMA((count,)),
            pltpu.SemaphoreType.DMA((count,)),
            pltpu.SemaphoreType.DMA,
        ],
        compiler_params=pltpu.CompilerParams(collective_id=ident, has_side_effects=True),
        name="coarse_gather",
    )(own)


def correct_kernel(axes, steps, rows, aggs, everyone, inverse, agg, settled, out, fixed):
    tile = lax.axis_index("gx") * axes[1] + lax.axis_index("gy")
    count = axes[0] * axes[1]

    @pl.when(pl.program_id(0) == 0)
    def _():
        low_lanes = lax.broadcasted_iota(jnp.int32, (steps // 2, LANES), 1) < aggs
        total = jnp.zeros((steps, aggs), F32)
        for d in range(0, count, 2):
            a, b = everyone[d], everyone[d + 1]
            upper = jnp.where(low_lanes, a, pltpu.roll(b, aggs, 1))
            lower = jnp.where(low_lanes, pltpu.roll(a, aggs, 1), b)
            total += lax.dot_general(
                jnp.concatenate([upper, lower], 0),
                inverse[:, d * aggs : (d + 2) * aggs],
                (((1,), (1,)), ((), ())),
                precision=lax.Precision.HIGHEST,
                preferred_element_type=F32,
            )
        high = total.astype(BF16)
        low = (total - high.astype(F32)).astype(BF16)
        fixed[...] = jnp.concatenate([high, low], 1)

    factor = fixed[...]

    @pl.loop(0, rows // 4)
    def _(i):
        for k in range(4):
            row = 4 * i + k
            hot = one_hot_of(agg[pl.ds(row, 1), :], aggs, tile * aggs)
            grown = jnp.dot(
                factor, jnp.concatenate([hot, hot], 0), preferred_element_type=F32
            )
            out[pl.ds(row, steps, stride=rows), :] = (
                settled[0, pl.ds(row + HALO, steps, stride=ROWS_L), :] + grown
            )


def halves(shape):
    block = (shape[0], LANES)
    return [pl.BlockSpec(block, lambda i: (0, 0)), pl.BlockSpec(block, lambda i: (0, 1))]


def whole(shape):
    return pl.BlockSpec(shape, lambda i: (0,) * len(shape))


def shards(axes, prev_wave, source, start_state, storage, leakage, cond_east, cond_south,
           owner_weight, aggregate, coarse_inverse):
    steps, rows, cols = prev_wave.shape
    aggs = coarse_inverse.shape[0]
    planes = 2 * steps + 8
    strip_rows = HALO * planes - steps
    rim_rows = HALO * steps
    flat = (steps * rows, cols)
    prev, src = prev_wave.reshape(flat), source.reshape(flat)
    coef = (start_state, storage, leakage, cond_east, cond_south, owner_weight)
    params = pltpu.CompilerParams(vmem_limit_bytes=VMEM_LIMIT)
    fields, field_specs = [], []
    for arr in (prev, src) + coef:
        fields += [arr, arr]
        field_specs += halves(arr.shape)

    def local(kernel, name, args, in_specs, outs, scratch):
        return pl.pallas_call(
            kernel,
            grid=(1,),
            out_shape=[jax.ShapeDtypeStruct(s, F32) for s in outs],
            in_specs=in_specs,
            out_specs=[whole(s) for s in outs],
            scratch_shapes=scratch,
            compiler_params=params,
            name=name,
        )(*args)

    strips = local(
        functools.partial(pack_kernel, axes, steps, rows), "halo_pack", fields, field_specs,
        [(3, rows, LANES)] * 2 + [(2, strip_rows, LANES)] * 2 + [(8, LANES)] * 4, [],
    )
    halo = exchange(axes, 0, *strips)
    waves, co, *rims = local(
        functools.partial(sweep_kernel, axes, steps, rows), "local_sweep",
        fields + list(halo), field_specs + [whole(h.shape) for h in halo],
        [(3, steps * ROWS_L, LANES), (9, 3, ROWS_L, LANES)]
        + [(ROWS_L, LANES)] * 2 + [(2, rim_rows + 8, LANES)] * 2 + [(8, LANES)] * 4,
        [
            pltpu.VMEM((3, planes * ROWS_L, LANES), F32),
            pltpu.VMEM((8, 3, VR, 8, LANES), F32),
            pltpu.VMEM((3, VR, 8, LANES), F32),
            pltpu.VMEM((3, VR, 8, LANES), F32),
            pltpu.VMEM((3, rim_rows, LANES), F32),
            pltpu.VMEM((3, rim_rows, LANES), F32),
        ],
    )
    rim = exchange(axes, 1, *rims)
    args = [waves, co, *rim]
    settled, coarse = local(
        functools.partial(settle_kernel, axes, steps, rows, aggs), "settle_and_restrict",
        args + [src, src, aggregate],
        [whole(a.shape) for a in args] + halves(flat) + [whole(aggregate.shape)],
        [(2, steps * ROWS_L, LANES), (steps // 2, 2 * aggs)],
        [
            pltpu.VMEM((3, VR, 8, LANES), F32),
            pltpu.VMEM((2, steps * ROWS_L, LANES), F32),
            pltpu.VMEM((3, rim_rows, LANES), F32),
            pltpu.VMEM((3, rim_rows, LANES), F32),
        ],
    )
    everyone = gather(axes, 2, coarse)
    out = pl.pallas_call(
        functools.partial(correct_kernel, axes, steps, rows, aggs),
        grid=(2,),
        out_shape=jax.ShapeDtypeStruct(flat, F32),
        in_specs=[
            whole(everyone.shape),
            whole(coarse_inverse.shape),
            pl.BlockSpec((rows, LANES), lambda i: (0, i)),
            pl.BlockSpec((1, steps * ROWS_L, LANES), lambda i: (i, 0, 0)),
        ],
        out_specs=pl.BlockSpec((steps * rows, LANES), lambda i: (0, i)),
        scratch_shapes=[pltpu.VMEM((steps, 2 * aggs), BF16)],
        compiler_params=params,
        name="correct",
    )(everyone, coarse_inverse, aggregate, settled)
    return out.reshape(prev_wave.shape)


def solution(mesh):
    axes = (mesh.shape["gx"], mesh.shape["gy"])
    plane = P("gy", "gx")
    wave = P(None, "gy", "gx")
    return jax.shard_map(
        functools.partial(shards, axes),
        mesh=mesh,
        in_specs=(wave, wave) + (plane,) * 7 + (P(("gx", "gy"), None),),
        out_specs=wave,
        check_vma=False,
    )
```

```python
import functools

import jax
import jax.numpy as jnp
from jax import lax
from jax.experimental import pallas as pl
from jax.experimental.pallas import tpu as pltpu
from jax.sharding import PartitionSpec as P

DEG = 8
OV = 2
HALO = OV + 1
LANES = 128
VR = 9
ROWS_L = 8 * VR
COEFS = 6
DELTA = 0.95
SIGMA = 1.0 / DELTA
GROUPS = 3
F32 = jnp.float32
BF16 = jnp.bfloat16
MESH = pl.DeviceIdType.MESH
VMEM_LIMIT = 56 * 1024 * 1024


def lane_id():
    return lax.broadcasted_iota(jnp.int32, (8, LANES), 1)


def sub_id():
    return lax.broadcasted_iota(jnp.int32, (8, LANES), 0)


def turn(x, by):
    by = by % LANES
    return pltpu.roll(x, by, 1) if not (isinstance(by, int) and by == 0) else x


def position(axes):
    gx, gy = lax.axis_index("gx"), lax.axis_index("gy")
    return gx > 0, gx < axes[0] - 1, gy > 0, gy < axes[1] - 1


def masked_coefs(refs, rows, half, axes, first_row):
    _, has_e, _, has_s = position(axes)
    start, sto, leak, east, south, owner = [ref[rows, :] for ref in refs]
    if half == 1:
        cut = jnp.logical_and(lane_id() == LANES - 1, jnp.logical_not(has_e))
        east = jnp.where(cut, 0.0, east)
    cut = jnp.logical_and(sub_id() + first_row == 63, jnp.logical_not(has_s))
    south = jnp.where(cut, 0.0, south)
    return start, sto, leak, east, south, owner.astype(F32)


def pack_kernel(axes, steps, rows, *refs):
    prev, src = refs[0:2], refs[2:4]
    coef = [refs[4 + 2 * p : 6 + 2 * p] for p in range(COEFS)]
    xw, xe, yn, ys, *corners = refs[4 + 2 * COEFS :]
    group = lane_id() // 4

    @pl.loop(0, rows // 8)
    def _(t):
        first = pl.multiple_of(t * 8, 8)
        for k, arr in enumerate((prev, src)):
            low = jnp.zeros((8, LANES), F32)
            high = jnp.zeros((8, LANES), F32)
            for n in range(steps):
                at = pl.ds(pl.multiple_of(n * rows + first, 8), 8)
                low = jnp.where(group == n, turn(arr[0][at, :], 4 * n), low)
                high = jnp.where(group == n, turn(arr[1][at, :], 4 * n - 125), high)
            xw[k, pl.ds(first, 8), :] = low
            xe[k, pl.ds(first, 8), :] = high
        at = pl.ds(first, 8)
        low = jnp.zeros((8, LANES), F32)
        high = jnp.zeros((8, LANES), F32)
        planes0 = masked_coefs([c[0] for c in coef], at, 0, axes, first)
        planes1 = masked_coefs([c[1] for c in coef], at, 1, axes, first)
        for p in range(COEFS):
            low = jnp.where(group == p, turn(planes0[p], 4 * p), low)
            high = jnp.where(group == p, turn(planes1[p], 4 * p - 125), high)
        xw[2, at, :] = low
        xe[2, at, :] = high

    for side, (out, first, base) in enumerate(((yn, 0, 0), (ys, rows - HALO, rows - 8))):
        for h in range(2):
            planes = masked_coefs([c[h] for c in coef], pl.ds(base, 8), h, axes, base)
            corner = jnp.zeros((8, LANES), F32)
            for q, j, at in strip_blocks(steps, side):
                if q < 2 * steps // 8:
                    arr, part = (prev, q) if q < steps // 8 else (src, q - steps // 8)
                    value = arr[h][pl.ds(8 * part * rows + first + j, 8, stride=rows), :]
                else:
                    row = first + j - base
                    pieces = [p[row : row + 1] for p in planes]
                    value = jnp.concatenate(pieces + [jnp.zeros((8 - COEFS, LANES), F32)], 0)
                out[h, at : at + 8, :] = value
                slot = 4 * (HALO * q + j)
                corner = jnp.where(group == slot // 4, turn(value, slot - (0, 125)[h]), corner)
            corners[2 * side + h][...] = corner


def strip_blocks(steps, side):
    at, blocks = 0, []
    for q in range(2 * steps // 8 + 1):
        for j in range(HALO):
            if steps // 8 <= q < 2 * steps // 8 and j == (HALO - 1, 0)[side]:
                continue
            blocks.append((q, j, at))
            at += 8
    return blocks


def exchange_kernel(axes, xw, xe, yn, ys, c_nw, c_ne, c_sw, c_se, *refs):
    outs = refs[:8]
    send, recv = refs[8:]
    gx, gy = lax.axis_index("gx"), lax.axis_index("gy")
    has_w, has_e, has_n, has_s = position(axes)
    west, east, north, south = gx - 1, gx + 1, gy - 1, gy + 1
    both = jnp.logical_and
    has_nw, has_ne = both(has_n, has_w), both(has_n, has_e)
    has_sw, has_se = both(has_s, has_w), both(has_s, has_e)
    from_w, from_e, from_n, from_s, from_nw, from_ne, from_sw, from_se = outs
    plan = (
        (yn, from_s, (gx, north), has_n, has_s),
        (ys, from_n, (gx, south), has_s, has_n),
        (xw, from_e, (west, gy), has_w, has_e),
        (xe, from_w, (east, gy), has_e, has_w),
        (c_nw, from_se, (west, north), has_nw, has_se),
        (c_ne, from_sw, (east, north), has_ne, has_sw),
        (c_sw, from_ne, (west, south), has_sw, has_ne),
        (c_se, from_nw, (east, south), has_se, has_nw),
    )
    barrier = pltpu.get_barrier_semaphore()
    copies = []
    for i, (src, dst, to, goes, comes) in enumerate(plan):

        @pl.when(goes)
        def _():
            pl.semaphore_signal(barrier, inc=1, device_id=to, device_id_type=MESH)

        copy = pltpu.make_async_remote_copy(
            src_ref=src, dst_ref=dst, send_sem=send.at[i], recv_sem=recv.at[i],
            device_id=to, device_id_type=MESH,
        )
        copies.append((copy, goes, comes))
    pl.semaphore_wait(barrier, sum(jnp.where(step[3], 1, 0) for step in plan))
    for copy, goes, _ in copies:
        pl.when(goes)(copy.start)
    for copy, goes, comes in copies:
        pl.when(goes)(copy.wait_send)
        pl.when(comes)(copy.wait_recv)


def exchange(axes, ident, *strips):
    return pl.pallas_call(
        functools.partial(exchange_kernel, axes),
        out_shape=[jax.ShapeDtypeStruct(s.shape, F32) for s in strips],
        in_specs=[pl.BlockSpec(memory_space=pl.ANY)] * 8,
        out_specs=[pl.BlockSpec(memory_space=pl.ANY)] * 8,
        scratch_shapes=[pltpu.SemaphoreType.DMA((8,)), pltpu.SemaphoreType.DMA((8,))],
        compiler_params=pltpu.CompilerParams(collective_id=ident, has_side_effects=True),
        name="neighbour_exchange",
    )(*strips)


def spread_matrix(cols):
    shape = (cols, GROUPS * LANES)
    at = lax.broadcasted_iota(jnp.int32, shape, 1)
    col = (at % LANES) * GROUPS + at // LANES - HALO
    return jnp.where(col == lax.broadcasted_iota(jnp.int32, shape, 0), 1.0, 0.0).astype(BF16)


def two_terms(values):
    high = values.astype(BF16)
    return jnp.concatenate([high, (values - high.astype(F32)).astype(BF16)], 0)


def moved(values, matrix, transposed=False):
    dims = (((1,), (1 if transposed else 0,)), ((), ()))
    both = lax.dot_general(two_terms(values), matrix, dims, preferred_element_type=F32)
    return both[: values.shape[0]] + both[values.shape[0] :]


def add_halo(parts, west, east, shift):
    lane = lane_id()
    at_86 = lane == 86
    far = turn(east, 85 + shift)
    return (
        jnp.where(lane == 0, turn(west, shift), jnp.where(lane == 87, far, parts[0])),
        jnp.where(lane == 0, turn(west, shift - 1), jnp.where(at_86, turn(east, 86 + shift), parts[1])),
        jnp.where(lane == 0, turn(west, shift - 2), jnp.where(at_86, far, parts[2])),
    )


def west_edge(parts, to):
    lane = lane_id()
    pair = turn(jnp.where(lane == 0, parts[2], parts[0]), to + 1)
    return jnp.where(lane == to, turn(parts[1], to), pair)


def east_edge(parts, to):
    lane = lane_id()
    last = jnp.where(lane == to + 1, turn(parts[1], to - 85 + LANES), turn(parts[2], to - 84 + LANES))
    return jnp.where(lane == to, turn(parts[0], to - 86 + LANES), last)


def add_west(parts, strip, shift, flag):
    lane, out = lane_id(), list(parts)
    near = jnp.where(flag, turn(strip, shift), 0.0)
    out[2] += jnp.where(lane == 0, near, 0.0)
    out[0] += jnp.where(lane == 1, near, 0.0)
    out[1] += jnp.where(jnp.logical_and(lane == 1, flag), turn(strip, shift - 1), 0.0)
    return out


def add_east(parts, strip, shift, flag):
    lane, out = lane_id(), list(parts)
    near = jnp.where(flag, turn(strip, 85 + shift), 0.0)
    out[2] += jnp.where(lane == 85, near, 0.0)
    out[0] += jnp.where(lane == 86, near, 0.0)
    out[1] += jnp.where(jnp.logical_and(lane == 86, flag), turn(strip, 84 + shift), 0.0)
    return out


def neighbours(y, g, v):
    down = y[g][v + 1] if v < VR - 1 else pltpu.roll(y[g][0], 7, 0)
    up = y[g][v - 1] if v else pltpu.roll(y[g][VR - 1], 1, 0)
    east = y[g + 1][v] if g < GROUPS - 1 else turn(y[0][v], LANES - 1)
    west = y[g - 1][v] if g else turn(y[GROUPS - 1][v], 1)
    return east, west, down, up


def sweep_kernel(axes, steps, rows, *refs):
    prev, src = refs[0:2], refs[2:4]
    coef = [refs[4 + 2 * p : 6 + 2 * p] for p in range(COEFS)]
    base = 4 + 2 * COEFS
    from_w, from_e, from_n, from_s, from_nw, from_ne, from_sw, from_se = refs[base : base + 8]
    waves, co, xw, xe, yn, ys = refs[base + 8 : base + 14]
    corners = refs[base + 14 : base + 18]
    ext, cc, gbuf, carry, north_rows, south_rows = refs[base + 18 :]
    has_w, has_e, has_n, has_s = position(axes)
    lane, sub = lane_id(), sub_id()
    zero = jnp.zeros((8, LANES), F32)

    def keep(flag, value):
        return jnp.where(flag, value, 0.0)

    spreader = spread_matrix(2 * LANES)

    def put_own(plane, t, parts, k, slot):
        at = pl.ds(t * 8, 8)
        west, east = keep(has_w, from_w[k, at, :]), keep(has_e, from_e[k, at, :])
        for g, value in enumerate(add_halo(parts, west, east, 4 * LANES - 4 * slot)):
            ext[g, pl.ds(plane * ROWS_L + HALO + 8 * t, 8), :] = value

    def part_of(wide, first):
        return [wide[first : first + 8, g * LANES : (g + 1) * LANES] for g in range(GROUPS)]

    @pl.loop(0, steps // 4)
    def _(i):
        for k, arr in enumerate((prev, src)):
            at = pl.ds(pl.multiple_of(4 * i * rows, 8), 4 * rows)
            wide = moved(jnp.concatenate([arr[0][at, :], arr[1][at, :]], 1), spreader)
            for m in range(4):
                n = 4 * i + m
                for t in range(rows // 8):
                    put_own(k * steps + n, t, part_of(wide, m * rows + 8 * t), k, n)

    lows, highs = [], []
    for t in range(rows // 8):
        at = pl.ds(8 * t, 8)
        lows += masked_coefs([c[0] for c in coef], at, 0, axes, 8 * t)
        highs += masked_coefs([c[1] for c in coef], at, 1, axes, 8 * t)
    wide = jnp.concatenate([jnp.concatenate(lows, 0), jnp.concatenate(highs, 0)], 1)
    wide = moved(wide, spreader)
    for t in range(rows // 8):
        for p in range(COEFS):
            put_own(2 * steps + p, t, part_of(wide, 8 * (t * COEFS + p)), 2, p)
    for side, (strip, cw, ce, flag, first) in enumerate((
        (from_n, from_nw, from_ne, has_n, 0),
        (from_s, from_sw, from_se, has_s, rows + HALO),
    )):
        wide = moved(keep(flag, jnp.concatenate([strip[0], strip[1]], 1)), spreader)
        west = keep(jnp.logical_and(flag, has_w), cw[...])
        east = keep(jnp.logical_and(flag, has_e), ce[...])
        for q, j, at in strip_blocks(steps, 1 - side):
            shift = 4 * LANES - 4 * (HALO * q + j)
            for g, value in enumerate(add_halo(part_of(wide, at), west, east, shift)):
                ext[g, pl.ds(8 * q * ROWS_L + first + j, 8, stride=ROWS_L), :] = value
    for row in (0, rows + 2 * HALO - 1):
        for q in range(steps // 8, 2 * steps // 8):
            for g in range(3):
                ext[g, pl.ds(8 * q * ROWS_L + row, 8, stride=ROWS_L), :] = zero
    for row in range(rows + 2 * HALO, ROWS_L):
        for q in range(2 * steps // 8 + 1):
            for g in range(3):
                ext[g, pl.ds(8 * q * ROWS_L + row, 8, stride=ROWS_L), :] = zero

    def plane(index, v, g):
        return ext[g, pl.ds(index * ROWS_L + v, 8, stride=VR), :]

    first_coef = 2 * steps
    easts = [[plane(2 * steps + 3, v, g) for v in range(VR)] for g in range(3)]
    for g in range(3):
        col = lane * GROUPS + g
        col_in = jnp.logical_and(col >= 1, col <= 260)
        col_own = jnp.logical_and(col >= HALO, col <= 258)
        col_there = jnp.logical_and(
            jnp.logical_or(col >= HALO, has_w), jnp.logical_or(col <= 258, has_e)
        )
        n_cols = (
            1.0
            + jnp.where(jnp.logical_and(col <= 4, has_w), 1.0, 0.0)
            + jnp.where(jnp.logical_and(col >= 257, has_e), 1.0, 0.0)
        )
        souths = [plane(first_coef + 4, v, g) for v in range(VR)]
        for v in range(VR):
            row = sub * VR + v
            row_in = jnp.logical_and(row >= 1, row <= 68)
            row_own = jnp.logical_and(row >= HALO, row <= 66)
            row_there = jnp.logical_and(
                jnp.logical_or(row >= HALO, has_n), jnp.logical_or(row <= 66, has_s)
            )
            inner = jnp.logical_and(row_in, col_in)
            own = jnp.logical_and(row_own, col_own)
            there = jnp.logical_and(jnp.logical_and(row_there, col_there), inner)
            n_rows = (
                1.0
                + jnp.where(jnp.logical_and(row <= 4, has_n), 1.0, 0.0)
                + jnp.where(jnp.logical_and(row >= 65, has_s), 1.0, 0.0)
            )
            start, sto, leak, east, south, owner = [
                plane(first_coef + p, v, g) for p in range(COEFS)
            ]
            ea_w = easts[g - 1][v] if g else turn(easts[GROUPS - 1][v], 1)
            so_n = souths[v - 1] if v else pltpu.roll(souths[VR - 1], 1, 0)
            diag = sto + leak + east + ea_w + south + so_n
            safe = jnp.where(there, diag, 1.0)
            scale = jnp.where(there, 2.0 * SIGMA / safe, 0.0)
            cc[0, g, v] = scale * east
            cc[1, g, v] = scale * ea_w
            cc[2, g, v] = scale * south
            cc[3, g, v] = scale * so_n
            cc[4, g, v] = scale
            cc[5, g, v] = scale * sto
            cc[6, g, v] = jnp.where(inner, 0.0, 2.0 * SIGMA)
            weight = jnp.where(own, owner, jnp.where(there, 1.0, 0.0))
            cc[7, g, v] = weight * (1.0 / TAU[DEG])
            den = jnp.where(there, owner + n_rows * n_cols - 1.0, 1.0)
            at = slice(8 * v, 8 * v + 8)
            co[0, g, at, :] = weight
            co[1, g, at, :] = jnp.where(there, 1.0 / den, 0.0)
            co[2, g, at, :] = diag
            co[3, g, at, :] = east
            co[4, g, at, :] = ea_w
            co[5, g, at, :] = south
            co[6, g, at, :] = so_n
            co[7, g, at, :] = sto
            co[8, g, at, :] = start
            carry[g, v] = start

    xw[...] = jnp.zeros_like(xw)
    xe[...] = jnp.zeros_like(xe)
    group = lane // 4

    def stencil(y, g, v):
        east, west, down, up = neighbours(y, g, v)
        return (cc[0, g, v] * east + cc[1, g, v] * west) + (cc[2, g, v] * down + cc[3, g, v] * up)

    def advance(n, held):
        old = [[None] * VR for _ in range(3)]
        for g in range(3):
            for v in range(VR):
                old[g][v] = plane(n, v, g)
                gbuf[g, v] = (
                    cc[4, g, v] * plane(steps + n, v, g)
                    + cc[5, g, v] * held[g][v]
                    + cc[6, g, v] * old[g][v]
                )
        now = [
            [0.5 * (stencil(old, g, v) + gbuf[g, v]) for v in range(VR)] for g in range(3)
        ]
        for k in range(1, DEG):
            new = [
                [stencil(now, g, v) + (TAU[k] * gbuf[g, v] - old[g][v]) for v in range(VR)]
                for g in range(3)
            ]
            old, now = now, new
        return now

    def finish(n, now):
        for g in range(3):
            for v in range(VR):
                at = pl.ds(pl.multiple_of(n * ROWS_L + 8 * v, 8), 8)
                waves[g, at, :] = now[g][v] * (1.0 / TAU[DEG])
        weighted = [[cc[7, g, v] * now[g][v] for v in range(VR)] for g in range(3)]
        for v in range(VR):
            at = slice(8 * v, 8 * v + 8)
            parts = [weighted[g][v] for g in range(GROUPS)]
            xw[at, :] = jnp.where(group == n, west_edge(parts, 4 * n), xw[at, :])
            xe[at, :] = jnp.where(group == n, east_edge(parts, 4 * n), xe[at, :])
        for j in range(HALO):
            for g in range(3):
                north_rows[g, pl.ds(j * steps + n, 1), :] = weighted[g][1 + j][0:1]
                south_rows[g, pl.ds(j * steps + n, 1), :] = weighted[g][3 + j][7:8]
        return [[now[g][v] * (1.0 / TAU[DEG]) for v in range(VR)] for g in range(3)]

    @pl.loop(0, steps)
    def _(n):
        held = [[carry[g, v] for v in range(VR)] for g in range(3)]
        held = finish(n, advance(n, held))
        for g in range(GROUPS):
            for v in range(VR):
                carry[g, v] = held[g][v]

    for side, (rows_of, out) in enumerate(((north_rows, yn), (south_rows, ys))):
        west, east = zero, zero
        for i in range(HALO * steps // 8):
            at = slice(8 * i, 8 * i + 8)
            parts = [rows_of[g, at, :] for g in range(GROUPS)]
            west = jnp.where(group == i, west_edge(parts, 4 * i), west)
            east = jnp.where(group == i, east_edge(parts, 4 * i), east)
        out[...] = rows_of[...]
        corners[2 * side][...] = west
        corners[2 * side + 1][...] = east


def chebyshev_scales():
    tau = [1.0, SIGMA]
    for _ in range(DEG):
        tau.append(2.0 * SIGMA * tau[-1] - tau[-2])
    return tau


TAU = chebyshev_scales()


def one_hot_of(row, count, first):
    ids = jnp.broadcast_to(row - first, (count, row.shape[1]))
    return jnp.where(
        ids == lax.broadcasted_iota(jnp.int32, ids.shape, 0), 1.0, 0.0
    ).astype(BF16)


def settle_kernel(axes, steps, rows, aggs, *refs):
    waves, co, from_w, from_e, from_n, from_s, from_nw, from_ne, from_sw, from_se = refs[:10]
    src = refs[10:12]
    agg = refs[12]
    settled, coarse = refs[13:15]
    before, both, rest, north, south = refs[15:]
    has_w, has_e, has_n, has_s = position(axes)
    lane, sub = lane_id(), sub_id()
    tile = lax.axis_index("gx") * axes[1] + lax.axis_index("gy")

    for g in range(3):
        for v in range(VR):
            before[g, v] = co[8, g, 8 * v : 8 * v + 8, :]


    def spread(row):
        return jnp.broadcast_to(row, (8, LANES))

    for strip, cw, ce, flag, out in (
        (from_n, from_nw, from_ne, has_n, north),
        (from_s, from_sw, from_se, has_s, south),
    ):
        for i in range(HALO * steps // 8):
            at = slice(8 * i, 8 * i + 8)
            parts = [strip[g, at, :] for g in range(GROUPS)]
            parts = add_west(parts, cw[...], -4 * i, has_w)
            parts = add_east(parts, ce[...], -4 * i, has_e)
            for g, value in enumerate(parts):
                out[g, at, :] = jnp.where(flag, value, 0.0)

    @pl.loop(0, steps)
    def _(n):
        now = [[None] * VR for _ in range(3)]
        for v in range(VR):
            at = slice(8 * v, 8 * v + 8)
            here = pl.ds(pl.multiple_of(n * ROWS_L + 8 * v, 8), 8)
            parts = [co[0, g, at, :] * waves[g, here, :] for g in range(GROUPS)]
            shift = 4 * LANES - 4 * n
            parts = add_west(parts, from_w[at, :], shift, has_w)
            parts = add_east(parts, from_e[at, :], shift, has_e)
            for g, total in enumerate(parts):
                if 2 <= v <= 4:
                    one = pl.ds((v - 2) * steps + n, 1)
                    total += jnp.where(sub == 0, spread(north[g, one, :]), 0.0)
                    total += jnp.where(sub == 7, spread(south[g, one, :]), 0.0)
                now[g][v] = total * co[1, g, at, :]
        out = [[None] * VR for _ in range(3)]
        for g in range(3):
            for v in range(VR):
                at = slice(8 * v, 8 * v + 8)
                cur = now[g][v]
                east, west, down, up = neighbours(now, g, v)
                image = (
                    co[2, g, at, :] * cur
                    - co[3, g, at, :] * east
                    - co[4, g, at, :] * west
                    - co[5, g, at, :] * down
                    - co[6, g, at, :] * up
                )
                out[g][v] = co[7, g, at, :] * before[g, v] - image
                before[g, v] = cur
        for v in range(VR):
            at = pl.ds(n * ROWS_L + v, 8, stride=VR)
            for g in range(GROUPS):
                both[g, 0, at, :] = now[g][v]
                both[g, 1, at, :] = out[g][v]

    spreader = spread_matrix(2 * LANES)

    @pl.loop(0, steps // 2)
    def _(i):
        pieces = [
            jnp.concatenate(
                [both[g, k, pl.ds((2 * i + m) * ROWS_L + HALO, rows), :] for g in range(GROUPS)], 1
            )
            for k in range(2)
            for m in range(2)
        ]
        plain = moved(jnp.concatenate(pieces, 0), spreader, transposed=True)
        at = pl.ds(pl.multiple_of(2 * i * rows, 8), 2 * rows)
        for h in range(2):
            lanes = slice(h * LANES, (h + 1) * LANES)
            settled[h, at, :] = plain[: 2 * rows, lanes]
            rest[h, at, :] = plain[2 * rows :, lanes] + src[h][at, :]

    def add_row(row, total):
        at = pl.ds(row, steps, stride=rows)
        values = jnp.concatenate([rest[0, at, :], rest[1, at, :]], 1)
        hot = one_hot_of(agg[pl.ds(row, 1), :], aggs, tile * aggs)
        return total + lax.dot_general(
            two_terms(values), hot, (((1,), (1,)), ((), ())), preferred_element_type=F32
        )

    def add_rows(i, total):
        for k in range(4):
            total = add_row(4 * i + k, total)
        return total

    total = lax.fori_loop(0, rows // 4, add_rows, jnp.zeros((2 * steps, aggs), F32))
    total = total[:steps] + total[steps:]
    coarse[...] = jnp.concatenate([total[: steps // 2], total[steps // 2 :]], 1)


def gather_kernel(axes, own, everyone, send, recv, local):
    n_x, n_y = axes
    count = n_x * n_y
    me = lax.axis_index("gx") * n_y + lax.axis_index("gy")

    def other(i):
        which = lax.rem(me + i, count)
        return which // n_y, lax.rem(which, n_y)

    barrier = pltpu.get_barrier_semaphore()

    @pl.loop(1, count)
    def _(i):
        pl.semaphore_signal(barrier, inc=1, device_id=other(i), device_id_type=MESH)

    pl.semaphore_wait(barrier, count - 1)
    mine = pltpu.make_async_copy(own, everyone.at[me], local)
    mine.start()

    def copy(i):
        return pltpu.make_async_remote_copy(
            src_ref=own, dst_ref=everyone.at[me], send_sem=send.at[i], recv_sem=recv.at[i],
            device_id=other(i), device_id_type=MESH,
        )

    @pl.loop(1, count)
    def _(i):
        copy(i).start()

    @pl.loop(1, count)
    def _(i):
        source = lax.rem(me + count - i, count)
        pltpu.make_async_remote_copy(
            src_ref=own, dst_ref=everyone.at[source], send_sem=send.at[i], recv_sem=recv.at[i],
            device_id=other(i), device_id_type=MESH,
        ).wait()

    mine.wait()


def gather(axes, ident, own):
    count = axes[0] * axes[1]
    return pl.pallas_call(
        functools.partial(gather_kernel, axes),
        out_shape=jax.ShapeDtypeStruct((count,) + own.shape, F32),
        in_specs=[pl.BlockSpec(memory_space=pl.ANY)],
        out_specs=pl.BlockSpec(memory_space=pl.ANY),
        scratch_shapes=[
            pltpu.SemaphoreType.DMA((count,)),
            pltpu.SemaphoreType.DMA((count,)),
            pltpu.SemaphoreType.DMA,
        ],
        compiler_params=pltpu.CompilerParams(collective_id=ident, has_side_effects=True),
        name="coarse_gather",
    )(own)


def correct_kernel(axes, steps, rows, aggs, everyone, inverse, agg, settled, out, fixed):
    tile = lax.axis_index("gx") * axes[1] + lax.axis_index("gy")
    count = axes[0] * axes[1]

    @pl.when(pl.program_id(0) == 0)
    def _():
        low_lanes = lax.broadcasted_iota(jnp.int32, (steps // 2, LANES), 1) < aggs
        total = jnp.zeros((steps, aggs), F32)
        for d in range(0, count, 2):
            a, b = everyone[d], everyone[d + 1]
            upper = jnp.where(low_lanes, a, pltpu.roll(b, aggs, 1))
            lower = jnp.where(low_lanes, pltpu.roll(a, aggs, 1), b)
            total += lax.dot_general(
                jnp.concatenate([upper, lower], 0),
                inverse[:, d * aggs : (d + 2) * aggs],
                (((1,), (1,)), ((), ())),
                precision=lax.Precision.HIGHEST,
                preferred_element_type=F32,
            )
        high = total.astype(BF16)
        low = (total - high.astype(F32)).astype(BF16)
        fixed[...] = jnp.concatenate([high, low], 1)

    factor = fixed[...]

    @pl.loop(0, rows // 4)
    def _(i):
        for k in range(4):
            row = 4 * i + k
            hot = one_hot_of(agg[pl.ds(row, 1), :], aggs, tile * aggs)
            grown = jnp.dot(
                factor, jnp.concatenate([hot, hot], 0), preferred_element_type=F32
            )
            out[pl.ds(row, steps, stride=rows), :] = (
                settled[0, pl.ds(row, steps, stride=rows), :] + grown
            )


def halves(shape):
    block = (shape[0], LANES)
    return [pl.BlockSpec(block, lambda i: (0, 0)), pl.BlockSpec(block, lambda i: (0, 1))]


def whole(shape):
    return pl.BlockSpec(shape, lambda i: (0,) * len(shape))


def shards(axes, prev_wave, source, start_state, storage, leakage, cond_east, cond_south,
           owner_weight, aggregate, coarse_inverse):
    steps, rows, cols = prev_wave.shape
    aggs = coarse_inverse.shape[0]
    planes = 2 * steps + 8
    strip_rows = HALO * planes - steps
    rim_rows = HALO * steps
    flat = (steps * rows, cols)
    prev, src = prev_wave.reshape(flat), source.reshape(flat)
    coef = (start_state, storage, leakage, cond_east, cond_south, owner_weight)
    params = pltpu.CompilerParams(vmem_limit_bytes=VMEM_LIMIT)
    fields, field_specs = [], []
    for arr in (prev, src) + coef:
        fields += [arr, arr]
        field_specs += halves(arr.shape)

    def local(kernel, name, args, in_specs, outs, scratch):
        return pl.pallas_call(
            kernel,
            grid=(1,),
            out_shape=[jax.ShapeDtypeStruct(s, F32) for s in outs],
            in_specs=in_specs,
            out_specs=[whole(s) for s in outs],
            scratch_shapes=scratch,
            compiler_params=params,
            name=name,
        )(*args)

    strips = local(
        functools.partial(pack_kernel, axes, steps, rows), "halo_pack", fields, field_specs,
        [(3, rows, LANES)] * 2 + [(2, strip_rows, LANES)] * 2 + [(8, LANES)] * 4, [],
    )
    halo = exchange(axes, 0, *strips)
    waves, co, *rims = local(
        functools.partial(sweep_kernel, axes, steps, rows), "local_sweep",
        fields + list(halo), field_specs + [whole(h.shape) for h in halo],
        [(3, steps * ROWS_L, LANES), (9, 3, ROWS_L, LANES)]
        + [(ROWS_L, LANES)] * 2 + [(3, rim_rows, LANES)] * 2 + [(8, LANES)] * 4,
        [
            pltpu.VMEM((3, planes * ROWS_L, LANES), F32),
            pltpu.VMEM((8, 3, VR, 8, LANES), F32),
            pltpu.VMEM((3, VR, 8, LANES), F32),
            pltpu.VMEM((3, VR, 8, LANES), F32),
            pltpu.VMEM((3, rim_rows, LANES), F32),
            pltpu.VMEM((3, rim_rows, LANES), F32),
        ],
    )
    rim = exchange(axes, 1, *rims)
    args = [waves, co, *rim]
    settled, coarse = local(
        functools.partial(settle_kernel, axes, steps, rows, aggs), "settle_and_restrict",
        args + [src, src, aggregate],
        [whole(a.shape) for a in args] + halves(flat) + [whole(aggregate.shape)],
        [(2, steps * rows, LANES), (steps // 2, 2 * aggs)],
        [
            pltpu.VMEM((3, VR, 8, LANES), F32),
            pltpu.VMEM((3, 2, steps * ROWS_L, LANES), F32),
            pltpu.VMEM((2, steps * rows, LANES), F32),
            pltpu.VMEM((3, rim_rows, LANES), F32),
            pltpu.VMEM((3, rim_rows, LANES), F32),
        ],
    )
    everyone = gather(axes, 2, coarse)
    out = pl.pallas_call(
        functools.partial(correct_kernel, axes, steps, rows, aggs),
        grid=(2,),
        out_shape=jax.ShapeDtypeStruct(flat, F32),
        in_specs=[
            whole(everyone.shape),
            whole(coarse_inverse.shape),
            pl.BlockSpec((rows, LANES), lambda i: (0, i)),
            pl.BlockSpec((1, steps * rows, LANES), lambda i: (i, 0, 0)),
        ],
        out_specs=pl.BlockSpec((steps * rows, LANES), lambda i: (0, i)),
        scratch_shapes=[pltpu.VMEM((steps, 2 * aggs), BF16)],
        compiler_params=params,
        name="correct",
    )(everyone, coarse_inverse, aggregate, settled)
    return out.reshape(prev_wave.shape)


def solution(mesh):
    axes = (mesh.shape["gx"], mesh.shape["gy"])
    plane = P("gy", "gx")
    wave = P(None, "gy", "gx")
    return jax.shard_map(
        functools.partial(shards, axes),
        mesh=mesh,
        in_specs=(wave, wave) + (plane,) * 7 + (P(("gx", "gy"), None),),
        out_specs=wave,
        check_vma=False,
    )
```

```python
import functools

import jax
import jax.numpy as jnp
from jax import lax
from jax.experimental import pallas as pl
from jax.experimental.pallas import tpu as pltpu
from jax.sharding import PartitionSpec as P

DEG = 8
OV = 2
HALO = OV + 1
LANES = 128
VR = 9
ROWS_L = 8 * VR
COEFS = 6
DELTA = 0.95
SIGMA = 1.0 / DELTA
GROUPS = 3
F32 = jnp.float32
BF16 = jnp.bfloat16
MESH = pl.DeviceIdType.MESH
VMEM_LIMIT = 56 * 1024 * 1024


def lane_id():
    return lax.broadcasted_iota(jnp.int32, (8, LANES), 1)


def sub_id():
    return lax.broadcasted_iota(jnp.int32, (8, LANES), 0)


def turn(x, by):
    by = by % LANES
    return pltpu.roll(x, by, 1) if not (isinstance(by, int) and by == 0) else x


def position(axes):
    gx, gy = lax.axis_index("gx"), lax.axis_index("gy")
    return gx > 0, gx < axes[0] - 1, gy > 0, gy < axes[1] - 1


def masked_coefs(refs, rows, half, axes, first_row):
    _, has_e, _, has_s = position(axes)
    start, sto, leak, east, south, owner = [ref[rows, :] for ref in refs]
    if half == 1:
        cut = jnp.logical_and(lane_id() == LANES - 1, jnp.logical_not(has_e))
        east = jnp.where(cut, 0.0, east)
    cut = jnp.logical_and(sub_id() + first_row == 63, jnp.logical_not(has_s))
    south = jnp.where(cut, 0.0, south)
    return start, sto, leak, east, south, owner.astype(F32)


def pack_kernel(axes, steps, rows, *refs):
    prev, src = refs[0:2], refs[2:4]
    coef = [refs[4 + 2 * p : 6 + 2 * p] for p in range(COEFS)]
    xw, xe, yn, ys, *corners = refs[4 + 2 * COEFS :]
    group = lane_id() // 4

    @pl.loop(0, rows // 8)
    def _(t):
        first = pl.multiple_of(t * 8, 8)
        for k, arr in enumerate((prev, src)):
            low = jnp.zeros((8, LANES), F32)
            high = jnp.zeros((8, LANES), F32)
            for n in range(steps):
                at = pl.ds(pl.multiple_of(n * rows + first, 8), 8)
                low = jnp.where(group == n, turn(arr[0][at, :], 4 * n), low)
                high = jnp.where(group == n, turn(arr[1][at, :], 4 * n - 125), high)
            xw[k, pl.ds(first, 8), :] = low
            xe[k, pl.ds(first, 8), :] = high
        at = pl.ds(first, 8)
        low = jnp.zeros((8, LANES), F32)
        high = jnp.zeros((8, LANES), F32)
        planes0 = masked_coefs([c[0] for c in coef], at, 0, axes, first)
        planes1 = masked_coefs([c[1] for c in coef], at, 1, axes, first)
        for p in range(COEFS):
            low = jnp.where(group == p, turn(planes0[p], 4 * p), low)
            high = jnp.where(group == p, turn(planes1[p], 4 * p - 125), high)
        xw[2, at, :] = low
        xe[2, at, :] = high

    for side, (out, first, base) in enumerate(((yn, 0, 0), (ys, rows - HALO, rows - 8))):
        for h in range(2):
            planes = masked_coefs([c[h] for c in coef], pl.ds(base, 8), h, axes, base)
            corner = jnp.zeros((8, LANES), F32)
            for q, j, at in strip_blocks(steps, side):
                if q < 2 * steps // 8:
                    arr, part = (prev, q) if q < steps // 8 else (src, q - steps // 8)
                    value = arr[h][pl.ds(8 * part * rows + first + j, 8, stride=rows), :]
                else:
                    row = first + j - base
                    pieces = [p[row : row + 1] for p in planes]
                    value = jnp.concatenate(pieces + [jnp.zeros((8 - COEFS, LANES), F32)], 0)
                out[h, at : at + 8, :] = value
                slot = 4 * (HALO * q + j)
                corner = jnp.where(group == slot // 4, turn(value, slot - (0, 125)[h]), corner)
            corners[2 * side + h][...] = corner


def strip_blocks(steps, side):
    at, blocks = 0, []
    for q in range(2 * steps // 8 + 1):
        for j in range(HALO):
            if steps // 8 <= q < 2 * steps // 8 and j == (HALO - 1, 0)[side]:
                continue
            blocks.append((q, j, at))
            at += 8
    return blocks


def exchange_kernel(axes, xw, xe, yn, ys, c_nw, c_ne, c_sw, c_se, *refs):
    outs = refs[:8]
    send, recv = refs[8:]
    gx, gy = lax.axis_index("gx"), lax.axis_index("gy")
    has_w, has_e, has_n, has_s = position(axes)
    west, east, north, south = gx - 1, gx + 1, gy - 1, gy + 1
    both = jnp.logical_and
    has_nw, has_ne = both(has_n, has_w), both(has_n, has_e)
    has_sw, has_se = both(has_s, has_w), both(has_s, has_e)
    from_w, from_e, from_n, from_s, from_nw, from_ne, from_sw, from_se = outs
    plan = (
        (yn, from_s, (gx, north), has_n, has_s),
        (ys, from_n, (gx, south), has_s, has_n),
        (xw, from_e, (west, gy), has_w, has_e),
        (xe, from_w, (east, gy), has_e, has_w),
        (c_nw, from_se, (west, north), has_nw, has_se),
        (c_ne, from_sw, (east, north), has_ne, has_sw),
        (c_sw, from_ne, (west, south), has_sw, has_ne),
        (c_se, from_nw, (east, south), has_se, has_nw),
    )
    barrier = pltpu.get_barrier_semaphore()
    copies = []
    for i, (src, dst, to, goes, comes) in enumerate(plan):

        @pl.when(goes)
        def _():
            pl.semaphore_signal(barrier, inc=1, device_id=to, device_id_type=MESH)

        copy = pltpu.make_async_remote_copy(
            src_ref=src, dst_ref=dst, send_sem=send.at[i], recv_sem=recv.at[i],
            device_id=to, device_id_type=MESH,
        )
        copies.append((copy, goes, comes))
    pl.semaphore_wait(barrier, sum(jnp.where(step[3], 1, 0) for step in plan))
    for copy, goes, _ in copies:
        pl.when(goes)(copy.start)
    for copy, goes, comes in copies:
        pl.when(goes)(copy.wait_send)
        pl.when(comes)(copy.wait_recv)


def exchange(axes, ident, *strips):
    return pl.pallas_call(
        functools.partial(exchange_kernel, axes),
        out_shape=[jax.ShapeDtypeStruct(s.shape, F32) for s in strips],
        in_specs=[pl.BlockSpec(memory_space=pl.ANY)] * 8,
        out_specs=[pl.BlockSpec(memory_space=pl.ANY)] * 8,
        scratch_shapes=[pltpu.SemaphoreType.DMA((8,)), pltpu.SemaphoreType.DMA((8,))],
        compiler_params=pltpu.CompilerParams(collective_id=ident, has_side_effects=True),
        name="neighbour_exchange",
    )(*strips)


def spread_matrix(cols):
    shape = (cols, GROUPS * LANES)
    at = lax.broadcasted_iota(jnp.int32, shape, 1)
    col = (at % LANES) * GROUPS + at // LANES - HALO
    return jnp.where(col == lax.broadcasted_iota(jnp.int32, shape, 0), 1.0, 0.0).astype(BF16)


def two_terms(values):
    high = values.astype(BF16)
    return jnp.concatenate([high, (values - high.astype(F32)).astype(BF16)], 0)


def moved(values, matrix, transposed=False):
    dims = (((1,), (1 if transposed else 0,)), ((), ()))
    both = lax.dot_general(two_terms(values), matrix, dims, preferred_element_type=F32)
    return both[: values.shape[0]] + both[values.shape[0] :]


def add_halo(parts, west, east, shift):
    lane = lane_id()
    at_86 = lane == 86
    far = turn(east, 85 + shift)
    return (
        jnp.where(lane == 0, turn(west, shift), jnp.where(lane == 87, far, parts[0])),
        jnp.where(lane == 0, turn(west, shift - 1), jnp.where(at_86, turn(east, 86 + shift), parts[1])),
        jnp.where(lane == 0, turn(west, shift - 2), jnp.where(at_86, far, parts[2])),
    )


def west_edge(parts, to):
    lane = lane_id()
    pair = turn(jnp.where(lane == 0, parts[2], parts[0]), to + 1)
    return jnp.where(lane == to, turn(parts[1], to), pair)


def east_edge(parts, to):
    lane = lane_id()
    last = jnp.where(lane == to + 1, turn(parts[1], to - 85 + LANES), turn(parts[2], to - 84 + LANES))
    return jnp.where(lane == to, turn(parts[0], to - 86 + LANES), last)


def add_west(parts, strip, shift, flag):
    lane, out = lane_id(), list(parts)
    near = jnp.where(flag, turn(strip, shift), 0.0)
    out[2] += jnp.where(lane == 0, near, 0.0)
    out[0] += jnp.where(lane == 1, near, 0.0)
    out[1] += jnp.where(jnp.logical_and(lane == 1, flag), turn(strip, shift - 1), 0.0)
    return out


def add_east(parts, strip, shift, flag):
    lane, out = lane_id(), list(parts)
    near = jnp.where(flag, turn(strip, 85 + shift), 0.0)
    out[2] += jnp.where(lane == 85, near, 0.0)
    out[0] += jnp.where(lane == 86, near, 0.0)
    out[1] += jnp.where(jnp.logical_and(lane == 86, flag), turn(strip, 84 + shift), 0.0)
    return out


def neighbours(y, g, v):
    down = y[g][v + 1] if v < VR - 1 else pltpu.roll(y[g][0], 7, 0)
    up = y[g][v - 1] if v else pltpu.roll(y[g][VR - 1], 1, 0)
    east = y[g + 1][v] if g < GROUPS - 1 else turn(y[0][v], LANES - 1)
    west = y[g - 1][v] if g else turn(y[GROUPS - 1][v], 1)
    return east, west, down, up


def sweep_kernel(axes, steps, rows, *refs):
    prev, src = refs[0:2], refs[2:4]
    coef = [refs[4 + 2 * p : 6 + 2 * p] for p in range(COEFS)]
    base = 4 + 2 * COEFS
    from_w, from_e, from_n, from_s, from_nw, from_ne, from_sw, from_se = refs[base : base + 8]
    waves, co, xw, xe, yn, ys = refs[base + 8 : base + 14]
    corners = refs[base + 14 : base + 18]
    ext, cc, gbuf, carry, north_rows, south_rows = refs[base + 18 :]
    has_w, has_e, has_n, has_s = position(axes)
    lane, sub = lane_id(), sub_id()
    zero = jnp.zeros((8, LANES), F32)

    def keep(flag, value):
        return jnp.where(flag, value, 0.0)

    spreader = spread_matrix(2 * LANES)

    def put_own(plane, t, parts, k, slot):
        at = pl.ds(t * 8, 8)
        west, east = keep(has_w, from_w[k, at, :]), keep(has_e, from_e[k, at, :])
        for g, value in enumerate(add_halo(parts, west, east, 4 * LANES - 4 * slot)):
            ext[g, pl.ds(plane * ROWS_L + HALO + 8 * t, 8), :] = value

    def part_of(wide, first):
        return [wide[first : first + 8, g * LANES : (g + 1) * LANES] for g in range(GROUPS)]

    @pl.loop(0, steps // 4)
    def _(i):
        for k, arr in enumerate((prev, src)):
            at = pl.ds(pl.multiple_of(4 * i * rows, 8), 4 * rows)
            wide = moved(jnp.concatenate([arr[0][at, :], arr[1][at, :]], 1), spreader)
            for m in range(4):
                n = 4 * i + m
                for t in range(rows // 8):
                    put_own(k * steps + n, t, part_of(wide, m * rows + 8 * t), k, n)

    lows, highs = [], []
    for t in range(rows // 8):
        at = pl.ds(8 * t, 8)
        lows += masked_coefs([c[0] for c in coef], at, 0, axes, 8 * t)
        highs += masked_coefs([c[1] for c in coef], at, 1, axes, 8 * t)
    wide = jnp.concatenate([jnp.concatenate(lows, 0), jnp.concatenate(highs, 0)], 1)
    wide = moved(wide, spreader)
    for t in range(rows // 8):
        for p in range(COEFS):
            put_own(2 * steps + p, t, part_of(wide, 8 * (t * COEFS + p)), 2, p)
    for side, (strip, cw, ce, flag, first) in enumerate((
        (from_n, from_nw, from_ne, has_n, 0),
        (from_s, from_sw, from_se, has_s, rows + HALO),
    )):
        wide = moved(keep(flag, jnp.concatenate([strip[0], strip[1]], 1)), spreader)
        west = keep(jnp.logical_and(flag, has_w), cw[...])
        east = keep(jnp.logical_and(flag, has_e), ce[...])
        for q, j, at in strip_blocks(steps, 1 - side):
            shift = 4 * LANES - 4 * (HALO * q + j)
            for g, value in enumerate(add_halo(part_of(wide, at), west, east, shift)):
                ext[g, pl.ds(8 * q * ROWS_L + first + j, 8, stride=ROWS_L), :] = value
    for row in (0, rows + 2 * HALO - 1):
        for q in range(steps // 8, 2 * steps // 8):
            for g in range(3):
                ext[g, pl.ds(8 * q * ROWS_L + row, 8, stride=ROWS_L), :] = zero
    for row in range(rows + 2 * HALO, ROWS_L):
        for q in range(2 * steps // 8 + 1):
            for g in range(3):
                ext[g, pl.ds(8 * q * ROWS_L + row, 8, stride=ROWS_L), :] = zero

    def plane(index, v, g):
        return ext[g, pl.ds(index * ROWS_L + v, 8, stride=VR), :]

    first_coef = 2 * steps
    easts = [[plane(2 * steps + 3, v, g) for v in range(VR)] for g in range(3)]
    for g in range(3):
        col = lane * GROUPS + g
        col_in = jnp.logical_and(col >= 1, col <= 260)
        col_own = jnp.logical_and(col >= HALO, col <= 258)
        col_there = jnp.logical_and(
            jnp.logical_or(col >= HALO, has_w), jnp.logical_or(col <= 258, has_e)
        )
        n_cols = (
            1.0
            + jnp.where(jnp.logical_and(col <= 4, has_w), 1.0, 0.0)
            + jnp.where(jnp.logical_and(col >= 257, has_e), 1.0, 0.0)
        )
        souths = [plane(first_coef + 4, v, g) for v in range(VR)]
        for v in range(VR):
            row = sub * VR + v
            row_in = jnp.logical_and(row >= 1, row <= 68)
            row_own = jnp.logical_and(row >= HALO, row <= 66)
            row_there = jnp.logical_and(
                jnp.logical_or(row >= HALO, has_n), jnp.logical_or(row <= 66, has_s)
            )
            inner = jnp.logical_and(row_in, col_in)
            own = jnp.logical_and(row_own, col_own)
            there = jnp.logical_and(jnp.logical_and(row_there, col_there), inner)
            n_rows = (
                1.0
                + jnp.where(jnp.logical_and(row <= 4, has_n), 1.0, 0.0)
                + jnp.where(jnp.logical_and(row >= 65, has_s), 1.0, 0.0)
            )
            start, sto, leak, east, south, owner = [
                plane(first_coef + p, v, g) for p in range(COEFS)
            ]
            ea_w = easts[g - 1][v] if g else turn(easts[GROUPS - 1][v], 1)
            so_n = souths[v - 1] if v else pltpu.roll(souths[VR - 1], 1, 0)
            diag = sto + leak + east + ea_w + south + so_n
            safe = jnp.where(there, diag, 1.0)
            scale = jnp.where(there, 2.0 * SIGMA / safe, 0.0)
            cc[0, g, v] = scale * east
            cc[1, g, v] = scale * ea_w
            cc[2, g, v] = scale * south
            cc[3, g, v] = scale * so_n
            cc[4, g, v] = scale
            cc[5, g, v] = scale * sto
            cc[6, g, v] = jnp.where(inner, 0.0, 2.0 * SIGMA)
            weight = jnp.where(own, owner, jnp.where(there, 1.0, 0.0))
            cc[7, g, v] = weight * (1.0 / TAU[DEG])
            den = jnp.where(there, owner + n_rows * n_cols - 1.0, 1.0)
            at = slice(8 * v, 8 * v + 8)
            co[0, g, at, :] = weight
            co[1, g, at, :] = jnp.where(there, 1.0 / den, 0.0)
            co[2, g, at, :] = diag
            co[3, g, at, :] = east
            co[4, g, at, :] = ea_w
            co[5, g, at, :] = south
            co[6, g, at, :] = so_n
            co[7, g, at, :] = sto
            co[8, g, at, :] = start
            carry[g, v] = start

    xw[...] = jnp.zeros_like(xw)
    xe[...] = jnp.zeros_like(xe)
    group = lane // 4

    def stencil(y, g, v):
        east, west, down, up = neighbours(y, g, v)
        return (cc[0, g, v] * east + cc[1, g, v] * west) + (cc[2, g, v] * down + cc[3, g, v] * up)

    def advance(n, held):
        def each(value):
            out = [[None] * VR for _ in range(GROUPS)]
            for v in range(VR):
                for g in range(GROUPS):
                    out[g][v] = value(g, v)
            return out

        old = each(lambda g, v: plane(n, v, g))
        for v in range(VR):
            for g in range(GROUPS):
                gbuf[g, v] = (
                    cc[4, g, v] * plane(steps + n, v, g)
                    + cc[5, g, v] * held[g][v]
                    + cc[6, g, v] * old[g][v]
                )
        now = each(lambda g, v: 0.5 * (stencil(old, g, v) + gbuf[g, v]))
        for k in range(1, DEG):
            new = each(lambda g, v: stencil(now, g, v) + (TAU[k] * gbuf[g, v] - old[g][v]))
            old, now = now, new
        return now

    def finish(n, now):
        for g in range(3):
            for v in range(VR):
                at = pl.ds(pl.multiple_of(n * ROWS_L + 8 * v, 8), 8)
                waves[g, at, :] = now[g][v] * (1.0 / TAU[DEG])
        weighted = [[cc[7, g, v] * now[g][v] for v in range(VR)] for g in range(3)]
        for v in range(VR):
            at = slice(8 * v, 8 * v + 8)
            parts = [weighted[g][v] for g in range(GROUPS)]
            xw[at, :] = jnp.where(group == n, west_edge(parts, 4 * n), xw[at, :])
            xe[at, :] = jnp.where(group == n, east_edge(parts, 4 * n), xe[at, :])
        for j in range(HALO):
            for g in range(3):
                north_rows[g, pl.ds(j * steps + n, 1), :] = weighted[g][1 + j][0:1]
                south_rows[g, pl.ds(j * steps + n, 1), :] = weighted[g][3 + j][7:8]
        return [[now[g][v] * (1.0 / TAU[DEG]) for v in range(VR)] for g in range(3)]

    @pl.loop(0, steps)
    def _(n):
        held = [[carry[g, v] for v in range(VR)] for g in range(3)]
        held = finish(n, advance(n, held))
        for g in range(GROUPS):
            for v in range(VR):
                carry[g, v] = held[g][v]

    for side, (rows_of, out) in enumerate(((north_rows, yn), (south_rows, ys))):
        west, east = zero, zero
        for i in range(HALO * steps // 8):
            at = slice(8 * i, 8 * i + 8)
            parts = [rows_of[g, at, :] for g in range(GROUPS)]
            west = jnp.where(group == i, west_edge(parts, 4 * i), west)
            east = jnp.where(group == i, east_edge(parts, 4 * i), east)
        out[...] = rows_of[...]
        corners[2 * side][...] = west
        corners[2 * side + 1][...] = east


def chebyshev_scales():
    tau = [1.0, SIGMA]
    for _ in range(DEG):
        tau.append(2.0 * SIGMA * tau[-1] - tau[-2])
    return tau


TAU = chebyshev_scales()


def one_hot_of(row, count, first):
    ids = jnp.broadcast_to(row - first, (count, row.shape[1]))
    return jnp.where(
        ids == lax.broadcasted_iota(jnp.int32, ids.shape, 0), 1.0, 0.0
    ).astype(BF16)


def settle_kernel(axes, steps, rows, aggs, *refs):
    waves, co, from_w, from_e, from_n, from_s, from_nw, from_ne, from_sw, from_se = refs[:10]
    src = refs[10:12]
    agg = refs[12]
    settled, coarse = refs[13:15]
    before, both, rest, north, south = refs[15:]
    has_w, has_e, has_n, has_s = position(axes)
    lane, sub = lane_id(), sub_id()
    tile = lax.axis_index("gx") * axes[1] + lax.axis_index("gy")

    for g in range(3):
        for v in range(VR):
            before[g, v] = co[8, g, 8 * v : 8 * v + 8, :]


    def spread(row):
        return jnp.broadcast_to(row, (8, LANES))

    for strip, cw, ce, flag, out in (
        (from_n, from_nw, from_ne, has_n, north),
        (from_s, from_sw, from_se, has_s, south),
    ):
        for i in range(HALO * steps // 8):
            at = slice(8 * i, 8 * i + 8)
            parts = [strip[g, at, :] for g in range(GROUPS)]
            parts = add_west(parts, cw[...], -4 * i, has_w)
            parts = add_east(parts, ce[...], -4 * i, has_e)
            for g, value in enumerate(parts):
                out[g, at, :] = jnp.where(flag, value, 0.0)

    @pl.loop(0, steps)
    def _(n):
        now = [[None] * VR for _ in range(3)]
        for v in range(VR):
            at = slice(8 * v, 8 * v + 8)
            here = pl.ds(pl.multiple_of(n * ROWS_L + 8 * v, 8), 8)
            parts = [co[0, g, at, :] * waves[g, here, :] for g in range(GROUPS)]
            shift = 4 * LANES - 4 * n
            parts = add_west(parts, from_w[at, :], shift, has_w)
            parts = add_east(parts, from_e[at, :], shift, has_e)
            for g, total in enumerate(parts):
                if 2 <= v <= 4:
                    one = pl.ds((v - 2) * steps + n, 1)
                    total += jnp.where(sub == 0, spread(north[g, one, :]), 0.0)
                    total += jnp.where(sub == 7, spread(south[g, one, :]), 0.0)
                now[g][v] = total * co[1, g, at, :]
        out = [[None] * VR for _ in range(3)]
        for g in range(3):
            for v in range(VR):
                at = slice(8 * v, 8 * v + 8)
                cur = now[g][v]
                east, west, down, up = neighbours(now, g, v)
                image = (
                    co[2, g, at, :] * cur
                    - co[3, g, at, :] * east
                    - co[4, g, at, :] * west
                    - co[5, g, at, :] * down
                    - co[6, g, at, :] * up
                )
                out[g][v] = co[7, g, at, :] * before[g, v] - image
                before[g, v] = cur
        for v in range(VR):
            at = pl.ds(n * ROWS_L + v, 8, stride=VR)
            for g in range(GROUPS):
                both[g, 0, at, :] = now[g][v]
                both[g, 1, at, :] = out[g][v]

    spreader = spread_matrix(2 * LANES)

    @pl.loop(0, steps // 2)
    def _(i):
        pieces = [
            jnp.concatenate(
                [both[g, k, pl.ds((2 * i + m) * ROWS_L + HALO, rows), :] for g in range(GROUPS)], 1
            )
            for k in range(2)
            for m in range(2)
        ]
        plain = moved(jnp.concatenate(pieces, 0), spreader, transposed=True)
        at = pl.ds(pl.multiple_of(2 * i * rows, 8), 2 * rows)
        for h in range(2):
            lanes = slice(h * LANES, (h + 1) * LANES)
            settled[h, at, :] = plain[: 2 * rows, lanes]
            rest[h, at, :] = plain[2 * rows :, lanes] + src[h][at, :]

    def add_rows(i, total):
        values, hots = [], []
        for k in range(8):
            row = 8 * i + k
            at = pl.ds(row, steps, stride=rows)
            values += [rest[0, at, :], rest[1, at, :]]
            hots.append(one_hot_of(agg[pl.ds(row, 1), :], aggs, tile * aggs))
        return total + lax.dot_general(
            two_terms(jnp.concatenate(values, 1)), jnp.concatenate(hots, 1),
            (((1,), (1,)), ((), ())), preferred_element_type=F32,
        )

    total = lax.fori_loop(0, rows // 8, add_rows, jnp.zeros((2 * steps, aggs), F32))
    total = total[:steps] + total[steps:]
    coarse[...] = jnp.concatenate([total[: steps // 2], total[steps // 2 :]], 1)


def gather_kernel(axes, own, everyone, send, recv, pass_send, pass_recv, local):
    n_x, n_y = axes
    chips = n_x // 2 * n_y
    gx, gy = lax.axis_index("gx"), lax.axis_index("gy")
    core = lax.rem(gx, 2)
    chip = gx // 2 * n_y + gy
    partner = (gx + 1 - 2 * core, gy)

    def place(which, at_core):
        x, y = 2 * (which // n_y) + at_core, lax.rem(which, n_y)
        return (x, y), x * n_y + y

    def step_to(i):
        return place(lax.rem(chip + i, chips), core)[0]

    def step_from(i, at_core):
        return place(lax.rem(chip + chips - i, chips), at_core)[1]

    barrier = pltpu.get_barrier_semaphore()

    @pl.loop(1, chips)
    def _(i):
        pl.semaphore_signal(barrier, inc=1, device_id=step_to(i), device_id_type=MESH)

    pl.semaphore_signal(barrier, inc=1, device_id=partner, device_id_type=MESH)
    pl.semaphore_wait(barrier, chips)

    def spread(i, block):
        return pltpu.make_async_remote_copy(
            src_ref=own, dst_ref=everyone.at[block], send_sem=send.at[i], recv_sem=recv.at[i],
            device_id=step_to(i), device_id_type=MESH,
        )

    def hand_over(i, src, block):
        return pltpu.make_async_remote_copy(
            src_ref=src, dst_ref=everyone.at[block], send_sem=pass_send.at[i],
            recv_sem=pass_recv.at[i], device_id=partner, device_id_type=MESH,
        )

    me = gx * n_y + gy
    mine = pltpu.make_async_copy(own, everyone.at[me], local)

    @pl.loop(1, chips)
    def _(i):
        spread(i, me).start()

    hand_over(0, own, me).start()
    mine.start()

    @pl.loop(1, chips)
    def _(i):
        block = step_from(i, core)
        spread(i, block).wait_recv()
        hand_over(i, everyone.at[block], block).start()

    @pl.loop(1, chips)
    def _(i):
        spread(i, me).wait_send()

    @pl.loop(0, chips)
    def _(i):
        hand_over(i, own, me).wait_send()
        hand_over(i, own, step_from(i, 1 - core)).wait_recv()

    mine.wait()


def gather(axes, ident, own):
    count = axes[0] * axes[1]
    return pl.pallas_call(
        functools.partial(gather_kernel, axes),
        out_shape=jax.ShapeDtypeStruct((count,) + own.shape, F32),
        in_specs=[pl.BlockSpec(memory_space=pl.ANY)],
        out_specs=pl.BlockSpec(memory_space=pl.ANY),
        scratch_shapes=[
            pltpu.SemaphoreType.DMA((count // 2,)),
            pltpu.SemaphoreType.DMA((count // 2,)),
            pltpu.SemaphoreType.DMA((count // 2,)),
            pltpu.SemaphoreType.DMA((count // 2,)),
            pltpu.SemaphoreType.DMA,
        ],
        compiler_params=pltpu.CompilerParams(collective_id=ident, has_side_effects=True),
        name="coarse_gather",
    )(own)


def correct_kernel(axes, steps, rows, aggs, everyone, inverse, agg, settled, out, fixed):
    tile = lax.axis_index("gx") * axes[1] + lax.axis_index("gy")
    count = axes[0] * axes[1]

    @pl.when(pl.program_id(0) == 0)
    def _():
        low_lanes = lax.broadcasted_iota(jnp.int32, (steps // 2, LANES), 1) < aggs
        total = jnp.zeros((steps, aggs), F32)
        for d in range(0, count, 2):
            a, b = everyone[d], everyone[d + 1]
            upper = jnp.where(low_lanes, a, pltpu.roll(b, aggs, 1))
            lower = jnp.where(low_lanes, pltpu.roll(a, aggs, 1), b)
            total += lax.dot_general(
                jnp.concatenate([upper, lower], 0),
                inverse[:, d * aggs : (d + 2) * aggs],
                (((1,), (1,)), ((), ())),
                precision=lax.Precision.HIGHEST,
                preferred_element_type=F32,
            )
        high = total.astype(BF16)
        low = (total - high.astype(F32)).astype(BF16)
        fixed[...] = jnp.concatenate([high, low], 1)

    factor = fixed[...]

    @pl.loop(0, rows // 8)
    def _(i):
        hot = jnp.concatenate(
            [one_hot_of(agg[pl.ds(8 * i + k, 1), :], aggs, tile * aggs) for k in range(8)], 1
        )
        grown = jnp.dot(factor, jnp.concatenate([hot, hot], 0), preferred_element_type=F32)
        for k in range(8):
            at = pl.ds(8 * i + k, steps, stride=rows)
            out[at, :] = settled[0, at, :] + grown[:, k * LANES : (k + 1) * LANES]


def halves(shape):
    block = (shape[0], LANES)
    return [pl.BlockSpec(block, lambda i: (0, 0)), pl.BlockSpec(block, lambda i: (0, 1))]


def whole(shape):
    return pl.BlockSpec(shape, lambda i: (0,) * len(shape))


def shards(axes, prev_wave, source, start_state, storage, leakage, cond_east, cond_south,
           owner_weight, aggregate, coarse_inverse):
    steps, rows, cols = prev_wave.shape
    aggs = coarse_inverse.shape[0]
    planes = 2 * steps + 8
    strip_rows = HALO * planes - steps
    rim_rows = HALO * steps
    flat = (steps * rows, cols)
    prev, src = prev_wave.reshape(flat), source.reshape(flat)
    coef = (start_state, storage, leakage, cond_east, cond_south, owner_weight)
    params = pltpu.CompilerParams(vmem_limit_bytes=VMEM_LIMIT)
    fields, field_specs = [], []
    for arr in (prev, src) + coef:
        fields += [arr, arr]
        field_specs += halves(arr.shape)

    def local(kernel, name, args, in_specs, outs, scratch):
        return pl.pallas_call(
            kernel,
            grid=(1,),
            out_shape=[jax.ShapeDtypeStruct(s, F32) for s in outs],
            in_specs=in_specs,
            out_specs=[whole(s) for s in outs],
            scratch_shapes=scratch,
            compiler_params=params,
            name=name,
        )(*args)

    strips = local(
        functools.partial(pack_kernel, axes, steps, rows), "halo_pack", fields, field_specs,
        [(3, rows, LANES)] * 2 + [(2, strip_rows, LANES)] * 2 + [(8, LANES)] * 4, [],
    )
    halo = exchange(axes, 0, *strips)
    waves, co, *rims = local(
        functools.partial(sweep_kernel, axes, steps, rows), "local_sweep",
        fields + list(halo), field_specs + [whole(h.shape) for h in halo],
        [(3, steps * ROWS_L, LANES), (9, 3, ROWS_L, LANES)]
        + [(ROWS_L, LANES)] * 2 + [(3, rim_rows, LANES)] * 2 + [(8, LANES)] * 4,
        [
            pltpu.VMEM((3, planes * ROWS_L, LANES), F32),
            pltpu.VMEM((8, 3, VR, 8, LANES), F32),
            pltpu.VMEM((3, VR, 8, LANES), F32),
            pltpu.VMEM((3, VR, 8, LANES), F32),
            pltpu.VMEM((3, rim_rows, LANES), F32),
            pltpu.VMEM((3, rim_rows, LANES), F32),
        ],
    )
    rim = exchange(axes, 1, *rims)
    args = [waves, co, *rim]
    settled, coarse = local(
        functools.partial(settle_kernel, axes, steps, rows, aggs), "settle_and_restrict",
        args + [src, src, aggregate],
        [whole(a.shape) for a in args] + halves(flat) + [whole(aggregate.shape)],
        [(2, steps * rows, LANES), (steps // 2, 2 * aggs)],
        [
            pltpu.VMEM((3, VR, 8, LANES), F32),
            pltpu.VMEM((3, 2, steps * ROWS_L, LANES), F32),
            pltpu.VMEM((2, steps * rows, LANES), F32),
            pltpu.VMEM((3, rim_rows, LANES), F32),
            pltpu.VMEM((3, rim_rows, LANES), F32),
        ],
    )
    everyone = gather(axes, 2, coarse)
    out = pl.pallas_call(
        functools.partial(correct_kernel, axes, steps, rows, aggs),
        grid=(2,),
        out_shape=jax.ShapeDtypeStruct(flat, F32),
        in_specs=[
            whole(everyone.shape),
            whole(coarse_inverse.shape),
            pl.BlockSpec((rows, LANES), lambda i: (0, i)),
            pl.BlockSpec((1, steps * rows, LANES), lambda i: (i, 0, 0)),
        ],
        out_specs=pl.BlockSpec((steps * rows, LANES), lambda i: (0, i)),
        scratch_shapes=[pltpu.VMEM((steps, 2 * aggs), BF16)],
        compiler_params=params,
        name="correct",
    )(everyone, coarse_inverse, aggregate, settled)
    return out.reshape(prev_wave.shape)


def solution(mesh):
    axes = (mesh.shape["gx"], mesh.shape["gy"])
    plane = P("gy", "gx")
    wave = P(None, "gy", "gx")
    return jax.shard_map(
        functools.partial(shards, axes),
        mesh=mesh,
        in_specs=(wave, wave) + (plane,) * 7 + (P(("gx", "gy"), None),),
        out_specs=wave,
        check_vma=False,
    )
```

```python
import functools

import jax
import jax.numpy as jnp
from jax import lax
from jax.experimental import pallas as pl
from jax.experimental.pallas import tpu as pltpu
from jax.sharding import PartitionSpec as P

DEG = 8
OV = 2
HALO = OV + 1
LANES = 128
VR = 9
ROWS_L = 8 * VR
COEFS = 6
DELTA = 0.95
SIGMA = 1.0 / DELTA
GROUPS = 3
F32 = jnp.float32
BF16 = jnp.bfloat16
MESH = pl.DeviceIdType.MESH
VMEM_LIMIT = 56 * 1024 * 1024


def lane_id():
    return lax.broadcasted_iota(jnp.int32, (8, LANES), 1)


def sub_id():
    return lax.broadcasted_iota(jnp.int32, (8, LANES), 0)


def turn(x, by):
    by = by % LANES
    return pltpu.roll(x, by, 1) if not (isinstance(by, int) and by == 0) else x


def position(axes):
    gx, gy = lax.axis_index("gx"), lax.axis_index("gy")
    return gx > 0, gx < axes[0] - 1, gy > 0, gy < axes[1] - 1


def masked_coefs(refs, rows, half, axes, first_row):
    _, has_e, _, has_s = position(axes)
    start, sto, leak, east, south, owner = [ref[rows, :] for ref in refs]
    if half == 1:
        cut = jnp.logical_and(lane_id() == LANES - 1, jnp.logical_not(has_e))
        east = jnp.where(cut, 0.0, east)
    cut = jnp.logical_and(sub_id() + first_row == 63, jnp.logical_not(has_s))
    south = jnp.where(cut, 0.0, south)
    return start, sto, leak, east, south, owner.astype(F32)


def fields_of(refs):
    return refs[0:2], refs[2:4], [refs[4 + 2 * p : 6 + 2 * p] for p in range(COEFS)]


def pack_columns(axes, steps, rows, fields, xw, xe):
    prev, src, coef = fields
    group = lane_id() // 4

    @pl.loop(0, rows // 8)
    def _(t):
        first = pl.multiple_of(t * 8, 8)
        for k, arr in enumerate((prev, src)):
            low = jnp.zeros((8, LANES), F32)
            high = jnp.zeros((8, LANES), F32)
            for n in range(steps):
                at = pl.ds(pl.multiple_of(n * rows + first, 8), 8)
                low = jnp.where(group == n, turn(arr[0][at, :], 4 * n), low)
                high = jnp.where(group == n, turn(arr[1][at, :], 4 * n - 125), high)
            xw[k, pl.ds(first, 8), :] = low
            xe[k, pl.ds(first, 8), :] = high
        at = pl.ds(first, 8)
        low = jnp.zeros((8, LANES), F32)
        high = jnp.zeros((8, LANES), F32)
        planes0 = masked_coefs([c[0] for c in coef], at, 0, axes, first)
        planes1 = masked_coefs([c[1] for c in coef], at, 1, axes, first)
        for p in range(COEFS):
            low = jnp.where(group == p, turn(planes0[p], 4 * p), low)
            high = jnp.where(group == p, turn(planes1[p], 4 * p - 125), high)
        xw[2, at, :] = low
        xe[2, at, :] = high


def pack_rows(axes, steps, rows, fields, yn, ys, corners):
    prev, src, coef = fields
    group = lane_id() // 4
    for side, (out, first, base) in enumerate(((yn, 0, 0), (ys, rows - HALO, rows - 8))):
        for h in range(2):
            planes = masked_coefs([c[h] for c in coef], pl.ds(base, 8), h, axes, base)
            corner = jnp.zeros((8, LANES), F32)
            for q, j, at in strip_blocks(steps, side):
                if q < 2 * steps // 8:
                    arr, part = (prev, q) if q < steps // 8 else (src, q - steps // 8)
                    value = arr[h][pl.ds(8 * part * rows + first + j, 8, stride=rows), :]
                else:
                    row = first + j - base
                    pieces = [p[row : row + 1] for p in planes]
                    value = jnp.concatenate(pieces + [jnp.zeros((8 - COEFS, LANES), F32)], 0)
                out[h, at : at + 8, :] = value
                slot = 4 * (HALO * q + j)
                corner = jnp.where(group == slot // 4, turn(value, slot - (0, 125)[h]), corner)
            corners[2 * side + h][...] = corner


def strip_blocks(steps, side):
    at, blocks = 0, []
    for q in range(2 * steps // 8 + 1):
        for j in range(HALO):
            if steps // 8 <= q < 2 * steps // 8 and j == (HALO - 1, 0)[side]:
                continue
            blocks.append((q, j, at))
            at += 8
    return blocks


def plan_of(axes, strips, outs, send, recv):
    xw, xe, yn, ys, c_nw, c_ne, c_sw, c_se = strips
    gx, gy = lax.axis_index("gx"), lax.axis_index("gy")
    has_w, has_e, has_n, has_s = position(axes)
    west, east, north, south = gx - 1, gx + 1, gy - 1, gy + 1
    both = jnp.logical_and
    has_nw, has_ne = both(has_n, has_w), both(has_n, has_e)
    has_sw, has_se = both(has_s, has_w), both(has_s, has_e)
    from_w, from_e, from_n, from_s, from_nw, from_ne, from_sw, from_se = outs
    steps = (
        (yn, from_s, (gx, north), has_n, has_s),
        (ys, from_n, (gx, south), has_s, has_n),
        (c_nw, from_se, (west, north), has_nw, has_se),
        (c_ne, from_sw, (east, north), has_ne, has_sw),
        (c_sw, from_ne, (west, south), has_sw, has_ne),
        (c_se, from_nw, (east, south), has_se, has_nw),
        (xw, from_e, (west, gy), has_w, has_e),
        (xe, from_w, (east, gy), has_e, has_w),
    )
    plan = []
    for i, (src, dst, to, goes, comes) in enumerate(steps):
        copy = pltpu.make_async_remote_copy(
            src_ref=src, dst_ref=dst, send_sem=send.at[i], recv_sem=recv.at[i],
            device_id=to, device_id_type=MESH,
        )
        plan.append((copy, to, goes, comes))
    return plan


def greet(plan):
    barrier = pltpu.get_barrier_semaphore()
    for _, to, goes, _ in plan:

        @pl.when(goes)
        def _():
            pl.semaphore_signal(barrier, inc=1, device_id=to, device_id_type=MESH)

    return lambda: pl.semaphore_wait(barrier, sum(jnp.where(step[2], 1, 0) for step in plan))


def start_all(plan):
    for copy, _, goes, _ in plan:
        pl.when(goes)(copy.start)


def wait_all(plan):
    for copy, _, goes, comes in plan:
        pl.when(goes)(copy.wait_send)
        pl.when(comes)(copy.wait_recv)


def exchange_kernel(axes, *refs):
    plan = plan_of(axes, refs[:8], refs[8:16], *refs[16:])
    greet(plan)()
    start_all(plan)
    wait_all(plan)


def halo_kernel(axes, steps, rows, *refs):
    count = 4 + 2 * COEFS
    fields, outs = fields_of(refs[:count]), refs[count : count + 8]
    strips = refs[count + 8 : count + 16]
    plan = plan_of(axes, strips, outs, *refs[count + 16 :])
    all_here = greet(plan)
    pack_rows(axes, steps, rows, fields, strips[2], strips[3], strips[4:])
    all_here()
    start_all(plan[:6])
    pack_columns(axes, steps, rows, fields, strips[0], strips[1])
    start_all(plan[6:])
    wait_all(plan)


def halo_exchange(axes, ident, steps, rows, fields, field_specs, shapes):
    return pl.pallas_call(
        functools.partial(halo_kernel, axes, steps, rows),
        grid=(1,),
        out_shape=[jax.ShapeDtypeStruct(s, F32) for s in shapes],
        in_specs=field_specs,
        out_specs=[pl.BlockSpec(memory_space=pl.ANY)] * 8,
        scratch_shapes=[pltpu.VMEM(s, F32) for s in shapes]
        + [pltpu.SemaphoreType.DMA((8,)), pltpu.SemaphoreType.DMA((8,))],
        compiler_params=pltpu.CompilerParams(
            collective_id=ident, has_side_effects=True, vmem_limit_bytes=VMEM_LIMIT
        ),
        name="halo_exchange",
    )(*fields)


def exchange(axes, ident, *strips):
    return pl.pallas_call(
        functools.partial(exchange_kernel, axes),
        out_shape=[jax.ShapeDtypeStruct(s.shape, F32) for s in strips],
        in_specs=[pl.BlockSpec(memory_space=pl.ANY)] * 8,
        out_specs=[pl.BlockSpec(memory_space=pl.ANY)] * 8,
        scratch_shapes=[pltpu.SemaphoreType.DMA((8,)), pltpu.SemaphoreType.DMA((8,))],
        compiler_params=pltpu.CompilerParams(collective_id=ident, has_side_effects=True),
        name="neighbour_exchange",
    )(*strips)


def spread_matrix(cols):
    shape = (cols, GROUPS * LANES)
    at = lax.broadcasted_iota(jnp.int32, shape, 1)
    col = (at % LANES) * GROUPS + at // LANES - HALO
    return jnp.where(col == lax.broadcasted_iota(jnp.int32, shape, 0), 1.0, 0.0).astype(BF16)


def collect_matrix(cols):
    shape = (GROUPS * LANES, cols)
    at = lax.broadcasted_iota(jnp.int32, shape, 0)
    col = (at % LANES) * GROUPS + at // LANES - HALO
    return jnp.where(col == lax.broadcasted_iota(jnp.int32, shape, 1), 1.0, 0.0).astype(BF16)


def two_terms(values):
    high = values.astype(BF16)
    return jnp.concatenate([high, (values - high.astype(F32)).astype(BF16)], 0)


def moved(values, matrix):
    both = jnp.dot(two_terms(values), matrix, preferred_element_type=F32)
    return both[: values.shape[0]] + both[values.shape[0] :]


def add_halo(parts, west, east, shift):
    lane = lane_id()
    at_86 = lane == 86
    far = turn(east, 85 + shift)
    return (
        jnp.where(lane == 0, turn(west, shift), jnp.where(lane == 87, far, parts[0])),
        jnp.where(lane == 0, turn(west, shift - 1), jnp.where(at_86, turn(east, 86 + shift), parts[1])),
        jnp.where(lane == 0, turn(west, shift - 2), jnp.where(at_86, far, parts[2])),
    )


def west_edge(parts, to):
    lane = lane_id()
    pair = turn(jnp.where(lane == 0, parts[2], parts[0]), to + 1)
    return jnp.where(lane == to, turn(parts[1], to), pair)


def east_edge(parts, to):
    lane = lane_id()
    last = jnp.where(lane == to + 1, turn(parts[1], to - 85 + LANES), turn(parts[2], to - 84 + LANES))
    return jnp.where(lane == to, turn(parts[0], to - 86 + LANES), last)


def add_west(parts, strip, shift, flag):
    lane, out = lane_id(), list(parts)
    near = jnp.where(flag, turn(strip, shift), 0.0)
    out[2] += jnp.where(lane == 0, near, 0.0)
    out[0] += jnp.where(lane == 1, near, 0.0)
    out[1] += jnp.where(jnp.logical_and(lane == 1, flag), turn(strip, shift - 1), 0.0)
    return out


def add_east(parts, strip, shift, flag):
    lane, out = lane_id(), list(parts)
    near = jnp.where(flag, turn(strip, 85 + shift), 0.0)
    out[2] += jnp.where(lane == 85, near, 0.0)
    out[0] += jnp.where(lane == 86, near, 0.0)
    out[1] += jnp.where(jnp.logical_and(lane == 86, flag), turn(strip, 84 + shift), 0.0)
    return out


def neighbours(y, g, v):
    down = y[g][v + 1] if v < VR - 1 else pltpu.roll(y[g][0], 7, 0)
    up = y[g][v - 1] if v else pltpu.roll(y[g][VR - 1], 1, 0)
    east = y[g + 1][v] if g < GROUPS - 1 else turn(y[0][v], LANES - 1)
    west = y[g - 1][v] if g else turn(y[GROUPS - 1][v], 1)
    return east, west, down, up


def sweep_kernel(axes, steps, rows, *refs):
    prev, src = refs[0:2], refs[2:4]
    coef = [refs[4 + 2 * p : 6 + 2 * p] for p in range(COEFS)]
    base = 4 + 2 * COEFS
    from_w, from_e, from_n, from_s, from_nw, from_ne, from_sw, from_se = refs[base : base + 8]
    waves, co, xw, xe, yn, ys = refs[base + 8 : base + 14]
    corners = refs[base + 14 : base + 18]
    ext, cc, gbuf, carry, north_rows, south_rows = refs[base + 18 :]
    has_w, has_e, has_n, has_s = position(axes)
    lane, sub = lane_id(), sub_id()
    zero = jnp.zeros((8, LANES), F32)

    def keep(flag, value):
        return jnp.where(flag, value, 0.0)

    spreader = spread_matrix(2 * LANES)

    def put_own(plane, t, parts, k, slot):
        at = pl.ds(t * 8, 8)
        west, east = keep(has_w, from_w[k, at, :]), keep(has_e, from_e[k, at, :])
        for g, value in enumerate(add_halo(parts, west, east, 4 * LANES - 4 * slot)):
            ext[g, pl.ds(plane * ROWS_L + HALO + 8 * t, 8), :] = value

    def part_of(wide, first):
        return [wide[first : first + 8, g * LANES : (g + 1) * LANES] for g in range(GROUPS)]

    @pl.loop(0, steps // 4)
    def _(i):
        for k, arr in enumerate((prev, src)):
            at = pl.ds(pl.multiple_of(4 * i * rows, 8), 4 * rows)
            wide = moved(jnp.concatenate([arr[0][at, :], arr[1][at, :]], 1), spreader)
            for m in range(4):
                n = 4 * i + m
                for t in range(rows // 8):
                    put_own(k * steps + n, t, part_of(wide, m * rows + 8 * t), k, n)

    lows, highs = [], []
    for t in range(rows // 8):
        at = pl.ds(8 * t, 8)
        lows += masked_coefs([c[0] for c in coef], at, 0, axes, 8 * t)
        highs += masked_coefs([c[1] for c in coef], at, 1, axes, 8 * t)
    wide = jnp.concatenate([jnp.concatenate(lows, 0), jnp.concatenate(highs, 0)], 1)
    wide = moved(wide, spreader)
    for t in range(rows // 8):
        for p in range(COEFS):
            put_own(2 * steps + p, t, part_of(wide, 8 * (t * COEFS + p)), 2, p)
    for side, (strip, cw, ce, flag, first) in enumerate((
        (from_n, from_nw, from_ne, has_n, 0),
        (from_s, from_sw, from_se, has_s, rows + HALO),
    )):
        wide = moved(keep(flag, jnp.concatenate([strip[0], strip[1]], 1)), spreader)
        west = keep(jnp.logical_and(flag, has_w), cw[...])
        east = keep(jnp.logical_and(flag, has_e), ce[...])
        for q, j, at in strip_blocks(steps, 1 - side):
            shift = 4 * LANES - 4 * (HALO * q + j)
            for g, value in enumerate(add_halo(part_of(wide, at), west, east, shift)):
                ext[g, pl.ds(8 * q * ROWS_L + first + j, 8, stride=ROWS_L), :] = value
    for row in (0, rows + 2 * HALO - 1):
        for q in range(steps // 8, 2 * steps // 8):
            for g in range(3):
                ext[g, pl.ds(8 * q * ROWS_L + row, 8, stride=ROWS_L), :] = zero
    for row in range(rows + 2 * HALO, ROWS_L):
        for q in range(2 * steps // 8 + 1):
            for g in range(3):
                ext[g, pl.ds(8 * q * ROWS_L + row, 8, stride=ROWS_L), :] = zero

    def plane(index, v, g):
        return ext[g, pl.ds(index * ROWS_L + v, 8, stride=VR), :]

    first_coef = 2 * steps
    easts = [[plane(2 * steps + 3, v, g) for v in range(VR)] for g in range(3)]
    for g in range(3):
        col = lane * GROUPS + g
        col_in = jnp.logical_and(col >= 1, col <= 260)
        col_own = jnp.logical_and(col >= HALO, col <= 258)
        col_there = jnp.logical_and(
            jnp.logical_or(col >= HALO, has_w), jnp.logical_or(col <= 258, has_e)
        )
        n_cols = (
            1.0
            + jnp.where(jnp.logical_and(col <= 4, has_w), 1.0, 0.0)
            + jnp.where(jnp.logical_and(col >= 257, has_e), 1.0, 0.0)
        )
        souths = [plane(first_coef + 4, v, g) for v in range(VR)]
        for v in range(VR):
            row = sub * VR + v
            row_in = jnp.logical_and(row >= 1, row <= 68)
            row_own = jnp.logical_and(row >= HALO, row <= 66)
            row_there = jnp.logical_and(
                jnp.logical_or(row >= HALO, has_n), jnp.logical_or(row <= 66, has_s)
            )
            inner = jnp.logical_and(row_in, col_in)
            own = jnp.logical_and(row_own, col_own)
            there = jnp.logical_and(jnp.logical_and(row_there, col_there), inner)
            n_rows = (
                1.0
                + jnp.where(jnp.logical_and(row <= 4, has_n), 1.0, 0.0)
                + jnp.where(jnp.logical_and(row >= 65, has_s), 1.0, 0.0)
            )
            start, sto, leak, east, south, owner = [
                plane(first_coef + p, v, g) for p in range(COEFS)
            ]
            ea_w = easts[g - 1][v] if g else turn(easts[GROUPS - 1][v], 1)
            so_n = souths[v - 1] if v else pltpu.roll(souths[VR - 1], 1, 0)
            diag = sto + leak + east + ea_w + south + so_n
            safe = jnp.where(there, diag, 1.0)
            scale = jnp.where(there, 2.0 * SIGMA / safe, 0.0)
            cc[0, g, v] = scale * east
            cc[1, g, v] = scale * ea_w
            cc[2, g, v] = scale * south
            cc[3, g, v] = scale * so_n
            cc[4, g, v] = scale
            cc[5, g, v] = scale * sto
            cc[6, g, v] = jnp.where(inner, 0.0, 2.0 * SIGMA)
            weight = jnp.where(own, owner, jnp.where(there, 1.0, 0.0))
            cc[7, g, v] = weight * (1.0 / TAU[DEG])
            den = jnp.where(there, owner + n_rows * n_cols - 1.0, 1.0)
            at = slice(8 * v, 8 * v + 8)
            co[0, g, at, :] = weight
            co[1, g, at, :] = jnp.where(there, 1.0 / den, 0.0)
            co[2, g, at, :] = diag
            co[3, g, at, :] = east
            co[4, g, at, :] = ea_w
            co[5, g, at, :] = south
            co[6, g, at, :] = so_n
            co[7, g, at, :] = sto
            co[8, g, at, :] = start
            carry[g, v] = start

    xw[...] = jnp.zeros_like(xw)
    xe[...] = jnp.zeros_like(xe)
    group = lane // 4

    def stencil(y, g, v):
        east, west, down, up = neighbours(y, g, v)
        return (cc[0, g, v] * east + cc[1, g, v] * west) + (cc[2, g, v] * down + cc[3, g, v] * up)

    def advance(n, held):
        def each(value):
            out = [[None] * VR for _ in range(GROUPS)]
            for v in range(VR):
                for g in range(GROUPS):
                    out[g][v] = value(g, v)
            return out

        old = each(lambda g, v: plane(n, v, g))
        for v in range(VR):
            for g in range(GROUPS):
                gbuf[g, v] = (
                    cc[4, g, v] * plane(steps + n, v, g)
                    + cc[5, g, v] * held[g][v]
                    + cc[6, g, v] * old[g][v]
                )
        now = each(lambda g, v: 0.5 * (stencil(old, g, v) + gbuf[g, v]))
        for k in range(1, DEG):
            new = each(lambda g, v: stencil(now, g, v) + (TAU[k] * gbuf[g, v] - old[g][v]))
            old, now = now, new
        return now

    def finish(n, now):
        for g in range(3):
            for v in range(VR):
                at = pl.ds(pl.multiple_of(n * ROWS_L + 8 * v, 8), 8)
                waves[g, at, :] = now[g][v] * (1.0 / TAU[DEG])
        weighted = [[cc[7, g, v] * now[g][v] for v in range(VR)] for g in range(3)]
        for v in range(VR):
            at = slice(8 * v, 8 * v + 8)
            parts = [weighted[g][v] for g in range(GROUPS)]
            xw[at, :] = jnp.where(group == n, west_edge(parts, 4 * n), xw[at, :])
            xe[at, :] = jnp.where(group == n, east_edge(parts, 4 * n), xe[at, :])
        for j in range(HALO):
            for g in range(3):
                north_rows[g, pl.ds(j * steps + n, 1), :] = weighted[g][1 + j][0:1]
                south_rows[g, pl.ds(j * steps + n, 1), :] = weighted[g][3 + j][7:8]
        return [[now[g][v] * (1.0 / TAU[DEG]) for v in range(VR)] for g in range(3)]

    @pl.loop(0, steps)
    def _(n):
        held = [[carry[g, v] for v in range(VR)] for g in range(3)]
        held = finish(n, advance(n, held))
        for g in range(GROUPS):
            for v in range(VR):
                carry[g, v] = held[g][v]

    collector = collect_matrix(2 * LANES)
    for side, (rows_of, out) in enumerate(((north_rows, yn), (south_rows, ys))):
        west, east = zero, zero
        for i in range(HALO * steps // 8):
            at = slice(8 * i, 8 * i + 8)
            parts = [rows_of[g, at, :] for g in range(GROUPS)]
            west = jnp.where(group == i, west_edge(parts, 4 * i), west)
            east = jnp.where(group == i, east_edge(parts, 4 * i), east)
        plain = moved(jnp.concatenate([rows_of[g] for g in range(GROUPS)], 1), collector)
        for h, pack in enumerate((west, east)):
            out[h, : HALO * steps, :] = plain[:, h * LANES : (h + 1) * LANES]
            out[h, HALO * steps :, :] = pack
            corners[2 * side + h][...] = pack


def chebyshev_scales():
    tau = [1.0, SIGMA]
    for _ in range(DEG):
        tau.append(2.0 * SIGMA * tau[-1] - tau[-2])
    return tau


TAU = chebyshev_scales()


def one_hot_of(row, count, first):
    ids = jnp.broadcast_to(row - first, (count, row.shape[1]))
    return jnp.where(
        ids == lax.broadcasted_iota(jnp.int32, ids.shape, 0), 1.0, 0.0
    ).astype(BF16)


def settle_kernel(axes, steps, rows, aggs, *refs):
    waves, co, from_w, from_e, from_n, from_s, from_nw, from_ne, from_sw, from_se = refs[:10]
    src = refs[10:12]
    agg = refs[12]
    settled, coarse = refs[13:15]
    before, both, rest, north, south = refs[15:]
    has_w, has_e, has_n, has_s = position(axes)
    lane, sub = lane_id(), sub_id()
    tile = lax.axis_index("gx") * axes[1] + lax.axis_index("gy")

    for g in range(3):
        for v in range(VR):
            before[g, v] = co[8, g, 8 * v : 8 * v + 8, :]


    def spread(row):
        return jnp.broadcast_to(row, (8, LANES))

    spreader = spread_matrix(2 * LANES)
    for strip, cw, ce, flag, out in (
        (from_n, from_nw, from_ne, has_n, north),
        (from_s, from_sw, from_se, has_s, south),
    ):
        rim = HALO * steps
        wide = moved(jnp.concatenate([strip[0, :rim, :], strip[1, :rim, :]], 1), spreader)
        west, east = strip[0, rim:, :], strip[1, rim:, :]
        for i in range(rim // 8):
            at = slice(8 * i, 8 * i + 8)
            parts = [wide[at, g * LANES : (g + 1) * LANES] for g in range(GROUPS)]
            parts[2] = jnp.where(lane == 0, turn(west, -1 - 4 * i), parts[2])
            parts[1] = jnp.where(lane == 86, turn(east, 85 - 4 * i), parts[1])
            parts = add_west(parts, cw[...], -4 * i, has_w)
            parts = add_east(parts, ce[...], -4 * i, has_e)
            for g, value in enumerate(parts):
                out[g, at, :] = jnp.where(flag, value, 0.0)

    @pl.loop(0, steps)
    def _(n):
        now = [[None] * VR for _ in range(3)]
        for v in range(VR):
            at = slice(8 * v, 8 * v + 8)
            here = pl.ds(pl.multiple_of(n * ROWS_L + 8 * v, 8), 8)
            parts = [co[0, g, at, :] * waves[g, here, :] for g in range(GROUPS)]
            shift = 4 * LANES - 4 * n
            parts = add_west(parts, from_w[at, :], shift, has_w)
            parts = add_east(parts, from_e[at, :], shift, has_e)
            for g, total in enumerate(parts):
                if 2 <= v <= 4:
                    one = pl.ds((v - 2) * steps + n, 1)
                    total += jnp.where(sub == 0, spread(north[g, one, :]), 0.0)
                    total += jnp.where(sub == 7, spread(south[g, one, :]), 0.0)
                now[g][v] = total * co[1, g, at, :]
        out = [[None] * VR for _ in range(3)]
        for g in range(3):
            for v in range(VR):
                at = slice(8 * v, 8 * v + 8)
                cur = now[g][v]
                east, west, down, up = neighbours(now, g, v)
                image = (
                    co[2, g, at, :] * cur
                    - co[3, g, at, :] * east
                    - co[4, g, at, :] * west
                    - co[5, g, at, :] * down
                    - co[6, g, at, :] * up
                )
                out[g][v] = co[7, g, at, :] * before[g, v] - image
                before[g, v] = cur
        for v in range(VR):
            at = pl.ds(n * ROWS_L + v, 8, stride=VR)
            for g in range(GROUPS):
                both[g, 0, at, :] = now[g][v]
                both[g, 1, at, :] = out[g][v]

    collector = collect_matrix(2 * LANES)

    @pl.loop(0, steps // 2)
    def _(i):
        pieces = [
            jnp.concatenate(
                [both[g, k, pl.ds((2 * i + m) * ROWS_L + HALO, rows), :] for g in range(GROUPS)], 1
            )
            for k in range(2)
            for m in range(2)
        ]
        plain = moved(jnp.concatenate(pieces, 0), collector)
        at = pl.ds(pl.multiple_of(2 * i * rows, 8), 2 * rows)
        for h in range(2):
            lanes = slice(h * LANES, (h + 1) * LANES)
            settled[h, at, :] = plain[: 2 * rows, lanes]
            rest[h, at, :] = plain[2 * rows :, lanes] + src[h][at, :]

    def add_rows(i, total):
        values, hots = [], []
        for k in range(8):
            row = 8 * i + k
            at = pl.ds(row, steps, stride=rows)
            values += [rest[0, at, :], rest[1, at, :]]
            hots.append(one_hot_of(agg[pl.ds(row, 1), :], aggs, tile * aggs))
        return total + lax.dot_general(
            two_terms(jnp.concatenate(values, 1)), jnp.concatenate(hots, 1),
            (((1,), (1,)), ((), ())), preferred_element_type=F32,
        )

    total = lax.fori_loop(0, rows // 8, add_rows, jnp.zeros((2 * steps, aggs), F32))
    total = total[:steps] + total[steps:]
    coarse[...] = jnp.concatenate([total[: steps // 2], total[steps // 2 :]], 1)


def gather_kernel(axes, own, everyone, send, recv, pass_send, pass_recv, local):
    n_x, n_y = axes
    chips = n_x // 2 * n_y
    gx, gy = lax.axis_index("gx"), lax.axis_index("gy")
    core = lax.rem(gx, 2)
    chip = gx // 2 * n_y + gy
    partner = (gx + 1 - 2 * core, gy)

    def place(which, at_core):
        x, y = 2 * (which // n_y) + at_core, lax.rem(which, n_y)
        return (x, y), x * n_y + y

    def step_to(i):
        return place(lax.rem(chip + i, chips), core)[0]

    def step_from(i, at_core):
        return place(lax.rem(chip + chips - i, chips), at_core)[1]

    barrier = pltpu.get_barrier_semaphore()

    @pl.loop(1, chips)
    def _(i):
        pl.semaphore_signal(barrier, inc=1, device_id=step_to(i), device_id_type=MESH)

    pl.semaphore_signal(barrier, inc=1, device_id=partner, device_id_type=MESH)
    pl.semaphore_wait(barrier, chips)

    def spread(i, block):
        return pltpu.make_async_remote_copy(
            src_ref=own, dst_ref=everyone.at[block], send_sem=send.at[i], recv_sem=recv.at[i],
            device_id=step_to(i), device_id_type=MESH,
        )

    def hand_over(i, src, block):
        return pltpu.make_async_remote_copy(
            src_ref=src, dst_ref=everyone.at[block], send_sem=pass_send.at[i],
            recv_sem=pass_recv.at[i], device_id=partner, device_id_type=MESH,
        )

    me = gx * n_y + gy
    mine = pltpu.make_async_copy(own, everyone.at[me], local)

    @pl.loop(1, chips)
    def _(i):
        spread(i, me).start()

    hand_over(0, own, me).start()
    mine.start()

    @pl.loop(1, chips)
    def _(i):
        block = step_from(i, core)
        spread(i, block).wait_recv()
        hand_over(i, everyone.at[block], block).start()

    @pl.loop(1, chips)
    def _(i):
        spread(i, me).wait_send()

    @pl.loop(0, chips)
    def _(i):
        hand_over(i, own, me).wait_send()
        hand_over(i, own, step_from(i, 1 - core)).wait_recv()

    mine.wait()


def gather(axes, ident, own):
    count = axes[0] * axes[1]
    return pl.pallas_call(
        functools.partial(gather_kernel, axes),
        out_shape=jax.ShapeDtypeStruct((count,) + own.shape, F32),
        in_specs=[pl.BlockSpec(memory_space=pl.ANY)],
        out_specs=pl.BlockSpec(memory_space=pl.ANY),
        scratch_shapes=[
            pltpu.SemaphoreType.DMA((count // 2,)),
            pltpu.SemaphoreType.DMA((count // 2,)),
            pltpu.SemaphoreType.DMA((count // 2,)),
            pltpu.SemaphoreType.DMA((count // 2,)),
            pltpu.SemaphoreType.DMA,
        ],
        compiler_params=pltpu.CompilerParams(collective_id=ident, has_side_effects=True),
        name="coarse_gather",
    )(own)


def correct_kernel(axes, steps, rows, aggs, everyone, inverse, agg, settled, out, fixed):
    tile = lax.axis_index("gx") * axes[1] + lax.axis_index("gy")
    count = axes[0] * axes[1]

    @pl.when(pl.program_id(0) == 0)
    def _():
        low_lanes = lax.broadcasted_iota(jnp.int32, (steps // 2, LANES), 1) < aggs
        total = jnp.zeros((steps, aggs), F32)
        for d in range(0, count, 2):
            a, b = everyone[d], everyone[d + 1]
            upper = jnp.where(low_lanes, a, pltpu.roll(b, aggs, 1))
            lower = jnp.where(low_lanes, pltpu.roll(a, aggs, 1), b)
            total += lax.dot_general(
                jnp.concatenate([upper, lower], 0),
                inverse[:, d * aggs : (d + 2) * aggs],
                (((1,), (1,)), ((), ())),
                precision=lax.Precision.HIGHEST,
                preferred_element_type=F32,
            )
        high = total.astype(BF16)
        low = (total - high.astype(F32)).astype(BF16)
        fixed[...] = jnp.concatenate([high, low], 1)

    factor = fixed[...]

    @pl.loop(0, rows // 8)
    def _(i):
        hot = jnp.concatenate(
            [one_hot_of(agg[pl.ds(8 * i + k, 1), :], aggs, tile * aggs) for k in range(8)], 1
        )
        grown = jnp.dot(factor, jnp.concatenate([hot, hot], 0), preferred_element_type=F32)
        for k in range(8):
            at = pl.ds(8 * i + k, steps, stride=rows)
            out[at, :] = settled[0, at, :] + grown[:, k * LANES : (k + 1) * LANES]


def halves(shape):
    block = (shape[0], LANES)
    return [pl.BlockSpec(block, lambda i: (0, 0)), pl.BlockSpec(block, lambda i: (0, 1))]


def whole(shape):
    return pl.BlockSpec(shape, lambda i: (0,) * len(shape))


def shards(axes, prev_wave, source, start_state, storage, leakage, cond_east, cond_south,
           owner_weight, aggregate, coarse_inverse):
    steps, rows, cols = prev_wave.shape
    aggs = coarse_inverse.shape[0]
    planes = 2 * steps + 8
    strip_rows = HALO * planes - steps
    rim_rows = HALO * steps
    flat = (steps * rows, cols)
    prev, src = prev_wave.reshape(flat), source.reshape(flat)
    coef = (start_state, storage, leakage, cond_east, cond_south, owner_weight)
    params = pltpu.CompilerParams(vmem_limit_bytes=VMEM_LIMIT)
    fields, field_specs = [], []
    for arr in (prev, src) + coef:
        fields += [arr, arr]
        field_specs += halves(arr.shape)

    def local(kernel, name, args, in_specs, outs, scratch):
        return pl.pallas_call(
            kernel,
            grid=(1,),
            out_shape=[jax.ShapeDtypeStruct(s, F32) for s in outs],
            in_specs=in_specs,
            out_specs=[whole(s) for s in outs],
            scratch_shapes=scratch,
            compiler_params=params,
            name=name,
        )(*args)

    shapes = [(3, rows, LANES)] * 2 + [(2, strip_rows, LANES)] * 2 + [(8, LANES)] * 4
    halo = halo_exchange(axes, 0, steps, rows, fields, field_specs, shapes)
    waves, co, *rims = local(
        functools.partial(sweep_kernel, axes, steps, rows), "local_sweep",
        fields + list(halo), field_specs + [whole(h.shape) for h in halo],
        [(3, steps * ROWS_L, LANES), (9, 3, ROWS_L, LANES)]
        + [(ROWS_L, LANES)] * 2 + [(2, rim_rows + 8, LANES)] * 2 + [(8, LANES)] * 4,
        [
            pltpu.VMEM((3, planes * ROWS_L, LANES), F32),
            pltpu.VMEM((8, 3, VR, 8, LANES), F32),
            pltpu.VMEM((3, VR, 8, LANES), F32),
            pltpu.VMEM((3, VR, 8, LANES), F32),
            pltpu.VMEM((3, rim_rows, LANES), F32),
            pltpu.VMEM((3, rim_rows, LANES), F32),
        ],
    )
    rim = exchange(axes, 1, *rims)
    args = [waves, co, *rim]
    settled, coarse = local(
        functools.partial(settle_kernel, axes, steps, rows, aggs), "settle_and_restrict",
        args + [src, src, aggregate],
        [whole(a.shape) for a in args] + halves(flat) + [whole(aggregate.shape)],
        [(2, steps * rows, LANES), (steps // 2, 2 * aggs)],
        [
            pltpu.VMEM((3, VR, 8, LANES), F32),
            pltpu.VMEM((3, 2, steps * ROWS_L, LANES), F32),
            pltpu.VMEM((2, steps * rows, LANES), F32),
            pltpu.VMEM((3, rim_rows, LANES), F32),
            pltpu.VMEM((3, rim_rows, LANES), F32),
        ],
    )
    everyone = gather(axes, 2, coarse)
    out = pl.pallas_call(
        functools.partial(correct_kernel, axes, steps, rows, aggs),
        grid=(2,),
        out_shape=jax.ShapeDtypeStruct(flat, F32),
        in_specs=[
            whole(everyone.shape),
            whole(coarse_inverse.shape),
            pl.BlockSpec((rows, LANES), lambda i: (0, i)),
            pl.BlockSpec((1, steps * rows, LANES), lambda i: (i, 0, 0)),
        ],
        out_specs=pl.BlockSpec((steps * rows, LANES), lambda i: (0, i)),
        scratch_shapes=[pltpu.VMEM((steps, 2 * aggs), BF16)],
        compiler_params=params,
        name="correct",
    )(everyone, coarse_inverse, aggregate, settled)
    return out.reshape(prev_wave.shape)


def solution(mesh):
    axes = (mesh.shape["gx"], mesh.shape["gy"])
    plane = P("gy", "gx")
    wave = P(None, "gy", "gx")
    return jax.shard_map(
        functools.partial(shards, axes),
        mesh=mesh,
        in_specs=(wave, wave) + (plane,) * 7 + (P(("gx", "gy"), None),),
        out_specs=wave,
        check_vma=False,
    )
```

```python
import functools

import jax
import jax.numpy as jnp
from jax import lax
from jax.experimental import pallas as pl
from jax.experimental.pallas import tpu as pltpu
from jax.sharding import PartitionSpec as P

DEG = 8
OV = 2
HALO = OV + 1
LANES = 128
VR = 9
ROWS_L = 8 * VR
COEFS = 6
DELTA = 0.95
SIGMA = 1.0 / DELTA
GROUPS = 3
CHUNKS = 4
F32 = jnp.float32
BF16 = jnp.bfloat16
MESH = pl.DeviceIdType.MESH
VMEM_LIMIT = 56 * 1024 * 1024


def lane_id():
    return lax.broadcasted_iota(jnp.int32, (8, LANES), 1)


def sub_id():
    return lax.broadcasted_iota(jnp.int32, (8, LANES), 0)


def turn(x, by):
    by = by % LANES
    return pltpu.roll(x, by, 1) if not (isinstance(by, int) and by == 0) else x


def position(axes):
    gx, gy = lax.axis_index("gx"), lax.axis_index("gy")
    return gx > 0, gx < axes[0] - 1, gy > 0, gy < axes[1] - 1


def masked_coefs(refs, rows, half, axes, first_row):
    _, has_e, _, has_s = position(axes)
    start, sto, leak, east, south, owner = [ref[rows, :] for ref in refs]
    if half == 1:
        cut = jnp.logical_and(lane_id() == LANES - 1, jnp.logical_not(has_e))
        east = jnp.where(cut, 0.0, east)
    cut = jnp.logical_and(sub_id() + first_row == 63, jnp.logical_not(has_s))
    south = jnp.where(cut, 0.0, south)
    return start, sto, leak, east, south, owner.astype(F32)


def fields_of(refs):
    return refs[0:2], refs[2:4], [refs[4 + 2 * p : 6 + 2 * p] for p in range(COEFS)]


def pack_columns(axes, steps, rows, fields, xw, xe):
    prev, src, coef = fields
    group = lane_id() // 4

    @pl.loop(0, rows // 8)
    def _(t):
        first = pl.multiple_of(t * 8, 8)
        for k, arr in enumerate((prev, src)):
            low = jnp.zeros((8, LANES), F32)
            high = jnp.zeros((8, LANES), F32)
            for n in range(steps):
                at = pl.ds(pl.multiple_of(n * rows + first, 8), 8)
                low = jnp.where(group == n, turn(arr[0][at, :], 4 * n), low)
                high = jnp.where(group == n, turn(arr[1][at, :], 4 * n - 125), high)
            xw[k, pl.ds(first, 8), :] = low
            xe[k, pl.ds(first, 8), :] = high
        at = pl.ds(first, 8)
        low = jnp.zeros((8, LANES), F32)
        high = jnp.zeros((8, LANES), F32)
        planes0 = masked_coefs([c[0] for c in coef], at, 0, axes, first)
        planes1 = masked_coefs([c[1] for c in coef], at, 1, axes, first)
        for p in range(COEFS):
            low = jnp.where(group == p, turn(planes0[p], 4 * p), low)
            high = jnp.where(group == p, turn(planes1[p], 4 * p - 125), high)
        xw[2, at, :] = low
        xe[2, at, :] = high


def pack_rows(axes, steps, rows, fields, yn, ys, corners):
    prev, src, coef = fields
    group = lane_id() // 4
    for side, (out, first, base) in enumerate(((yn, 0, 0), (ys, rows - HALO, rows - 8))):
        for h in range(2):
            planes = masked_coefs([c[h] for c in coef], pl.ds(base, 8), h, axes, base)
            corner = jnp.zeros((8, LANES), F32)
            for q, j, at in strip_blocks(steps, side):
                if q < 2 * steps // 8:
                    arr, part = (prev, q) if q < steps // 8 else (src, q - steps // 8)
                    value = arr[h][pl.ds(8 * part * rows + first + j, 8, stride=rows), :]
                else:
                    row = first + j - base
                    pieces = [p[row : row + 1] for p in planes]
                    value = jnp.concatenate(pieces + [jnp.zeros((8 - COEFS, LANES), F32)], 0)
                out[h, at : at + 8, :] = value
                slot = 4 * (HALO * q + j)
                corner = jnp.where(group == slot // 4, turn(value, slot - (0, 125)[h]), corner)
            corners[2 * side + h][...] = corner


def strip_blocks(steps, side):
    at, blocks = 0, []
    for q in range(2 * steps // 8 + 1):
        for j in range(HALO):
            if steps // 8 <= q < 2 * steps // 8 and j == (HALO - 1, 0)[side]:
                continue
            blocks.append((q, j, at))
            at += 8
    return blocks


def plan_of(axes, strips, outs, send, recv):
    xw, xe, yn, ys, c_nw, c_ne, c_sw, c_se = strips
    gx, gy = lax.axis_index("gx"), lax.axis_index("gy")
    has_w, has_e, has_n, has_s = position(axes)
    west, east, north, south = gx - 1, gx + 1, gy - 1, gy + 1
    both = jnp.logical_and
    has_nw, has_ne = both(has_n, has_w), both(has_n, has_e)
    has_sw, has_se = both(has_s, has_w), both(has_s, has_e)
    from_w, from_e, from_n, from_s, from_nw, from_ne, from_sw, from_se = outs
    steps = (
        (yn, from_s, (gx, north), has_n, has_s),
        (ys, from_n, (gx, south), has_s, has_n),
        (c_nw, from_se, (west, north), has_nw, has_se),
        (c_ne, from_sw, (east, north), has_ne, has_sw),
        (c_sw, from_ne, (west, south), has_sw, has_ne),
        (c_se, from_nw, (east, south), has_se, has_nw),
        (xw, from_e, (west, gy), has_w, has_e),
        (xe, from_w, (east, gy), has_e, has_w),
    )
    plan = []
    for i, (src, dst, to, goes, comes) in enumerate(steps):
        copy = pltpu.make_async_remote_copy(
            src_ref=src, dst_ref=dst, send_sem=send.at[i], recv_sem=recv.at[i],
            device_id=to, device_id_type=MESH,
        )
        plan.append((copy, to, goes, comes))
    return plan


def greet(plan):
    barrier = pltpu.get_barrier_semaphore()
    for _, to, goes, _ in plan:

        @pl.when(goes)
        def _():
            pl.semaphore_signal(barrier, inc=1, device_id=to, device_id_type=MESH)

    return lambda: pl.semaphore_wait(barrier, sum(jnp.where(step[2], 1, 0) for step in plan))


def start_all(plan):
    for copy, _, goes, _ in plan:
        pl.when(goes)(copy.start)


def wait_all(plan):
    for copy, _, goes, comes in plan:
        pl.when(goes)(copy.wait_send)
        pl.when(comes)(copy.wait_recv)


def exchange_kernel(axes, *refs):
    plan = plan_of(axes, refs[:8], refs[8:16], *refs[16:])
    greet(plan)()
    start_all(plan)
    wait_all(plan)


def halo_kernel(axes, steps, rows, *refs):
    count = 4 + 2 * COEFS
    fields, outs = fields_of(refs[:count]), refs[count : count + 8]
    strips = refs[count + 8 : count + 16]
    plan = plan_of(axes, strips, outs, *refs[count + 16 :])
    all_here = greet(plan)
    pack_rows(axes, steps, rows, fields, strips[2], strips[3], strips[4:])
    all_here()
    start_all(plan[:6])
    pack_columns(axes, steps, rows, fields, strips[0], strips[1])
    start_all(plan[6:])
    wait_all(plan)


def halo_exchange(axes, ident, steps, rows, fields, field_specs, shapes):
    return pl.pallas_call(
        functools.partial(halo_kernel, axes, steps, rows),
        grid=(1,),
        out_shape=[jax.ShapeDtypeStruct(s, F32) for s in shapes],
        in_specs=field_specs,
        out_specs=[pl.BlockSpec(memory_space=pl.ANY)] * 8,
        scratch_shapes=[pltpu.VMEM(s, F32) for s in shapes]
        + [pltpu.SemaphoreType.DMA((8,)), pltpu.SemaphoreType.DMA((8,))],
        compiler_params=pltpu.CompilerParams(
            collective_id=ident, has_side_effects=True, vmem_limit_bytes=VMEM_LIMIT
        ),
        name="halo_exchange",
    )(*fields)


def exchange(axes, ident, *strips):
    return pl.pallas_call(
        functools.partial(exchange_kernel, axes),
        out_shape=[jax.ShapeDtypeStruct(s.shape, F32) for s in strips],
        in_specs=[pl.BlockSpec(memory_space=pl.ANY)] * 8,
        out_specs=[pl.BlockSpec(memory_space=pl.ANY)] * 8,
        scratch_shapes=[pltpu.SemaphoreType.DMA((8,)), pltpu.SemaphoreType.DMA((8,))],
        compiler_params=pltpu.CompilerParams(collective_id=ident, has_side_effects=True),
        name="neighbour_exchange",
    )(*strips)


def spread_matrix(cols):
    shape = (cols, GROUPS * LANES)
    at = lax.broadcasted_iota(jnp.int32, shape, 1)
    col = (at % LANES) * GROUPS + at // LANES - HALO
    return jnp.where(col == lax.broadcasted_iota(jnp.int32, shape, 0), 1.0, 0.0).astype(BF16)


def collect_matrix(cols):
    shape = (GROUPS * LANES, cols)
    at = lax.broadcasted_iota(jnp.int32, shape, 0)
    col = (at % LANES) * GROUPS + at // LANES - HALO
    return jnp.where(col == lax.broadcasted_iota(jnp.int32, shape, 1), 1.0, 0.0).astype(BF16)


def two_terms(values):
    high = values.astype(BF16)
    return jnp.concatenate([high, (values - high.astype(F32)).astype(BF16)], 0)


def moved(values, matrix):
    both = jnp.dot(two_terms(values), matrix, preferred_element_type=F32)
    return both[: values.shape[0]] + both[values.shape[0] :]


def add_halo(parts, west, east, shift):
    lane = lane_id()
    at_86 = lane == 86
    far = turn(east, 85 + shift)
    return (
        jnp.where(lane == 0, turn(west, shift), jnp.where(lane == 87, far, parts[0])),
        jnp.where(lane == 0, turn(west, shift - 1), jnp.where(at_86, turn(east, 86 + shift), parts[1])),
        jnp.where(lane == 0, turn(west, shift - 2), jnp.where(at_86, far, parts[2])),
    )


def west_edge(parts, to):
    lane = lane_id()
    pair = turn(jnp.where(lane == 0, parts[2], parts[0]), to + 1)
    return jnp.where(lane == to, turn(parts[1], to), pair)


def east_edge(parts, to):
    lane = lane_id()
    last = jnp.where(lane == to + 1, turn(parts[1], to - 85 + LANES), turn(parts[2], to - 84 + LANES))
    return jnp.where(lane == to, turn(parts[0], to - 86 + LANES), last)


def add_west(parts, strip, shift, flag):
    lane, out = lane_id(), list(parts)
    near = jnp.where(flag, turn(strip, shift), 0.0)
    out[2] += jnp.where(lane == 0, near, 0.0)
    out[0] += jnp.where(lane == 1, near, 0.0)
    out[1] += jnp.where(jnp.logical_and(lane == 1, flag), turn(strip, shift - 1), 0.0)
    return out


def add_east(parts, strip, shift, flag):
    lane, out = lane_id(), list(parts)
    near = jnp.where(flag, turn(strip, 85 + shift), 0.0)
    out[2] += jnp.where(lane == 85, near, 0.0)
    out[0] += jnp.where(lane == 86, near, 0.0)
    out[1] += jnp.where(jnp.logical_and(lane == 86, flag), turn(strip, 84 + shift), 0.0)
    return out


def neighbours(y, g, v):
    down = y[g][v + 1] if v < VR - 1 else pltpu.roll(y[g][0], 7, 0)
    up = y[g][v - 1] if v else pltpu.roll(y[g][VR - 1], 1, 0)
    east = y[g + 1][v] if g < GROUPS - 1 else turn(y[0][v], LANES - 1)
    west = y[g - 1][v] if g else turn(y[GROUPS - 1][v], 1)
    return east, west, down, up


def sweep_kernel(axes, steps, rows, *refs):
    prev, src = refs[0:2], refs[2:4]
    coef = [refs[4 + 2 * p : 6 + 2 * p] for p in range(COEFS)]
    base = 4 + 2 * COEFS
    from_w, from_e, from_n, from_s, from_nw, from_ne, from_sw, from_se = refs[base : base + 8]
    waves, co, xw, xe, yn, ys = refs[base + 8 : base + 14]
    corners = refs[base + 14 : base + 18]
    ext, cc, gbuf, carry, north_rows, south_rows = refs[base + 18 :]
    has_w, has_e, has_n, has_s = position(axes)
    lane, sub = lane_id(), sub_id()
    zero = jnp.zeros((8, LANES), F32)

    def keep(flag, value):
        return jnp.where(flag, value, 0.0)

    def plane(index, v, g):
        return ext[g, pl.ds(index * ROWS_L + v, 8, stride=VR), :]

    chunk = steps // CHUNKS
    first_step = pl.program_id(0) * chunk

    @pl.when(pl.program_id(0) == 0)
    def _():
        spreader = spread_matrix(2 * LANES)

        def put_own(plane, t, parts, k, slot):
            at = pl.ds(t * 8, 8)
            west, east = keep(has_w, from_w[k, at, :]), keep(has_e, from_e[k, at, :])
            for g, value in enumerate(add_halo(parts, west, east, 4 * LANES - 4 * slot)):
                ext[g, pl.ds(plane * ROWS_L + HALO + 8 * t, 8), :] = value

        def part_of(wide, first):
            return [wide[first : first + 8, g * LANES : (g + 1) * LANES] for g in range(GROUPS)]

        @pl.loop(0, steps // 4)
        def _(i):
            for k, arr in enumerate((prev, src)):
                at = pl.ds(pl.multiple_of(4 * i * rows, 8), 4 * rows)
                wide = moved(jnp.concatenate([arr[0][at, :], arr[1][at, :]], 1), spreader)
                for m in range(4):
                    n = 4 * i + m
                    for t in range(rows // 8):
                        put_own(k * steps + n, t, part_of(wide, m * rows + 8 * t), k, n)

        lows, highs = [], []
        for t in range(rows // 8):
            at = pl.ds(8 * t, 8)
            lows += masked_coefs([c[0] for c in coef], at, 0, axes, 8 * t)
            highs += masked_coefs([c[1] for c in coef], at, 1, axes, 8 * t)
        wide = jnp.concatenate([jnp.concatenate(lows, 0), jnp.concatenate(highs, 0)], 1)
        wide = moved(wide, spreader)
        for t in range(rows // 8):
            for p in range(COEFS):
                put_own(2 * steps + p, t, part_of(wide, 8 * (t * COEFS + p)), 2, p)
        for side, (strip, cw, ce, flag, first) in enumerate((
            (from_n, from_nw, from_ne, has_n, 0),
            (from_s, from_sw, from_se, has_s, rows + HALO),
        )):
            wide = moved(keep(flag, jnp.concatenate([strip[0], strip[1]], 1)), spreader)
            west = keep(jnp.logical_and(flag, has_w), cw[...])
            east = keep(jnp.logical_and(flag, has_e), ce[...])
            for q, j, at in strip_blocks(steps, 1 - side):
                shift = 4 * LANES - 4 * (HALO * q + j)
                for g, value in enumerate(add_halo(part_of(wide, at), west, east, shift)):
                    ext[g, pl.ds(8 * q * ROWS_L + first + j, 8, stride=ROWS_L), :] = value
        for row in (0, rows + 2 * HALO - 1):
            for q in range(steps // 8, 2 * steps // 8):
                for g in range(3):
                    ext[g, pl.ds(8 * q * ROWS_L + row, 8, stride=ROWS_L), :] = zero
        for row in range(rows + 2 * HALO, ROWS_L):
            for q in range(2 * steps // 8 + 1):
                for g in range(3):
                    ext[g, pl.ds(8 * q * ROWS_L + row, 8, stride=ROWS_L), :] = zero

        first_coef = 2 * steps
        easts = [[plane(2 * steps + 3, v, g) for v in range(VR)] for g in range(3)]
        for g in range(3):
            col = lane * GROUPS + g
            col_in = jnp.logical_and(col >= 1, col <= 260)
            col_own = jnp.logical_and(col >= HALO, col <= 258)
            col_there = jnp.logical_and(
                jnp.logical_or(col >= HALO, has_w), jnp.logical_or(col <= 258, has_e)
            )
            n_cols = (
                1.0
                + jnp.where(jnp.logical_and(col <= 4, has_w), 1.0, 0.0)
                + jnp.where(jnp.logical_and(col >= 257, has_e), 1.0, 0.0)
            )
            souths = [plane(first_coef + 4, v, g) for v in range(VR)]
            for v in range(VR):
                row = sub * VR + v
                row_in = jnp.logical_and(row >= 1, row <= 68)
                row_own = jnp.logical_and(row >= HALO, row <= 66)
                row_there = jnp.logical_and(
                    jnp.logical_or(row >= HALO, has_n), jnp.logical_or(row <= 66, has_s)
                )
                inner = jnp.logical_and(row_in, col_in)
                own = jnp.logical_and(row_own, col_own)
                there = jnp.logical_and(jnp.logical_and(row_there, col_there), inner)
                n_rows = (
                    1.0
                    + jnp.where(jnp.logical_and(row <= 4, has_n), 1.0, 0.0)
                    + jnp.where(jnp.logical_and(row >= 65, has_s), 1.0, 0.0)
                )
                start, sto, leak, east, south, owner = [
                    plane(first_coef + p, v, g) for p in range(COEFS)
                ]
                ea_w = easts[g - 1][v] if g else turn(easts[GROUPS - 1][v], 1)
                so_n = souths[v - 1] if v else pltpu.roll(souths[VR - 1], 1, 0)
                diag = sto + leak + east + ea_w + south + so_n
                safe = jnp.where(there, diag, 1.0)
                scale = jnp.where(there, 2.0 * SIGMA / safe, 0.0)
                cc[0, g, v] = scale * east
                cc[1, g, v] = scale * ea_w
                cc[2, g, v] = scale * south
                cc[3, g, v] = scale * so_n
                cc[4, g, v] = scale
                cc[5, g, v] = scale * sto
                cc[6, g, v] = jnp.where(inner, 0.0, 2.0 * SIGMA)
                weight = jnp.where(own, owner, jnp.where(there, 1.0, 0.0))
                cc[7, g, v] = weight * (1.0 / TAU[DEG])
                den = jnp.where(there, owner + n_rows * n_cols - 1.0, 1.0)
                at = slice(8 * v, 8 * v + 8)
                co[0, g, at, :] = weight
                co[1, g, at, :] = jnp.where(there, 1.0 / den, 0.0)
                co[2, g, at, :] = diag
                co[3, g, at, :] = east
                co[4, g, at, :] = ea_w
                co[5, g, at, :] = south
                co[6, g, at, :] = so_n
                co[7, g, at, :] = sto
                co[8, g, at, :] = start
                carry[g, v] = start

        xw[...] = jnp.zeros_like(xw)
        xe[...] = jnp.zeros_like(xe)

    group = lane // 4

    def stencil(y, g, v):
        east, west, down, up = neighbours(y, g, v)
        return (cc[0, g, v] * east + cc[1, g, v] * west) + (cc[2, g, v] * down + cc[3, g, v] * up)

    def advance(n, held):
        def each(value):
            out = [[None] * VR for _ in range(GROUPS)]
            for v in range(VR):
                for g in range(GROUPS):
                    out[g][v] = value(g, v)
            return out

        old = each(lambda g, v: plane(n, v, g))
        for v in range(VR):
            for g in range(GROUPS):
                gbuf[g, v] = (
                    cc[4, g, v] * plane(steps + n, v, g)
                    + cc[5, g, v] * held[g][v]
                    + cc[6, g, v] * old[g][v]
                )
        now = each(lambda g, v: 0.5 * (stencil(old, g, v) + gbuf[g, v]))
        for k in range(1, DEG):
            new = each(lambda g, v: stencil(now, g, v) + (TAU[k] * gbuf[g, v] - old[g][v]))
            old, now = now, new
        return now

    def finish(n, now):
        for g in range(3):
            for v in range(VR):
                at = pl.ds(pl.multiple_of((n - first_step) * ROWS_L + 8 * v, 8), 8)
                waves[g, at, :] = now[g][v] * (1.0 / TAU[DEG])
        weighted = [[cc[7, g, v] * now[g][v] for v in range(VR)] for g in range(3)]
        for v in range(VR):
            at = slice(8 * v, 8 * v + 8)
            parts = [weighted[g][v] for g in range(GROUPS)]
            xw[at, :] = jnp.where(group == n, west_edge(parts, 4 * n), xw[at, :])
            xe[at, :] = jnp.where(group == n, east_edge(parts, 4 * n), xe[at, :])
        for j in range(HALO):
            for g in range(3):
                north_rows[g, pl.ds(j * steps + n, 1), :] = weighted[g][1 + j][0:1]
                south_rows[g, pl.ds(j * steps + n, 1), :] = weighted[g][3 + j][7:8]
        return [[now[g][v] * (1.0 / TAU[DEG]) for v in range(VR)] for g in range(3)]

    @pl.loop(0, chunk)
    def _(m):
        n = first_step + m
        held = [[carry[g, v] for v in range(VR)] for g in range(3)]
        held = finish(n, advance(n, held))
        for g in range(GROUPS):
            for v in range(VR):
                carry[g, v] = held[g][v]

    @pl.when(pl.program_id(0) == CHUNKS - 1)
    def _():
        collector = collect_matrix(2 * LANES)
        for side, (rows_of, out) in enumerate(((north_rows, yn), (south_rows, ys))):
            west, east = zero, zero
            for i in range(HALO * steps // 8):
                at = slice(8 * i, 8 * i + 8)
                parts = [rows_of[g, at, :] for g in range(GROUPS)]
                west = jnp.where(group == i, west_edge(parts, 4 * i), west)
                east = jnp.where(group == i, east_edge(parts, 4 * i), east)
            plain = moved(jnp.concatenate([rows_of[g] for g in range(GROUPS)], 1), collector)
            for h, pack in enumerate((west, east)):
                out[h, : HALO * steps, :] = plain[:, h * LANES : (h + 1) * LANES]
                out[h, HALO * steps :, :] = pack
                corners[2 * side + h][...] = pack


def chebyshev_scales():
    tau = [1.0, SIGMA]
    for _ in range(DEG):
        tau.append(2.0 * SIGMA * tau[-1] - tau[-2])
    return tau


TAU = chebyshev_scales()


def one_hot_of(row, count, first):
    ids = jnp.broadcast_to(row - first, (count, row.shape[1]))
    return jnp.where(
        ids == lax.broadcasted_iota(jnp.int32, ids.shape, 0), 1.0, 0.0
    ).astype(BF16)


def settle_kernel(axes, steps, rows, aggs, *refs):
    waves, co, from_w, from_e, from_n, from_s, from_nw, from_ne, from_sw, from_se = refs[:10]
    src = refs[10:12]
    agg = refs[12]
    settled, coarse = refs[13:15]
    before, both, rest, north, south = refs[15:]
    has_w, has_e, has_n, has_s = position(axes)
    lane, sub = lane_id(), sub_id()
    tile = lax.axis_index("gx") * axes[1] + lax.axis_index("gy")

    def spread(row):
        return jnp.broadcast_to(row, (8, LANES))

    chunk = steps // CHUNKS
    first_step = pl.program_id(0) * chunk

    @pl.when(pl.program_id(0) == 0)
    def _():
        for g in range(3):
            for v in range(VR):
                before[g, v] = co[8, g, 8 * v : 8 * v + 8, :]


        spreader = spread_matrix(2 * LANES)
        for strip, cw, ce, flag, out in (
            (from_n, from_nw, from_ne, has_n, north),
            (from_s, from_sw, from_se, has_s, south),
        ):
            rim = HALO * steps
            wide = moved(jnp.concatenate([strip[0, :rim, :], strip[1, :rim, :]], 1), spreader)
            west, east = strip[0, rim:, :], strip[1, rim:, :]
            for i in range(rim // 8):
                at = slice(8 * i, 8 * i + 8)
                parts = [wide[at, g * LANES : (g + 1) * LANES] for g in range(GROUPS)]
                parts[2] = jnp.where(lane == 0, turn(west, -1 - 4 * i), parts[2])
                parts[1] = jnp.where(lane == 86, turn(east, 85 - 4 * i), parts[1])
                parts = add_west(parts, cw[...], -4 * i, has_w)
                parts = add_east(parts, ce[...], -4 * i, has_e)
                for g, value in enumerate(parts):
                    out[g, at, :] = jnp.where(flag, value, 0.0)

    @pl.loop(0, chunk)
    def _(m):
        n = first_step + m
        now = [[None] * VR for _ in range(3)]
        for v in range(VR):
            at = slice(8 * v, 8 * v + 8)
            here = pl.ds(pl.multiple_of(m * ROWS_L + 8 * v, 8), 8)
            parts = [co[0, g, at, :] * waves[g, here, :] for g in range(GROUPS)]
            shift = 4 * LANES - 4 * n
            parts = add_west(parts, from_w[at, :], shift, has_w)
            parts = add_east(parts, from_e[at, :], shift, has_e)
            for g, total in enumerate(parts):
                if 2 <= v <= 4:
                    one = pl.ds((v - 2) * steps + n, 1)
                    total += jnp.where(sub == 0, spread(north[g, one, :]), 0.0)
                    total += jnp.where(sub == 7, spread(south[g, one, :]), 0.0)
                now[g][v] = total * co[1, g, at, :]
        out = [[None] * VR for _ in range(3)]
        for g in range(3):
            for v in range(VR):
                at = slice(8 * v, 8 * v + 8)
                cur = now[g][v]
                east, west, down, up = neighbours(now, g, v)
                image = (
                    co[2, g, at, :] * cur
                    - co[3, g, at, :] * east
                    - co[4, g, at, :] * west
                    - co[5, g, at, :] * down
                    - co[6, g, at, :] * up
                )
                out[g][v] = co[7, g, at, :] * before[g, v] - image
                before[g, v] = cur
        for v in range(VR):
            at = pl.ds(m * ROWS_L + v, 8, stride=VR)
            for g in range(GROUPS):
                both[g, 0, at, :] = now[g][v]
                both[g, 1, at, :] = out[g][v]

    collector = collect_matrix(2 * LANES)

    @pl.loop(0, chunk // 2)
    def _(i):
        pieces = [
            jnp.concatenate(
                [both[g, k, pl.ds((2 * i + m) * ROWS_L + HALO, rows), :] for g in range(GROUPS)], 1
            )
            for k in range(2)
            for m in range(2)
        ]
        plain = moved(jnp.concatenate(pieces, 0), collector)
        at = pl.ds(pl.multiple_of(2 * i * rows, 8), 2 * rows)
        for h in range(2):
            lanes = slice(h * LANES, (h + 1) * LANES)
            settled[h, at, :] = plain[: 2 * rows, lanes]
            there = pl.ds(pl.multiple_of((first_step + 2 * i) * rows, 8), 2 * rows)
            rest[h, there, :] = plain[2 * rows :, lanes] + src[h][at, :]

    @pl.when(pl.program_id(0) == CHUNKS - 1)
    def _():
        def add_rows(i, total):
            values, hots = [], []
            for k in range(8):
                row = 8 * i + k
                at = pl.ds(row, steps, stride=rows)
                values += [rest[0, at, :], rest[1, at, :]]
                hots.append(one_hot_of(agg[pl.ds(row, 1), :], aggs, tile * aggs))
            return total + lax.dot_general(
                two_terms(jnp.concatenate(values, 1)), jnp.concatenate(hots, 1),
                (((1,), (1,)), ((), ())), preferred_element_type=F32,
            )

        total = lax.fori_loop(0, rows // 8, add_rows, jnp.zeros((2 * steps, aggs), F32))
        total = total[:steps] + total[steps:]
        coarse[...] = jnp.concatenate([total[: steps // 2], total[steps // 2 :]], 1)


def gather_kernel(axes, own, everyone, send, recv, pass_send, pass_recv, local):
    n_x, n_y = axes
    chips = n_x // 2 * n_y
    gx, gy = lax.axis_index("gx"), lax.axis_index("gy")
    core = lax.rem(gx, 2)
    chip = gx // 2 * n_y + gy
    partner = (gx + 1 - 2 * core, gy)

    def place(which, at_core):
        x, y = 2 * (which // n_y) + at_core, lax.rem(which, n_y)
        return (x, y), x * n_y + y

    def step_to(i):
        return place(lax.rem(chip + i, chips), core)[0]

    def step_from(i, at_core):
        return place(lax.rem(chip + chips - i, chips), at_core)[1]

    barrier = pltpu.get_barrier_semaphore()

    @pl.loop(1, chips)
    def _(i):
        pl.semaphore_signal(barrier, inc=1, device_id=step_to(i), device_id_type=MESH)

    pl.semaphore_signal(barrier, inc=1, device_id=partner, device_id_type=MESH)
    pl.semaphore_wait(barrier, chips)

    def spread(i, block):
        return pltpu.make_async_remote_copy(
            src_ref=own, dst_ref=everyone.at[block], send_sem=send.at[i], recv_sem=recv.at[i],
            device_id=step_to(i), device_id_type=MESH,
        )

    def hand_over(i, src, block):
        return pltpu.make_async_remote_copy(
            src_ref=src, dst_ref=everyone.at[block], send_sem=pass_send.at[i],
            recv_sem=pass_recv.at[i], device_id=partner, device_id_type=MESH,
        )

    me = gx * n_y + gy
    mine = pltpu.make_async_copy(own, everyone.at[me], local)

    @pl.loop(1, chips)
    def _(i):
        spread(i, me).start()

    hand_over(0, own, me).start()
    mine.start()

    @pl.loop(1, chips)
    def _(i):
        block = step_from(i, core)
        spread(i, block).wait_recv()
        hand_over(i, everyone.at[block], block).start()

    @pl.loop(1, chips)
    def _(i):
        spread(i, me).wait_send()

    @pl.loop(0, chips)
    def _(i):
        hand_over(i, own, me).wait_send()
        hand_over(i, own, step_from(i, 1 - core)).wait_recv()

    mine.wait()


def gather(axes, ident, own):
    count = axes[0] * axes[1]
    return pl.pallas_call(
        functools.partial(gather_kernel, axes),
        out_shape=jax.ShapeDtypeStruct((count,) + own.shape, F32),
        in_specs=[pl.BlockSpec(memory_space=pl.ANY)],
        out_specs=pl.BlockSpec(memory_space=pl.ANY),
        scratch_shapes=[
            pltpu.SemaphoreType.DMA((count // 2,)),
            pltpu.SemaphoreType.DMA((count // 2,)),
            pltpu.SemaphoreType.DMA((count // 2,)),
            pltpu.SemaphoreType.DMA((count // 2,)),
            pltpu.SemaphoreType.DMA,
        ],
        compiler_params=pltpu.CompilerParams(collective_id=ident, has_side_effects=True),
        name="coarse_gather",
    )(own)


def correct_kernel(axes, steps, rows, aggs, everyone, inverse, agg, settled, out, fixed):
    tile = lax.axis_index("gx") * axes[1] + lax.axis_index("gy")
    count = axes[0] * axes[1]

    @pl.when(pl.program_id(0) == 0)
    def _():
        low_lanes = lax.broadcasted_iota(jnp.int32, (steps // 2, LANES), 1) < aggs
        total = jnp.zeros((steps, aggs), F32)
        for d in range(0, count, 2):
            a, b = everyone[d], everyone[d + 1]
            upper = jnp.where(low_lanes, a, pltpu.roll(b, aggs, 1))
            lower = jnp.where(low_lanes, pltpu.roll(a, aggs, 1), b)
            total += lax.dot_general(
                jnp.concatenate([upper, lower], 0),
                inverse[:, d * aggs : (d + 2) * aggs],
                (((1,), (1,)), ((), ())),
                precision=lax.Precision.HIGHEST,
                preferred_element_type=F32,
            )
        high = total.astype(BF16)
        low = (total - high.astype(F32)).astype(BF16)
        fixed[...] = jnp.concatenate([high, low], 1)

    factor = fixed[...]

    @pl.loop(0, rows // 8)
    def _(i):
        hot = jnp.concatenate(
            [one_hot_of(agg[pl.ds(8 * i + k, 1), :], aggs, tile * aggs) for k in range(8)], 1
        )
        grown = jnp.dot(factor, jnp.concatenate([hot, hot], 0), preferred_element_type=F32)
        for k in range(8):
            at = pl.ds(8 * i + k, steps, stride=rows)
            out[at, :] = settled[0, at, :] + grown[:, k * LANES : (k + 1) * LANES]


def halves(shape):
    block = (shape[0], LANES)
    return [pl.BlockSpec(block, lambda i: (0, 0)), pl.BlockSpec(block, lambda i: (0, 1))]


def whole(shape):
    return pl.BlockSpec(shape, lambda i: (0,) * len(shape))


def shards(axes, prev_wave, source, start_state, storage, leakage, cond_east, cond_south,
           owner_weight, aggregate, coarse_inverse):
    steps, rows, cols = prev_wave.shape
    aggs = coarse_inverse.shape[0]
    planes = 2 * steps + 8
    strip_rows = HALO * planes - steps
    rim_rows = HALO * steps
    flat = (steps * rows, cols)
    prev, src = prev_wave.reshape(flat), source.reshape(flat)
    coef = (start_state, storage, leakage, cond_east, cond_south, owner_weight)
    params = pltpu.CompilerParams(vmem_limit_bytes=VMEM_LIMIT)
    fields, field_specs = [], []
    for arr in (prev, src) + coef:
        fields += [arr, arr]
        field_specs += halves(arr.shape)

    def local(kernel, name, args, in_specs, outs, out_specs, scratch):
        return pl.pallas_call(
            kernel,
            grid=(CHUNKS,),
            out_shape=[jax.ShapeDtypeStruct(s, F32) for s in outs],
            in_specs=in_specs,
            out_specs=out_specs + [whole(s) for s in outs[1:]],
            scratch_shapes=scratch,
            compiler_params=params,
            name=name,
        )(*args)

    shapes = [(3, rows, LANES)] * 2 + [(2, strip_rows, LANES)] * 2 + [(8, LANES)] * 4
    halo = halo_exchange(axes, 0, steps, rows, fields, field_specs, shapes)
    wave_spec = pl.BlockSpec((3, steps * ROWS_L // CHUNKS, LANES), lambda i: (0, i, 0))
    waves, co, *rims = local(
        functools.partial(sweep_kernel, axes, steps, rows), "local_sweep",
        fields + list(halo), field_specs + [whole(h.shape) for h in halo],
        [(3, steps * ROWS_L, LANES), (9, 3, ROWS_L, LANES)]
        + [(ROWS_L, LANES)] * 2 + [(2, rim_rows + 8, LANES)] * 2 + [(8, LANES)] * 4,
        [wave_spec],
        [
            pltpu.VMEM((3, planes * ROWS_L, LANES), F32),
            pltpu.VMEM((8, 3, VR, 8, LANES), F32),
            pltpu.VMEM((3, VR, 8, LANES), F32),
            pltpu.VMEM((3, VR, 8, LANES), F32),
            pltpu.VMEM((3, rim_rows, LANES), F32),
            pltpu.VMEM((3, rim_rows, LANES), F32),
        ],
    )
    rim = exchange(axes, 1, *rims)
    args = [waves, co, *rim]
    settled, coarse = local(
        functools.partial(settle_kernel, axes, steps, rows, aggs), "settle_and_restrict",
        args + [src, src, aggregate],
        [wave_spec]
        + [whole(a.shape) for a in args[1:]]
        + [
            pl.BlockSpec((steps * rows // CHUNKS, LANES), lambda i: (i, 0)),
            pl.BlockSpec((steps * rows // CHUNKS, LANES), lambda i: (i, 1)),
            whole(aggregate.shape),
        ],
        [(2, steps * rows, LANES), (steps // 2, 2 * aggs)],
        [pl.BlockSpec((2, steps * rows // CHUNKS, LANES), lambda i: (0, i, 0))],
        [
            pltpu.VMEM((3, VR, 8, LANES), F32),
            pltpu.VMEM((3, 2, steps * ROWS_L // CHUNKS, LANES), F32),
            pltpu.VMEM((2, steps * rows, LANES), F32),
            pltpu.VMEM((3, rim_rows, LANES), F32),
            pltpu.VMEM((3, rim_rows, LANES), F32),
        ],
    )
    everyone = gather(axes, 2, coarse)
    out = pl.pallas_call(
        functools.partial(correct_kernel, axes, steps, rows, aggs),
        grid=(2,),
        out_shape=jax.ShapeDtypeStruct(flat, F32),
        in_specs=[
            whole(everyone.shape),
            whole(coarse_inverse.shape),
            pl.BlockSpec((rows, LANES), lambda i: (0, i)),
            pl.BlockSpec((1, steps * rows, LANES), lambda i: (i, 0, 0)),
        ],
        out_specs=pl.BlockSpec((steps * rows, LANES), lambda i: (0, i)),
        scratch_shapes=[pltpu.VMEM((steps, 2 * aggs), BF16)],
        compiler_params=params,
        name="correct",
    )(everyone, coarse_inverse, aggregate, settled)
    return out.reshape(prev_wave.shape)


def solution(mesh):
    axes = (mesh.shape["gx"], mesh.shape["gy"])
    plane = P("gy", "gx")
    wave = P(None, "gy", "gx")
    return jax.shard_map(
        functools.partial(shards, axes),
        mesh=mesh,
        in_specs=(wave, wave) + (plane,) * 7 + (P(("gx", "gy"), None),),
        out_specs=wave,
        check_vma=False,
    )
```
